32 devices in a mesh: inst: 4 (over y, x), space: 8 (over z, core).
Axes of the slice: x: 2, y: 2, z: 4, core: 2. Of those that a mesh axis runs over, the one named last changes fastest.
Arguments:
- adjoint: float32 [4, 5, 256, 64, 128], P('inst', None, 'space'), may hold values from -6 to 6
- source: float32 [4, 5, 256, 64, 128], P('inst', None, 'space'), may hold values from -6 to 6
- viscosity: float32 [256, 64, 128], P('space'), may hold values from 0.2 to 2
- kappa: float32 [5], replicated, may hold values from 0.5 to 2
- coupling: float32 [5, 5], replicated, may hold values from -2.4 to 2.4
- bc_flags: int32 [5, 3], replicated, may hold values 0 or 1
- inst_map: int32 [4], replicated, may hold values from 0 to 3, each once
Outputs:
- residual: float32 [4, 5, 256, 64, 128], P('inst', None, 'space')
The draws below stay inside these ranges and needn't reach their ends.
Inputs may be any that keep to these rules, and one draw needn't show every extreme that they name: `inst_map`: a permutation of 0 to 3. `bc_flags`: 1 marks a face of zero normal flux, 0 a face held at zero.
All inputs are finite; a program needn't handle non-finite values.
Results may differ from the reference program's by a relative error of at most 0.0001.
Values sent between devices are 32-bit elements; how exact they have to be, the bound alone decides.
No kernel may reach another device: no remote copies, remote signals or barrier semaphores. Data moves between devices by JAX's collectives and lax.ppermute only.
A program may use at most 128 MiB of HBM per device.

```python
import math
import jax
import jax.numpy as jnp
from jax import lax

NTH = 256
NR = 64
NX = 128
N_INST = 4


def plant(values, own_key, smallest, high):
    dims = values.shape
    place = [jax.random.randint(jax.random.fold_in(own_key, axis), (), 0, dims[axis]) for axis in range(len(dims))]
    values = values.at[tuple(place)].set(smallest)
    longest = dims.index(max(dims))
    place[longest] = (place[longest] + 1) % dims[longest]
    return values.at[tuple(place)].set(high)


def steps_of(stream_key, dims, pieces, low, largest):
    factor_of, own = 1.0, jax.random.fold_in(stream_key, 6)
    for dim, blocks in pieces:
        steps = jnp.exp(jax.random.uniform(jax.random.fold_in(own, dim), (blocks,), jnp.float32, low / len(pieces), largest / len(pieces)))
        factor_of = factor_of * jnp.repeat(steps, dims[dim] // blocks).reshape([-1 if axis == dim else 1 for axis in range(len(dims))])
    return factor_of


def scatter_about(own_key, shape, width, most, split=(), kind=jnp.bfloat16):
    result = jax.random.normal(own_key, shape, jnp.float32) * width
    if len(split) > 0:
        result = steps_of(own_key, shape, split, -0.22, 0.18) * result
    return jnp.clip(result, min=-most, max=most).astype(kind)


def setup_inputs(seed: int = 0) -> dict:
    key_list = jax.random.split(jax.random.key(seed), 8)
    return {
        "adjoint": scatter_about(key_list[0], (N_INST, 5, NTH, NR, NX), 1.0, 6.0, ((0, 4), (2, 8)), jnp.float32),
        "source": scatter_about(key_list[1], (N_INST, 5, NTH, NR, NX), 1.0, 6.0, ((0, 4), (2, 8)), jnp.float32),
        "viscosity": jnp.clip(jnp.exp(math.log(2.0) - 2.3025851 * jax.random.uniform(key_list[2], (NTH, NR, NX), jnp.float32) ** steps_of(key_list[2], (NTH, NR, NX), ((0, 8),), -0.2, 0.2)), 0.2, 2.0),
        "kappa": jnp.clip(jnp.exp(jax.random.uniform(key_list[3], (5,), jnp.float32, math.log(0.5), math.log(2.0))), 0.5, 2.0),
        "coupling": scatter_about(key_list[4], (5, 5), 0.4, 2.4, (), jnp.float32),
        "bc_flags": plant((jax.random.randint(key_list[5], (5, 3), 0, 2) < 1).astype(jnp.int32), jax.random.fold_in(key_list[5], 1), 0, 1),
        "inst_map": jax.random.permutation(key_list[6], N_INST).astype(jnp.int32),
    }


def spectral_matrix(labels, slots):
    labels = labels.astype(jnp.int32)
    offset = labels[:, None] - labels[None, :]
    parity = (1 - 2 * (jnp.abs(offset) % 2)).astype(jnp.float32)
    sines = jnp.sin(jnp.pi * offset.astype(jnp.float32) / slots)
    safe = jnp.where(offset == 0, jnp.float32(1.0), sines)
    return jnp.where(offset == 0, jnp.float32(0.0), 0.5 * parity / safe)


def mode_tables(points):
    indices = jnp.arange(points, dtype=jnp.int32)
    product = (indices[:, None] * indices[None, :]) % points
    angles = 2.0 * jnp.pi * product.astype(jnp.float32) / points
    return jnp.cos(angles), jnp.sin(angles)


def cycle_response(points, cycle_index, near):
    indices = jnp.arange(points, dtype=jnp.int32)
    wave_number = jnp.minimum(indices, points - indices)
    cutoff = jnp.maximum(4, (points * (cycle_index + 1)) // (2 * near))
    return (wave_number[None, :] < cutoff[:, None]).astype(jnp.float32)


def smooth_cycles(pencil, first_cycle, near):
    points = pencil.shape[1]
    cycles = pencil.shape[2]
    cosines, sines_table = mode_tables(points)
    cycle_index = first_cycle + jnp.arange(cycles, dtype=jnp.int32)
    response = (cycle_response(points, cycle_index, near).T / points)[None, :, :, None]
    coef_cos = jnp.einsum("tk,ftrx->fkrx", cosines, pencil, precision=lax.Precision.HIGHEST)
    coef_sin = jnp.einsum("tk,ftrx->fkrx", sines_table, pencil, precision=lax.Precision.HIGHEST)
    smoothed = jnp.einsum("tk,fkrx->ftrx", cosines, coef_cos * response, precision=lax.Precision.HIGHEST)
    smoothed = smoothed + jnp.einsum("tk,fkrx->ftrx", sines_table, coef_sin * response, precision=lax.Precision.HIGHEST)
    weights = jnp.maximum(1.0 - cycle_index.astype(jnp.float32) / near, 0.0)[None, None, :, None]
    return pencil + weights * (smoothed - pencil)


def viscous(center, nbr_up, nbr_dn, visc, visc_up, visc_dn, kappa, flags):
    cycles = center.shape[2]
    cells_x = center.shape[3]
    cycle_weight = (1.0 / (jnp.arange(cycles, dtype=jnp.float32) + 1.0))[None, :, None]
    theta = cycle_weight * (0.5 * (visc + visc_up) * (center - nbr_up) + 0.5 * (visc + visc_dn) * (center - nbr_dn))
    face_r = 0.5 * (visc[:, :-1, :] + visc[:, 1:, :])
    flux_r = face_r * (center[:, :, :-1, :] - center[:, :, 1:, :])
    radial = jnp.pad(flux_r, ((0, 0), (0, 0), (0, 1), (0, 0))) - jnp.pad(flux_r, ((0, 0), (0, 0), (1, 0), (0, 0)))
    face_x = 0.5 * (visc[:, :, :-1] + visc[:, :, 1:])
    flux_x = face_x * (center[:, :, :, :-1] - center[:, :, :, 1:])
    axial = jnp.pad(flux_x, ((0, 0), (0, 0), (0, 0), (0, 1))) - jnp.pad(flux_x, ((0, 0), (0, 0), (0, 0), (1, 0)))
    open_faces = (1 - flags).astype(jnp.float32)
    outer = open_faces[:, 2][:, None, None, None] * visc[None, :, -1:, :] * center[:, :, -1:, :]
    outer = jnp.pad(outer, ((0, 0), (0, 0), (cycles - 1, 0), (0, 0)))
    inflow = open_faces[:, 0][:, None, None, None] * visc[None, :, :, :1] * center[:, :, :, :1]
    inflow = jnp.pad(inflow, ((0, 0), (0, 0), (0, 0), (0, cells_x - 1)))
    outflow = open_faces[:, 1][:, None, None, None] * visc[None, :, :, -1:] * center[:, :, :, -1:]
    outflow = jnp.pad(outflow, ((0, 0), (0, 0), (0, 0), (cells_x - 1, 0)))
    return kappa[:, None, None, None] * (theta + radial + axial + outer + inflow + outflow)


def reference(adjoint, source, viscosity, kappa, coupling, bc_flags, inst_map):
    matrix = spectral_matrix(inst_map, N_INST)
    near = NR // 2
    visc_up = jnp.roll(viscosity, -1, axis=0)
    visc_dn = jnp.roll(viscosity, 1, axis=0)
    results = []
    for slot in range(N_INST):
        center = adjoint[slot]
        spectral = jnp.tensordot(matrix[:, slot], adjoint, axes=1, precision=lax.Precision.HIGHEST)
        coupled = jnp.einsum("gf,gtrx->ftrx", coupling, center, precision=lax.Precision.HIGHEST)
        diffused = viscous(center, jnp.roll(center, -1, axis=1), jnp.roll(center, 1, axis=1), viscosity, visc_up, visc_dn, kappa, bc_flags)
        pre = source[slot] + coupled + diffused + spectral
        inner = smooth_cycles(pre[:, :, :near, :], jnp.int32(0), near)
        results.append(jnp.concatenate([inner, pre[:, :, near:, :]], axis=2))
    return jnp.stack(results, axis=0)
```

```python
import functools

import jax
import jax.numpy as jnp
import numpy as np
from jax import lax
from jax.experimental import pallas as pl
from jax.experimental.pallas import tpu as pltpu
from jax.sharding import PartitionSpec as P

GROUP = 4
NEAR_SIZES = (2, 2, 1)
FAR_SIZES = (3, 2)
SMEM = pl.BlockSpec(memory_space=pltpu.SMEM)
VMEM_LIMIT = 48 * 1024 * 1024


def spectral_matrix(labels, slots):
    offset = labels[:, None] - labels[None, :]
    parity = (1 - 2 * (jnp.abs(offset) % 2)).astype(jnp.float32)
    sines = jnp.sin(jnp.pi * offset.astype(jnp.float32) / slots)
    safe = jnp.where(offset == 0, jnp.float32(1.0), sines)
    return jnp.where(offset == 0, jnp.float32(0.0), 0.5 * parity / safe)


def mode_layout(points, near):
    half = points // 2
    pairs = near // 2
    bases, base, scale = [], np.zeros(near, np.float32), np.zeros(near, np.float32)
    for r in range(near):
        cutoff = max(4, points * (r + 1) // (2 * near))
        weight = max(1.0 - r / near, 0.0)
        kept = [m for m in range(half + 1) if m < cutoff]
        out = [m for m in range(half + 1) if m >= cutoff]
        count = [sum(1 if m in (0, half) else 2 for m in modes) for modes in (kept, out)]
        low = count[0] <= count[1]
        rows = []
        for m in kept if low else out:
            norm = np.sqrt((1.0 if m in (0, half) else 2.0) / points)
            rows.append((m, 0, norm))
            if m not in (0, half):
                rows.append((m, points // 4, norm))
        bases.append(rows)
        base[r] = 1.0 - weight if low else 1.0
        scale[r] = weight if low else -weight
    depth = max(len(bases[p]) + len(bases[p + pairs]) for p in range(pairs))
    depth = -(-depth // 8) * 8
    mode = np.zeros((pairs, depth), np.int32)
    phase = np.zeros((pairs, depth), np.int32)
    which = np.zeros((pairs, depth), np.int32)
    norm = np.zeros((pairs, depth), np.float32)
    for p in range(pairs):
        rows = [(0,) + row for row in bases[p]] + [(1,) + row for row in bases[p + pairs]]
        for i, (a, m, ph, nm) in enumerate(rows):
            mode[p, i], phase[p, i], which[p, i], norm[p, i] = m, ph, a, nm
    pair_base = np.stack([base[:pairs], base[pairs:]], axis=1)
    pair_scale = np.stack([scale[:pairs], scale[pairs:]], axis=1)
    return mode, phase, which, norm, pair_base, pair_scale


def filter_tables(points, near, block, place):
    mode, phase, which, norm, base, scale = mode_layout(points, near)
    owned = mode.shape[0] // GROUP
    depth = mode.shape[1]
    rank = place % GROUP
    mine = lambda table: lax.dynamic_slice_in_dim(jnp.asarray(table), rank * owned, owned, 0)
    mode, phase, which, norm, base, scale = map(mine, (mode, phase, which, norm, base, scale))
    sector = (place - rank) + (rank ^ jnp.arange(GROUP, dtype=jnp.int32))
    theta = sector[:, None] * block + jnp.arange(block, dtype=jnp.int32)[None, :]
    theta = theta.reshape(-1)
    index = (mode[:, :, None] * theta[None, None, :] - phase[:, :, None] + points) % points
    wave = norm[:, :, None] * jnp.cos(index.astype(jnp.float32) * np.float32(2.0 * np.pi / points))
    side = which[:, :, None, None] == jnp.arange(2, dtype=jnp.int32)[None, None, :, None]
    table = jnp.where(side, wave[:, :, None, :], jnp.float32(0.0))
    back = jnp.transpose(table * scale[:, None, :, None], (0, 2, 3, 1))
    width = 2 * GROUP * block
    return (
        table.reshape(owned, depth, width),
        back.reshape(owned, width, depth),
        base.reshape(-1),
    )


def local_kernel(
    coupling, kappa, flags, adj, before, after, src, mu, mu_before, mu_after, low, high, out
):
    fields, planes, rows, cells = adj.shape
    step = pl.program_id(0)
    first = step == 0
    last = step == pl.num_programs(0) - 1
    row = lax.broadcasted_iota(jnp.int32, (rows, cells), 0)
    col = lax.broadcasted_iota(jnp.int32, (rows, cells), 1)
    ring = 0.5 / (row.astype(jnp.float32) + 1.0)

    def pick(source, behind, ahead, f, k):
        if k < 0:
            return jnp.where(first, low[f, 0], behind)
        if k >= planes:
            return jnp.where(last, high[f, 0], ahead)
        return source

    def visc(k):
        return pick(mu[max(0, min(k, planes - 1))], mu_before[0], mu_after[0], fields, k)

    def cell(f, k):
        return pick(adj[f, max(0, min(k, planes - 1))], before[f, 0], after[f, 0], f, k)

    for k in range(planes):
        m = visc(k)
        up = ring * (m + visc(k + 1))
        down = ring * (m + visc(k - 1))
        outer = jnp.where(row < rows - 1, 0.5 * (m + pltpu.roll(m, rows - 1, 0)), 0.0)
        inner = jnp.where(row > 0, 0.5 * (m + pltpu.roll(m, 1, 0)), 0.0)
        east = jnp.where(col < cells - 1, 0.5 * (m + pltpu.roll(m, cells - 1, 1)), 0.0)
        west = jnp.where(col > 0, 0.5 * (m + pltpu.roll(m, 1, 1)), 0.0)
        diag = up + down + outer + inner + east + west
        for f in range(fields):
            p = adj[f, k]
            opens = [(1 - flags[f, i]).astype(jnp.float32) for i in range(3)]
            wall = jnp.where(col == 0, opens[0], 0.0)
            wall = wall + jnp.where(col == cells - 1, opens[1], 0.0)
            wall = wall + jnp.where(row == rows - 1, opens[2], 0.0)
            flux = (diag + wall * m) * p
            flux = flux - up * cell(f, k + 1) - down * cell(f, k - 1)
            flux = flux - outer * pltpu.roll(p, rows - 1, 0) - inner * pltpu.roll(p, 1, 0)
            flux = flux - east * pltpu.roll(p, cells - 1, 1) - west * pltpu.roll(p, 1, 1)
            total = src[f, k] + kappa[f] * flux
            for g in range(fields):
                total = total + coupling[g, f] * adj[g, k]
            out[f, k] = total


def local_part(center, source, viscosity, kappa, coupling, flags, low, high):
    fields, block, rows, cells = center.shape
    planes = min(4, block)
    steps = block // planes
    whole = lambda width, index: pl.BlockSpec((fields, width, rows, cells), lambda i: (0, index(i), 0, 0))
    plane = lambda width, index: pl.BlockSpec((width, rows, cells), lambda i: (index(i), 0, 0))
    behind = lambda i: jnp.maximum(i * planes - 1, 0)
    ahead = lambda i: jnp.minimum(i * planes + planes, block - 1)
    here = lambda i: i
    halo = pl.BlockSpec((fields + 1, 1, rows, cells), lambda i: (0, 0, 0, 0))
    return pl.pallas_call(
        local_kernel,
        grid=(steps,),
        in_specs=[
            SMEM,
            SMEM,
            SMEM,
            whole(planes, here),
            whole(1, behind),
            whole(1, ahead),
            whole(planes, here),
            plane(planes, here),
            plane(1, behind),
            plane(1, ahead),
            halo,
            halo,
        ],
        out_specs=whole(planes, here),
        out_shape=jax.ShapeDtypeStruct(center.shape, jnp.float32),
        compiler_params=pltpu.CompilerParams(vmem_limit_bytes=VMEM_LIMIT),
        cost_estimate=pl.CostEstimate(
            flops=40 * center.size, bytes_accessed=16 * center.size, transcendentals=0
        ),
        name="local_part",
    )(coupling, kappa, flags, center, center, center, source, viscosity, viscosity, viscosity, low, high)


def sums(coef, local, others):
    steps = (len(others) - 2) // 2
    half = local.shape[1] // 2
    far_hi, mix_lo = others[:steps], others[steps]
    far_lo, mix_hi = others[steps + 1], others[steps + 2 :]
    top = local[0, :half] + mix_lo[0]
    for s in range(steps):
        top = top + coef[s] * far_hi[s][0]
    bottom = local[0, half:] + coef[steps] * far_lo[0]
    for s in range(steps):
        bottom = bottom + mix_hi[s][0]
    return top, bottom


def spread_kernel(count, rank, coef, local, *refs):
    others, outs, (flat, stage) = refs[:count], refs[count : count + GROUP], refs[count + GROUP :]
    top, bottom = sums(coef, local, others)
    block, near, cells = local.shape[1:]
    size = top.shape[0] * near
    flat[:size] = top.reshape(size, cells)
    flat[size:] = bottom.reshape(size, cells)
    pairs = near // 2
    owned = pairs // GROUP
    for o in range(GROUP):
        for j in range(owned):
            for a in range(2):
                r = o * owned + j + a * pairs
                stage[o, 2 * j + a] = flat[pl.ds(r, block, stride=near), :]
    for k in range(GROUP):
        outs[k][0] = stage[rank[0] ^ k]


def spread(rank, coef, local, others, first, fields, near):
    block, rows, cells = local.shape[1:]
    cycles = near // GROUP
    part = lambda width: pl.BlockSpec((1, width, near, cells), lambda i: (i, 0, 0, 0))
    return pl.pallas_call(
        functools.partial(spread_kernel, len(others)),
        grid=(fields,),
        in_specs=[SMEM, SMEM, pl.BlockSpec((1, block, near, cells), lambda i: (first + i, 0, 0, 0))]
        + [part(block // 2)] * len(others),
        out_specs=[pl.BlockSpec((1, cycles, block, cells), lambda i: (i, 0, 0, 0))] * GROUP,
        out_shape=[jax.ShapeDtypeStruct((fields, cycles, block, cells), jnp.float32)] * GROUP,
        scratch_shapes=[
            pltpu.VMEM((block * near, cells), jnp.float32),
            pltpu.VMEM((GROUP, cycles, block, cells), jnp.float32),
        ],
        compiler_params=pltpu.CompilerParams(vmem_limit_bytes=VMEM_LIMIT),
        cost_estimate=pl.CostEstimate(
            flops=4 * fields * block * near * cells,
            bytes_accessed=16 * fields * block * near * cells,
            transcendentals=0,
        ),
        name="spread",
    )(rank, coef, local, *others)


def coefficient_kernel(table, *refs):
    parts, out = refs[:GROUP], refs[GROUP]
    for j in range(table.shape[0]):
        column = jnp.concatenate([parts[k][0, 2 * j + a] for a in range(2) for k in range(GROUP)], axis=0)
        out[0, j] = jnp.dot(
            table[j], column, precision=lax.Precision.HIGHEST, preferred_element_type=jnp.float32
        )


def coefficients(table, parts):
    fields, cycles, block, cells = parts[0].shape
    owned, depth, width = table.shape
    return pl.pallas_call(
        coefficient_kernel,
        grid=(fields,),
        in_specs=[pl.BlockSpec(table.shape, lambda i: (0, 0, 0))]
        + [pl.BlockSpec((1, cycles, block, cells), lambda i: (i, 0, 0, 0))] * GROUP,
        out_specs=pl.BlockSpec((1, owned, depth, cells), lambda i: (i, 0, 0, 0)),
        out_shape=jax.ShapeDtypeStruct((fields, owned, depth, cells), jnp.float32),
        compiler_params=pltpu.CompilerParams(vmem_limit_bytes=VMEM_LIMIT),
        cost_estimate=pl.CostEstimate(
            flops=12 * fields * owned * depth * width * cells,
            bytes_accessed=4 * (table.size + fields * owned * (depth + width) * cells),
            transcendentals=0,
        ),
        name="coefficients",
    )(table, *parts)


def filtered_kernel(base, back, own, other, *refs):
    parts, outs = refs[:GROUP], refs[GROUP:]
    block = parts[0].shape[2]
    for j in range(back.shape[0]):
        total = own[0, j] + other[0, j]
        waves = jnp.dot(
            back[j], total, precision=lax.Precision.HIGHEST, preferred_element_type=jnp.float32
        )
        for a in range(2):
            for k in range(GROUP):
                start = (a * GROUP + k) * block
                outs[k][0, 2 * j + a] = (
                    base[2 * j + a] * parts[k][0, 2 * j + a] + waves[start : start + block]
                )


def filtered(base, back, own, other, parts):
    fields, cycles, block, cells = parts[0].shape
    owned, width, depth = back.shape
    part = pl.BlockSpec((1, cycles, block, cells), lambda i: (i, 0, 0, 0))
    modes = pl.BlockSpec((1, owned, depth, cells), lambda i: (i, 0, 0, 0))
    return pl.pallas_call(
        filtered_kernel,
        grid=(fields,),
        in_specs=[SMEM, pl.BlockSpec(back.shape, lambda i: (0, 0, 0)), modes, modes] + [part] * GROUP,
        out_specs=[part] * GROUP,
        out_shape=[jax.ShapeDtypeStruct(parts[0].shape, jnp.float32)] * GROUP,
        compiler_params=pltpu.CompilerParams(vmem_limit_bytes=VMEM_LIMIT),
        cost_estimate=pl.CostEstimate(
            flops=12 * fields * owned * depth * width * cells,
            bytes_accessed=4 * (back.size + 2 * fields * owned * (depth + width) * cells),
            transcendentals=0,
        ),
        name="filtered",
    )(base, back, own, other, *parts)


def near_kernel(rank, *refs):
    parts, out, stage = refs[:GROUP], refs[-2], refs[-1]
    near = out.shape[2]
    pairs = near // 2
    owned = pairs // GROUP
    for k in range(GROUP):
        stage[rank[0] ^ k] = parts[k][0]
    for o in range(GROUP):
        for j in range(owned):
            for a in range(2):
                out[0, :, o * owned + j + a * pairs, :] = stage[o, 2 * j + a]


def place_near(rank, parts, held, first, shape, near):
    fields, cycles, block, cells = parts[0].shape
    carried = [] if held is None else [held]
    return pl.pallas_call(
        near_kernel,
        grid=(fields,),
        in_specs=[SMEM]
        + [pl.BlockSpec((1, cycles, block, cells), lambda i: (i, 0, 0, 0))] * GROUP
        + [pl.BlockSpec(memory_space=pl.ANY)] * len(carried),
        out_specs=pl.BlockSpec((1, block, near, cells), lambda i: (first + i, 0, 0, 0)),
        out_shape=jax.ShapeDtypeStruct(shape, jnp.float32),
        scratch_shapes=[pltpu.VMEM((GROUP, cycles, block, cells), jnp.float32)],
        input_output_aliases={1 + GROUP: 0} if carried else {},
        compiler_params=pltpu.CompilerParams(vmem_limit_bytes=VMEM_LIMIT),
        cost_estimate=pl.CostEstimate(
            flops=0, bytes_accessed=8 * fields * block * near * cells, transcendentals=0
        ),
        name="place_near",
    )(rank, *parts, *carried)


def far_kernel(coef, local, *refs):
    others, out = refs[:-2], refs[-1]
    half = local.shape[1] // 2
    top, bottom = sums(coef, local, others)
    out[0, :half] = top
    out[0, half:] = bottom


def place_far(coef, local, others, held, first, fields, near):
    block, rows, cells = local.shape[1:]
    side = pl.BlockSpec((1, block, near, cells), lambda i: (first + i, 0, 1, 0))
    return pl.pallas_call(
        far_kernel,
        grid=(fields,),
        in_specs=[SMEM, side]
        + [pl.BlockSpec((1, block // 2, near, cells), lambda i: (i, 0, 0, 0))] * len(others)
        + [pl.BlockSpec(memory_space=pl.ANY)],
        out_specs=side,
        out_shape=jax.ShapeDtypeStruct(held.shape, jnp.float32),
        input_output_aliases={2 + len(others): 0},
        compiler_params=pltpu.CompilerParams(vmem_limit_bytes=VMEM_LIMIT),
        cost_estimate=pl.CostEstimate(
            flops=4 * fields * block * near * cells,
            bytes_accessed=16 * fields * block * near * cells,
            transcendentals=0,
        ),
        name="place_far",
    )(coef, local, *others, held)


def spans(sizes, total):
    ends = np.minimum(np.cumsum(sizes), total)
    ends[-1] = total
    starts = np.concatenate([[0], ends[:-1]])
    return [(int(s), int(e)) for s, e in zip(starts, ends) if e > s]


def body(adjoint, source, viscosity, kappa, coupling, bc_flags, inst_map):
    slots = lax.axis_size("inst")
    sectors = lax.axis_size("space")
    center = adjoint[0]
    fields, block, cycles, cells = center.shape
    near = cycles // 2
    half = block // 2
    span = slots // 2

    def turned(i, s):
        return ((i // 2 + s) % span) * 2 + i % 2

    def to_pair(x):
        return lax.ppermute(x, "inst", [(i, i ^ 1) for i in range(slots)])

    def to_turned(x, s):
        return lax.ppermute(x, "inst", [(i, turned(i, s)) for i in range(slots)])

    def to_sector(x, k):
        return lax.ppermute(x, "space", [(i, i ^ k) for i in range(sectors)])

    matrix = spectral_matrix(inst_map, slots)
    slot = lax.axis_index("inst")
    pair = slot ^ 1
    weight = lambda i, j: matrix[i, j]
    shifts = range(1, span)
    coef = jnp.stack([weight(turned(slot, span - s), slot) for s in shifts] + [weight(pair, slot)])

    def first_step(lo, hi, base):
        top = center[lo:hi, :half, base : base + near]
        bottom = center[lo:hi, half:, base : base + near]
        return top, bottom, [to_turned(top, s) for s in shifts], to_pair(bottom)

    def second_step(top, bottom, hi_parts, lo_part):
        mix = weight(slot, pair) * top
        for s, part in zip(shifts, hi_parts):
            mix = mix + weight(turned(slot, span - s), pair) * part
        mix_lo = to_pair(mix)
        mix_hi = []
        for s in shifts:
            target = turned(slot, s)
            mix_hi.append(
                to_turned(weight(slot, target) * bottom + weight(pair, target) * lo_part, s)
            )
        return hi_parts + [mix_lo, lo_part] + mix_hi

    near_spans = spans(NEAR_SIZES, fields)
    far_spans = spans(FAR_SIZES, fields)

    def edge(start):
        return jnp.concatenate(
            [center[:, start : start + 1], viscosity[None, start : start + 1]], axis=0
        )

    ring = lambda step: [(i, (i + step) % sectors) for i in range(sectors)]
    low = lax.ppermute(edge(block - 1), "space", ring(1))
    high = lax.ppermute(edge(0), "space", ring(-1))

    local = local_part(center, source[0], viscosity, kappa, coupling, bc_flags, low, high)

    place = lax.axis_index("space")
    rank = (place % GROUP).reshape(1)
    points = block * sectors
    table, back, base = filter_tables(points, near, block, place)

    result = None
    for lo, hi in near_spans:
        others = second_step(*first_step(lo, hi, 0))
        mine = spread(rank, coef, local, others, lo, hi - lo, near)
        parts = [mine[0]] + [to_sector(mine[k], k) for k in range(1, GROUP)]
        own = coefficients(table, parts)
        stride = GROUP
        while 2 * stride < sectors:
            own = own + to_sector(own, stride)
            stride = 2 * stride
        other = to_sector(own, stride) if stride < sectors else jnp.zeros_like(own)
        done = filtered(base, back, own, other, parts)
        done = [done[0]] + [to_sector(done[k], k) for k in range(1, GROUP)]
        result = place_near(rank, done, result, lo, center.shape, near)
    for lo, hi in far_spans:
        others = second_step(*first_step(lo, hi, near))
        result = place_far(coef, local, others, result, lo, hi - lo, near)
    return result[None]


def solution(mesh):
    return jax.shard_map(
        body,
        mesh=mesh,
        in_specs=(
            P("inst", None, "space", None, None),
            P("inst", None, "space", None, None),
            P("space", None, None),
            P(),
            P(),
            P(),
            P(),
        ),
        out_specs=P("inst", None, "space", None, None),
        check_vma=False,
    )
```

```python
import functools

import jax
import jax.numpy as jnp
import numpy as np
from jax import lax
from jax.experimental import pallas as pl
from jax.experimental.pallas import tpu as pltpu
from jax.sharding import PartitionSpec as P

QUAD = 4
NEAR_SIZES = (2, 2, 1)
FAR_SIZES = (3, 2)
ORDER = (
    ("pack", 0),
    ("pack", 1),
    ("local", 0),
    ("mix", 0),
    ("mix", 1),
    ("spread", 0),
    ("pack", 2),
    ("coef", 0),
    ("spread", 1),
    ("pack", 3),
    ("mix", 2),
    ("spread", 2),
    ("pack", 4),
    ("coef", 1),
    ("filter", 0),
    ("mix", 3),
    ("coef", 2),
    ("near", 0),
    ("filter", 1),
    ("mix", 4),
    ("near", 1),
    ("filter", 2),
    ("far", 3),
    ("near", 2),
    ("far", 4),
)
SMEM = pl.BlockSpec(memory_space=pltpu.SMEM)
ANY = pl.BlockSpec(memory_space=pl.ANY)
PARAMS = pltpu.CompilerParams(vmem_limit_bytes=48 * 1024 * 1024)


def spectral_values(slots):
    offset = np.arange(1 - slots, slots)
    safe = np.where(offset == 0, 1.0, np.sin(np.pi * offset / slots))
    return np.where(offset == 0, 0.0, 0.5 * (1.0 - 2.0 * (np.abs(offset) % 2)) / safe)


def mode_layout(points, near):
    half = points // 2
    pairs = near // 2
    theta = np.arange(points)
    bases, base, scale = [], np.zeros(near), np.zeros(near)
    for r in range(near):
        cutoff = max(4, points * (r + 1) // (2 * near))
        weight = max(1.0 - r / near, 0.0)
        kept = [m for m in range(half + 1) if m < cutoff]
        out = [m for m in range(half + 1) if m >= cutoff]
        count = [sum(1 if m in (0, half) else 2 for m in modes) for modes in (kept, out)]
        low = count[0] <= count[1]
        rows = []
        for m in kept if low else out:
            angle = 2.0 * np.pi * (m * theta % points) / points
            if m in (0, half):
                rows.append(np.cos(angle) / np.sqrt(points))
            else:
                rows.append(np.cos(angle) * np.sqrt(2.0 / points))
                rows.append(np.sin(angle) * np.sqrt(2.0 / points))
        bases.append(rows)
        base[r] = 1.0 - weight if low else 1.0
        scale[r] = weight if low else -weight
    depth = max(len(bases[p]) + len(bases[p + pairs]) for p in range(pairs))
    depth = -(-depth // 8) * 8
    table = np.zeros((pairs, depth, points), np.float32)
    split = np.zeros(pairs, np.int32)
    for p in range(pairs):
        rows = bases[p] + bases[p + pairs]
        table[p, : len(rows)] = np.stack(rows)
        split[p] = len(bases[p])
    return table, split, base, scale


class Scalars:
    def __init__(self, ints, reals, slots, near):
        self.ints, self.reals, self.slots, self.near = ints, reals, slots, near
        self.slot, self.place = ints[0], ints[1]
        self.rank = self.place % QUAD

    def weight(self, i, j):
        return self.reals[self.ints[2 + i] - self.ints[2 + j] + self.slots - 1]

    def split(self, pair):
        return self.ints[2 + self.slots + pair]

    def base(self, r):
        return self.reals[2 * self.slots - 1 + r]

    def scale(self, r):
        return self.reals[2 * self.slots - 1 + self.near + r]

    def first(self):
        return first_partner(self.slot, self.place % 2, self.slots)

    def target(self, s):
        return later_partner(self.slot, self.place % 2, self.slots, s)


def first_partner(slot, core, slots):
    if slots == 4:
        return slot ^ (2 - core)
    return slot ^ 1


def later_partner(slot, core, slots, s):
    if slots == 4:
        return slot ^ (1 + core)
    return (slot // 2 + s) % (slots // 2) * 2 + slot % 2


def call(kernel, name, token, grid, inputs, in_specs, out_specs, out_shape, scratch=(), cost=(0, 0), alias=None):
    extra = [] if token is None else [token]
    return pl.pallas_call(
        lambda *refs: kernel(*refs[: len(inputs)], *refs[len(inputs) + len(extra) :]),
        grid=grid,
        in_specs=list(in_specs) + [ANY] * len(extra),
        out_specs=out_specs,
        out_shape=out_shape,
        scratch_shapes=list(scratch),
        input_output_aliases=alias or {},
        compiler_params=PARAMS,
        cost_estimate=pl.CostEstimate(flops=cost[0], bytes_accessed=cost[1], transcendentals=0),
        name=name,
    )(*inputs, *extra)


def shaped(*shape):
    return jax.ShapeDtypeStruct(shape, jnp.float32)


def pack(center, viscosity, lo, hi, base, near, edges, token):
    fields, block, rows, cells = center.shape

    def kernel(center, viscosity, *refs):
        outs, sem = refs[:-1], refs[-1]
        moves = [(center.at[pl.ds(lo, hi - lo), :, pl.ds(base, near)], outs[0])]
        if edges:
            for out, start in zip(outs[1:], (block - 1, 0)):
                moves.append((center.at[:, pl.ds(start, 1)], out.at[pl.ds(0, fields)]))
                moves.append((viscosity.at[pl.ds(start, 1)], out.at[fields]))
        copies = [pltpu.make_async_copy(a, b, sem.at[i]) for i, (a, b) in enumerate(moves)]
        for copy in copies:
            copy.start()
        for copy in copies:
            copy.wait()

    shapes = [shaped(hi - lo, block, near, cells)]
    if edges:
        shapes += [shaped(fields + 1, 1, rows, cells)] * 2
    return call(
        kernel,
        "pack",
        token,
        (),
        [center, viscosity],
        [ANY, ANY],
        [ANY] * len(shapes),
        shapes,
        [pltpu.SemaphoreType.DMA((5,))],
        (0, 8 * (hi - lo) * block * near * cells),
    )


def local_kernel(
    coupling, kappa, flags, adj, before, after, src, mu, mu_before, mu_after, low, high, out
):
    fields, planes, rows, cells = adj.shape
    step = pl.program_id(0)
    first = step == 0
    last = step == pl.num_programs(0) - 1
    row = lax.broadcasted_iota(jnp.int32, (rows, cells), 0)
    col = lax.broadcasted_iota(jnp.int32, (rows, cells), 1)
    ring = 0.5 / (row.astype(jnp.float32) + 1.0)

    def pick(source, behind, ahead, f, k):
        if k < 0:
            return jnp.where(first, low[f, 0], behind)
        if k >= planes:
            return jnp.where(last, high[f, 0], ahead)
        return source

    def visc(k):
        return pick(mu[max(0, min(k, planes - 1))], mu_before[0], mu_after[0], fields, k)

    def cell(f, k):
        return pick(adj[f, max(0, min(k, planes - 1))], before[f, 0], after[f, 0], f, k)

    for k in range(planes):
        m = visc(k)
        up = ring * (m + visc(k + 1))
        down = ring * (m + visc(k - 1))
        outer = jnp.where(row < rows - 1, 0.5 * (m + pltpu.roll(m, rows - 1, 0)), 0.0)
        inner = jnp.where(row > 0, 0.5 * (m + pltpu.roll(m, 1, 0)), 0.0)
        east = jnp.where(col < cells - 1, 0.5 * (m + pltpu.roll(m, cells - 1, 1)), 0.0)
        west = jnp.where(col > 0, 0.5 * (m + pltpu.roll(m, 1, 1)), 0.0)
        diag = up + down + outer + inner + east + west
        for f in range(fields):
            p = adj[f, k]
            opens = [(1 - flags[f, i]).astype(jnp.float32) for i in range(3)]
            wall = jnp.where(col == 0, opens[0], 0.0)
            wall = wall + jnp.where(col == cells - 1, opens[1], 0.0)
            wall = wall + jnp.where(row == rows - 1, opens[2], 0.0)
            flux = (diag + wall * m) * p
            flux = flux - up * cell(f, k + 1) - down * cell(f, k - 1)
            flux = flux - outer * pltpu.roll(p, rows - 1, 0) - inner * pltpu.roll(p, 1, 0)
            flux = flux - east * pltpu.roll(p, cells - 1, 1) - west * pltpu.roll(p, 1, 1)
            total = src[f, k] + kappa[f] * flux
            for g in range(fields):
                total = total + coupling[g, f] * adj[g, k]
            out[f, k] = total


def local_part(center, source, viscosity, kappa, coupling, flags, low, high, token):
    fields, block, rows, cells = center.shape
    planes = min(4, block)

    def whole(width, index):
        return pl.BlockSpec((fields, width, rows, cells), lambda i: (0, index(i), 0, 0))

    def plane(width, index):
        return pl.BlockSpec((width, rows, cells), lambda i: (index(i), 0, 0))

    behind = lambda i: jnp.maximum(i * planes - 1, 0)
    ahead = lambda i: jnp.minimum(i * planes + planes, block - 1)
    here = lambda i: i
    halo = pl.BlockSpec((fields + 1, 1, rows, cells), lambda i: (0, 0, 0, 0))
    return call(
        local_kernel,
        "local_part",
        token,
        (block // planes,),
        [coupling, kappa, flags, center, center, center, source, viscosity, viscosity, viscosity, low, high],
        [
            SMEM,
            SMEM,
            SMEM,
            whole(planes, here),
            whole(1, behind),
            whole(1, ahead),
            whole(planes, here),
            plane(planes, here),
            plane(1, behind),
            plane(1, ahead),
            halo,
            halo,
        ],
        whole(planes, here),
        shaped(*center.shape),
        cost=(40 * center.size, 16 * center.size),
    )


def sums(scalars, local, others):
    total = local[0] + scalars.weight(scalars.first(), scalars.slot) * others[0][0]
    for part in others[1:]:
        total = total + part[0]
    return total


class Plan:
    def __init__(self, ints, reals, slots, shape, near, table, back):
        self.ints, self.reals, self.slots, self.near = ints, reals, slots, near
        self.shape, self.table, self.back = shape, table, back
        self.fields, self.block, self.rows, self.cells = shape
        self.pairs = near // 2
        self.owned = self.pairs // QUAD
        self.cycles = near // QUAD
        self.depth = table.shape[2]

    def scalars(self, ints, reals):
        return Scalars(ints, reals, self.slots, self.near)

    def side(self, first, index):
        return pl.BlockSpec((1, self.block, self.near, self.cells), lambda i: (first + i, 0, index, 0))

    def part(self):
        return pl.BlockSpec((1, self.cycles, self.block, self.cells), lambda i: (i, 0, 0, 0))

    def size(self, fields):
        return fields * self.block * self.near * self.cells

    def mix(self, center, first, lo, hi, index, token):
        count = max(1, self.slots // 2 - 1)

        def kernel(ints, reals, own, got, *outs):
            scalars = self.scalars(ints, reals)
            for s in range(count):
                target = scalars.target(s + 1)
                outs[s][0] = (
                    scalars.weight(scalars.slot, target) * own[0]
                    + scalars.weight(scalars.first(), target) * got[0]
                )

        return call(
            kernel,
            "mix",
            token,
            (hi - lo,),
            [self.ints, self.reals, center, first],
            [SMEM, SMEM, self.side(lo, index), self.side(0, 0)],
            [self.side(0, 0)] * count,
            [shaped(hi - lo, self.block, self.near, self.cells)] * count,
            cost=(3 * self.size(hi - lo), 12 * self.size(hi - lo)),
        )

    def spread(self, local, others, lo, hi, token):
        def kernel(ints, reals, local, *refs):
            others, outs = refs[: len(refs) - QUAD - 2], refs[-QUAD - 2 : -2]
            flat, stage = refs[-2:]
            scalars = self.scalars(ints, reals)
            flat[...] = sums(scalars, local, others).reshape(flat.shape)
            for o in range(QUAD):
                for j in range(self.owned):
                    for a in range(2):
                        r = o * self.owned + j + a * self.pairs
                        stage[o, 2 * j + a] = flat[pl.ds(r, self.block, stride=self.near), :]
            for k in range(QUAD):
                outs[k][0] = stage[scalars.rank ^ k]

        return call(
            kernel,
            "spread",
            token,
            (hi - lo,),
            [self.ints, self.reals, local] + others,
            [SMEM, SMEM, self.side(lo, 0)] + [self.side(0, 0)] * len(others),
            [self.part()] * QUAD,
            [shaped(hi - lo, self.cycles, self.block, self.cells)] * QUAD,
            [
                pltpu.VMEM((self.block * self.near, self.cells), jnp.float32),
                pltpu.VMEM((QUAD, self.cycles, self.block, self.cells), jnp.float32),
            ],
            (4 * self.size(hi - lo), 16 * self.size(hi - lo)),
        )

    def own_rows(self, shape):
        return pl.BlockSpec(
            (1, self.owned) + shape, lambda i, ints: (ints[1] // QUAD, ints[1] % QUAD, 0, 0)
        )

    def table_call(self, kernel, name, fields, inputs, in_specs, out_specs, out_shape, scratch, token):
        extra = [] if token is None else [token]
        count = len(inputs)
        return pl.pallas_call(
            lambda *refs: kernel(*refs[: count + 1], *refs[count + 1 + len(extra) :]),
            grid_spec=pltpu.PrefetchScalarGridSpec(
                num_scalar_prefetch=1,
                grid=(fields,),
                in_specs=in_specs + [ANY] * len(extra),
                out_specs=out_specs,
                scratch_shapes=scratch,
            ),
            out_shape=out_shape,
            compiler_params=PARAMS,
            cost_estimate=pl.CostEstimate(
                flops=12 * self.size(fields) * self.depth,
                bytes_accessed=16 * self.size(fields),
                transcendentals=0,
            ),
            name=name,
        )(self.ints, *inputs, *extra)

    def block4(self, *shape):
        return pl.BlockSpec((1,) + shape, lambda i, ints: (i, 0, 0, 0))

    def coefficients(self, parts, token):
        fields = parts[0].shape[0]

        def kernel(ints, reals, table, *refs):
            parts, out, column = refs[:QUAD], refs[QUAD], refs[QUAD + 1]
            scalars = self.scalars(ints, reals)
            row = lax.broadcasted_iota(jnp.int32, (self.depth, self.cells), 0)
            for k in range(QUAD):
                column[:, scalars.rank ^ k] = parts[k][0]
            for j in range(self.owned):
                modes = [
                    jnp.dot(
                        table[0, j],
                        column[2 * j + a].reshape(QUAD * self.block, self.cells),
                        precision=lax.Precision.HIGHEST,
                        preferred_element_type=jnp.float32,
                    )
                    for a in range(2)
                ]
                split = scalars.split(scalars.rank * self.owned + j)
                out[0, j] = jnp.where(row < split, modes[0], modes[1])

        return self.table_call(
            kernel,
            "coefficients",
            fields,
            [self.reals, self.table] + parts,
            [SMEM, self.own_rows(self.table.shape[2:])]
            + [self.block4(self.cycles, self.block, self.cells)] * QUAD,
            self.block4(self.owned, self.depth, self.cells),
            shaped(fields, self.owned, self.depth, self.cells),
            [pltpu.VMEM((self.cycles, QUAD, self.block, self.cells), jnp.float32)],
            token,
        )

    def filtered(self, own, other, parts, token):
        fields = parts[0].shape[0]

        def kernel(ints, reals, back, own, other, *refs):
            parts, outs, waves = refs[:QUAD], refs[QUAD : 2 * QUAD], refs[2 * QUAD]
            scalars = self.scalars(ints, reals)
            row = lax.broadcasted_iota(jnp.int32, (self.depth, self.cells), 0)
            for j in range(self.owned):
                pair = scalars.rank * self.owned + j
                total = own[0, j] + other[0, j]
                keep = row < scalars.split(pair)
                for a in range(2):
                    waves[2 * j + a] = jnp.dot(
                        back[0, j],
                        jnp.where(keep if a == 0 else jnp.logical_not(keep), total, 0.0),
                        precision=lax.Precision.HIGHEST,
                        preferred_element_type=jnp.float32,
                    ).reshape(QUAD, self.block, self.cells)
                    r = pair + a * self.pairs
                    for k in range(QUAD):
                        outs[k][0, 2 * j + a] = (
                            scalars.base(r) * parts[k][0, 2 * j + a]
                            + scalars.scale(r) * waves[2 * j + a, scalars.rank ^ k]
                        )

        part = self.block4(self.cycles, self.block, self.cells)
        modes = self.block4(self.owned, self.depth, self.cells)
        return self.table_call(
            kernel,
            "filtered",
            fields,
            [self.reals, self.back, own, other] + parts,
            [SMEM, self.own_rows(self.back.shape[2:]), modes, modes] + [part] * QUAD,
            [part] * QUAD,
            [shaped(*parts[0].shape)] * QUAD,
            [pltpu.VMEM((self.cycles, QUAD, self.block, self.cells), jnp.float32)],
            token,
        )

    def place_near(self, parts, held, lo, hi, token):
        def kernel(ints, reals, *refs):
            parts, out, stage = refs[:QUAD], refs[-2], refs[-1]
            scalars = self.scalars(ints, reals)
            for k in range(QUAD):
                stage[scalars.rank ^ k] = parts[k][0]
            for o in range(QUAD):
                for j in range(self.owned):
                    for a in range(2):
                        out[0, :, o * self.owned + j + a * self.pairs, :] = stage[o, 2 * j + a]

        carried = [] if held is None else [held]
        return call(
            kernel,
            "place_near",
            token,
            (hi - lo,),
            [self.ints, self.reals] + parts + carried,
            [SMEM, SMEM] + [self.part()] * QUAD + [ANY] * len(carried),
            self.side(lo, 0),
            shaped(*self.shape),
            [pltpu.VMEM((QUAD, self.cycles, self.block, self.cells), jnp.float32)],
            (0, 8 * self.size(hi - lo)),
            {2 + QUAD: 0} if carried else None,
        )

    def place_far(self, local, others, held, lo, hi, token):
        def kernel(ints, reals, local, *refs):
            others, out = refs[: len(refs) - 1 - len(carried)], refs[-1]
            out[0] = sums(self.scalars(ints, reals), local, others)

        carried = [] if held is None else [held]
        return call(
            kernel,
            "place_far",
            token,
            (hi - lo,),
            [self.ints, self.reals, local] + others + carried,
            [SMEM, SMEM, self.side(lo, 1)]
            + [self.side(0, 0)] * len(others)
            + [ANY] * len(carried),
            self.side(lo, 1),
            shaped(*self.shape),
            (),
            (4 * self.size(hi - lo), 16 * self.size(hi - lo)),
            {3 + len(others): 0} if carried else None,
        )


def spans(sizes, total):
    ends = np.cumsum(sizes)
    return [(int(end - size), int(end)) for size, end in zip(sizes, ends)]


def body(adjoint, source, viscosity, kappa, coupling, bc_flags, inst_map):
    slots = lax.axis_size("inst")
    sectors = lax.axis_size("space")
    center = adjoint[0]
    fields, block, cycles, cells = center.shape
    near = cycles // 2
    points = block * sectors
    quads = sectors // QUAD

    def to_partner(x, pick):
        pairs = []
        for i in range(slots):
            for p in range(sectors):
                pairs.append((i * sectors + p, pick(i, p % 2) * sectors + p))
        return lax.ppermute(x, ("inst", "space"), pairs)

    def to_first(x):
        return to_partner(x, lambda i, core: first_partner(i, core, slots))

    def to_later(x, s):
        return to_partner(x, lambda i, core: later_partner(i, core, slots, s))

    def to_sector(x, k):
        return lax.ppermute(x, "space", [(i, i ^ k) for i in range(sectors)])

    def ring(x, step):
        return lax.ppermute(x, "space", [(i, (i + step) % sectors) for i in range(sectors)])

    table, split, base, scale = mode_layout(points, near)
    table = table.reshape(table.shape[0], table.shape[1], quads, QUAD * block).transpose(2, 0, 1, 3)
    here = jnp.stack([lax.axis_index("inst"), lax.axis_index("space")])
    ints = jnp.concatenate([here, inst_map, jnp.asarray(split)])
    reals = jnp.asarray(np.concatenate([spectral_values(slots), base, scale]).astype(np.float32))
    plan = Plan(
        ints,
        reals,
        slots,
        center.shape,
        near,
        jnp.asarray(np.ascontiguousarray(table)),
        jnp.asarray(np.ascontiguousarray(table.transpose(0, 1, 3, 2))),
    )

    groups = [(lo, hi, 0) for lo, hi in spans(NEAR_SIZES, fields)]
    groups += [(lo, hi, 1) for lo, hi in spans(FAR_SIZES, fields)]
    first, others, parts, own, done = {}, {}, {}, {}, {}
    token, local, held, halos = None, None, None, None
    for step, g in ORDER:
        lo, hi, index = groups[g]
        if step == "pack":
            packed = pack(center, viscosity, lo, hi, index * near, near, halos is None, token)
            token = packed[0]
            first[g] = to_first(packed[0])
            if halos is None:
                halos = ring(packed[1], 1), ring(packed[2], -1)
        elif step == "local":
            local = token = local_part(
                center, source[0], viscosity, kappa, coupling, bc_flags, *halos, token
            )
        elif step == "mix":
            mixed = plan.mix(center, first[g], lo, hi, index, token)
            token = mixed[0]
            others[g] = [first[g]] + [to_later(x, s + 1) for s, x in enumerate(mixed)]
        elif step == "spread":
            mine = plan.spread(local, others[g], lo, hi, token)
            token = mine[0]
            parts[g] = [mine[0]] + [to_sector(mine[k], k) for k in range(1, QUAD)]
        elif step == "coef":
            part = token = plan.coefficients(parts[g], token)
            stride = QUAD
            while 2 * stride < sectors:
                part = part + to_sector(part, stride)
                stride = 2 * stride
            other = to_sector(part, stride) if stride < sectors else jnp.zeros_like(part)
            own[g] = part, other
        elif step == "filter":
            mine = plan.filtered(*own[g], parts[g], token)
            token = mine[0]
            done[g] = [mine[0]] + [to_sector(mine[k], k) for k in range(1, QUAD)]
        elif step == "near":
            held = token = plan.place_near(done[g], held, lo, hi, None if token is held else token)
        else:
            held = token = plan.place_far(
                local, others[g], held, lo, hi, None if token is held else token
            )
    return held[None]


def solution(mesh):
    return jax.shard_map(
        body,
        mesh=mesh,
        in_specs=(
            P("inst", None, "space", None, None),
            P("inst", None, "space", None, None),
            P("space", None, None),
            P(),
            P(),
            P(),
            P(),
        ),
        out_specs=P("inst", None, "space", None, None),
        check_vma=False,
    )
```

```python
import functools

import jax
import jax.numpy as jnp
import numpy as np
from jax import lax
from jax.experimental import pallas as pl
from jax.experimental.pallas import tpu as pltpu
from jax.sharding import PartitionSpec as P

QUAD = 4
NEAR_SIZES = (2, 2, 1)
FAR_SIZES = (3, 2)
ORDER = (
    ("pack", 0),
    ("pack", 1),
    ("local", 0),
    ("mix", 0),
    ("mix", 1),
    ("spread", 0),
    ("pack", 2),
    ("join", 0),
    ("spread", 1),
    ("pack", 3),
    ("coef", 0),
    ("join", 1),
    ("mix", 2),
    ("spread", 2),
    ("pack", 4),
    ("filter", 0),
    ("coef", 1),
    ("join", 2),
    ("mix", 3),
    ("back", 0),
    ("coef", 2),
    ("near", 0),
    ("filter", 1),
    ("mix", 4),
    ("back", 1),
    ("near", 1),
    ("filter", 2),
    ("far", 3),
    ("back", 2),
    ("near", 2),
    ("far", 4),
)
SMEM = pl.BlockSpec(memory_space=pltpu.SMEM)
ANY = pl.BlockSpec(memory_space=pl.ANY)
COST = pl.CostEstimate(flops=0, bytes_accessed=0, transcendentals=0)
PARAMS = pltpu.CompilerParams(vmem_limit_bytes=48 * 1024 * 1024)


def spectral_values(slots):
    offset = np.arange(1 - slots, slots)
    safe = np.where(offset == 0, 1.0, np.sin(np.pi * offset / slots))
    return np.where(offset == 0, 0.0, 0.5 * (1.0 - 2.0 * (np.abs(offset) % 2)) / safe)


def mode_layout(points, near):
    half = points // 2
    pairs = near // 2
    theta = np.arange(points)
    bases, base, scale = [], np.zeros(near), np.zeros(near)
    for r in range(near):
        cutoff = max(4, points * (r + 1) // (2 * near))
        weight = max(1.0 - r / near, 0.0)
        kept = [m for m in range(half + 1) if m < cutoff]
        out = [m for m in range(half + 1) if m >= cutoff]
        count = [sum(1 if m in (0, half) else 2 for m in modes) for modes in (kept, out)]
        low = count[0] <= count[1]
        rows = []
        for m in kept if low else out:
            angle = 2.0 * np.pi * (m * theta % points) / points
            if m in (0, half):
                rows.append(np.cos(angle) / np.sqrt(points))
            else:
                rows.append(np.cos(angle) * np.sqrt(2.0 / points))
                rows.append(np.sin(angle) * np.sqrt(2.0 / points))
        bases.append(rows)
        base[r] = 1.0 - weight if low else 1.0
        scale[r] = weight if low else -weight
    depth = max(len(bases[p]) + len(bases[p + pairs]) for p in range(pairs))
    depth = -(-depth // 8) * 8
    table = np.zeros((pairs, depth, points), np.float32)
    split = np.zeros(pairs, np.int32)
    for p in range(pairs):
        rows = bases[p] + bases[p + pairs]
        table[p, : len(rows)] = np.stack(rows)
        split[p] = len(bases[p])
    return table, split, base, scale


class Scalars:
    def __init__(self, ints, reals, slots, near):
        self.ints, self.reals, self.slots, self.near = ints, reals, slots, near
        self.slot, self.place = ints[0], ints[1]
        self.rank = self.place % QUAD

    def weight(self, i, j):
        return self.reals[self.ints[2 + i] - self.ints[2 + j] + self.slots - 1]

    def split(self, pair):
        return self.ints[2 + self.slots + pair]

    def base(self, r):
        return self.reals[2 * self.slots - 1 + r]

    def scale(self, r):
        return self.reals[2 * self.slots - 1 + self.near + r]

    def first(self):
        return first_partner(self.slot, self.place % 2, self.slots)

    def target(self, s):
        return later_partner(self.slot, self.place % 2, self.slots, s)


def first_partner(slot, core, slots):
    if slots == 4:
        return slot ^ (2 - core)
    return slot ^ 1


def later_partner(slot, core, slots, s):
    if slots == 4:
        return slot ^ (1 + core)
    return (slot // 2 + s) % (slots // 2) * 2 + slot % 2


def call(kernel, name, token, grid, inputs, in_specs, out_specs, out_shape, scratch=(), alias=None):
    extra = [] if token is None else [token]
    return pl.pallas_call(
        lambda *refs: kernel(*refs[: len(inputs)], *refs[len(inputs) + len(extra) :]),
        grid=grid,
        in_specs=list(in_specs) + [ANY] * len(extra),
        out_specs=out_specs,
        out_shape=out_shape,
        scratch_shapes=list(scratch),
        input_output_aliases=alias or {},
        compiler_params=PARAMS,
        cost_estimate=COST,
        name=name,
    )(*inputs, *extra)


def shaped(*shape):
    return jax.ShapeDtypeStruct(shape, jnp.float32)


def pack(center, viscosity, lo, hi, index, near, edges, token):
    fields, block, rows, cells = center.shape
    inputs, in_specs = [center], [pl.BlockSpec((1, block, near, cells), lambda i: (lo + i, 0, index, 0))]
    shapes = [shaped(hi - lo, block, near, cells)]
    out_specs = [pl.BlockSpec((1, block, near, cells), lambda i: (i, 0, 0, 0))]
    if edges:
        for start in (block - 1, 0):
            inputs += [center, viscosity]
            in_specs.append(pl.BlockSpec((fields, 1, rows, cells), lambda i, s=start: (0, s, 0, 0)))
            in_specs.append(pl.BlockSpec((1, rows, cells), lambda i, s=start: (s, 0, 0)))
            shapes.append(shaped(fields + 1, 1, rows, cells))
            out_specs.append(pl.BlockSpec((fields + 1, 1, rows, cells), lambda i: (0, 0, 0, 0)))

    def kernel(source, *refs):
        out, rest = refs[len(inputs) - 1], refs[len(inputs) :]
        out[...] = source[...]
        for e, edge in enumerate(rest):
            edge[:fields] = refs[2 * e][...]
            edge[fields] = refs[2 * e + 1][...]

    return call(kernel, "pack", token, (hi - lo,), inputs, in_specs, out_specs, shapes)


def local_kernel(
    coupling, kappa, flags, adj, before, after, src, mu, mu_before, mu_after, low, high, out
):
    fields, planes, rows, cells = adj.shape
    step = pl.program_id(0)
    first = step == 0
    last = step == pl.num_programs(0) - 1
    row = lax.broadcasted_iota(jnp.int32, (rows, cells), 0)
    col = lax.broadcasted_iota(jnp.int32, (rows, cells), 1)
    ring = 0.5 / (row.astype(jnp.float32) + 1.0)

    def pick(source, behind, ahead, f, k):
        if k < 0:
            return jnp.where(first, low[f, 0], behind)
        if k >= planes:
            return jnp.where(last, high[f, 0], ahead)
        return source

    def visc(k):
        return pick(mu[max(0, min(k, planes - 1))], mu_before[0], mu_after[0], fields, k)

    def cell(f, k):
        return pick(adj[f, max(0, min(k, planes - 1))], before[f, 0], after[f, 0], f, k)

    for k in range(planes):
        m = visc(k)
        up = ring * (m + visc(k + 1))
        down = ring * (m + visc(k - 1))
        outer = jnp.where(row < rows - 1, 0.5 * (m + pltpu.roll(m, rows - 1, 0)), 0.0)
        inner = jnp.where(row > 0, 0.5 * (m + pltpu.roll(m, 1, 0)), 0.0)
        east = jnp.where(col < cells - 1, 0.5 * (m + pltpu.roll(m, cells - 1, 1)), 0.0)
        west = jnp.where(col > 0, 0.5 * (m + pltpu.roll(m, 1, 1)), 0.0)
        diag = up + down + outer + inner + east + west
        for f in range(fields):
            p = adj[f, k]
            opens = [(1 - flags[f, i]).astype(jnp.float32) for i in range(3)]
            wall = jnp.where(col == 0, opens[0], 0.0)
            wall = wall + jnp.where(col == cells - 1, opens[1], 0.0)
            wall = wall + jnp.where(row == rows - 1, opens[2], 0.0)
            flux = (diag + wall * m) * p
            flux = flux - up * cell(f, k + 1) - down * cell(f, k - 1)
            flux = flux - outer * pltpu.roll(p, rows - 1, 0) - inner * pltpu.roll(p, 1, 0)
            flux = flux - east * pltpu.roll(p, cells - 1, 1) - west * pltpu.roll(p, 1, 1)
            total = src[f, k] + kappa[f] * flux
            for g in range(fields):
                total = total + coupling[g, f] * adj[g, k]
            out[f, k] = total


def local_part(center, source, viscosity, kappa, coupling, flags, low, high, token):
    fields, block, rows, cells = center.shape
    planes = min(4, block)

    def whole(width, index):
        return pl.BlockSpec((fields, width, rows, cells), lambda i: (0, index(i), 0, 0))

    def plane(width, index):
        return pl.BlockSpec((width, rows, cells), lambda i: (index(i), 0, 0))

    behind = lambda i: jnp.maximum(i * planes - 1, 0)
    ahead = lambda i: jnp.minimum(i * planes + planes, block - 1)
    here = lambda i: i
    halo = pl.BlockSpec((fields + 1, 1, rows, cells), lambda i: (0, 0, 0, 0))
    return call(
        local_kernel,
        "local_part",
        token,
        (block // planes,),
        [coupling, kappa, flags, center, center, center, source, viscosity, viscosity, viscosity, low, high],
        [
            SMEM,
            SMEM,
            SMEM,
            whole(planes, here),
            whole(1, behind),
            whole(1, ahead),
            whole(planes, here),
            plane(planes, here),
            plane(1, behind),
            plane(1, ahead),
            halo,
            halo,
        ],
        whole(planes, here),
        shaped(*center.shape),
    )


def sums(scalars, local, others):
    total = local[0] + scalars.weight(scalars.first(), scalars.slot) * others[0][0]
    for part in others[1:]:
        total = total + part[0]
    return total


class Plan:
    def __init__(self, ints, reals, slots, shape, near, table, back):
        self.ints, self.reals, self.slots, self.near = ints, reals, slots, near
        self.shape, self.table, self.back = shape, table, back
        self.fields, self.block, self.rows, self.cells = shape
        self.pairs = near // 2
        self.owned = self.pairs // QUAD
        self.cycles = near // QUAD
        self.depth = table.shape[2]

    def scalars(self, ints, reals):
        return Scalars(ints, reals, self.slots, self.near)

    def side(self, first, index):
        return pl.BlockSpec((1, self.block, self.near, self.cells), lambda i: (first + i, 0, index, 0))

    def part(self):
        return pl.BlockSpec((1, self.cycles, self.block, self.cells), lambda i, *_: (i, 0, 0, 0))

    def parts(self, count, first=0):
        shape = (count, 1, self.cycles, self.block, self.cells)
        return pl.BlockSpec(shape, lambda i, *_: (first, i, 0, 0, 0))

    def quad_shapes(self, fields):
        one = (fields, self.cycles, self.block, self.cells)
        return [shaped(*one), shaped(2, *one), shaped(2, *one)]

    def mix(self, center, first, lo, hi, index, token):
        count = max(1, self.slots // 2 - 1)

        def kernel(ints, reals, own, got, *outs):
            scalars = self.scalars(ints, reals)
            for s in range(count):
                target = scalars.target(s + 1)
                outs[s][0] = (
                    scalars.weight(scalars.slot, target) * own[0]
                    + scalars.weight(scalars.first(), target) * got[0]
                )

        return call(
            kernel,
            "mix",
            token,
            (hi - lo,),
            [self.ints, self.reals, center, first],
            [SMEM, SMEM, self.side(lo, index), self.side(0, 0)],
            [self.side(0, 0)] * count,
            [shaped(hi - lo, self.block, self.near, self.cells)] * count,
        )

    def spread(self, local, others, lo, hi, token):
        def kernel(ints, reals, local, *refs):
            others, (mine, core, chip), (flat, stage) = refs[:-5], refs[-5:-2], refs[-2:]
            scalars = self.scalars(ints, reals)
            flat[...] = sums(scalars, local, others).reshape(flat.shape)
            for o in range(QUAD):
                for j in range(self.owned):
                    for a in range(2):
                        r = o * self.owned + j + a * self.pairs
                        stage[o, 2 * j + a] = flat[pl.ds(r, self.block, stride=self.near), :]
            mine[0] = stage[scalars.rank]
            core[0, 0] = stage[scalars.rank ^ 1]
            core[1, 0] = stage[scalars.rank ^ 3]
            chip[0, 0] = stage[scalars.rank ^ 2]

        return call(
            kernel,
            "spread",
            token,
            (hi - lo,),
            [self.ints, self.reals, local] + others,
            [SMEM, SMEM, self.side(lo, 0)] + [self.side(0, 0)] * len(others),
            [self.part(), self.parts(2), self.parts(1)],
            self.quad_shapes(hi - lo),
            [
                pltpu.VMEM((self.block * self.near, self.cells), jnp.float32),
                pltpu.VMEM((QUAD, self.cycles, self.block, self.cells), jnp.float32),
            ],
        )

    def join(self, held, new, token):
        def kernel(held, new, out):
            out[...] = new[...]

        return call(
            kernel,
            "join",
            token,
            (held.shape[1],),
            [held, new],
            [ANY, self.parts(1, 1)],
            self.parts(1, 1),
            shaped(*held.shape),
            alias={0: 0},
        )

    def own_rows(self, shape):
        return pl.BlockSpec(
            (1, self.owned) + shape, lambda i, ints: (ints[1] // QUAD, ints[1] % QUAD, 0, 0)
        )

    def table_call(self, kernel, name, fields, inputs, in_specs, out_specs, out_shape, scratch, token):
        extra = [] if token is None else [token]
        count = len(inputs)
        return pl.pallas_call(
            lambda *refs: kernel(*refs[: count + 1], *refs[count + 1 + len(extra) :]),
            grid_spec=pltpu.PrefetchScalarGridSpec(
                num_scalar_prefetch=1,
                grid=(fields,),
                in_specs=in_specs + [ANY] * len(extra),
                out_specs=out_specs,
                scratch_shapes=scratch,
            ),
            out_shape=out_shape,
            compiler_params=PARAMS,
            cost_estimate=COST,
            name=name,
        )(self.ints, *inputs, *extra)

    def block4(self, *shape):
        return pl.BlockSpec((1,) + shape, lambda i, ints: (i, 0, 0, 0))

    def coefficients(self, mine, core, chip, token):
        fields = mine.shape[0]

        def kernel(ints, reals, table, mine, core, chip, out, column):
            scalars = self.scalars(ints, reals)
            row = lax.broadcasted_iota(jnp.int32, (self.depth, self.cells), 0)
            for k, part in enumerate((mine[0], core[0, 0], chip[0, 0], chip[1, 0])):
                column[:, scalars.rank ^ k] = part
            for j in range(self.owned):
                modes = [
                    jnp.dot(
                        table[0, j],
                        column[2 * j + a].reshape(QUAD * self.block, self.cells),
                        precision=lax.Precision.HIGHEST,
                        preferred_element_type=jnp.float32,
                    )
                    for a in range(2)
                ]
                split = scalars.split(scalars.rank * self.owned + j)
                out[0, j] = jnp.where(row < split, modes[0], modes[1])

        return self.table_call(
            kernel,
            "coefficients",
            fields,
            [self.reals, self.table, mine, core, chip],
            [SMEM, self.own_rows(self.table.shape[2:]), self.part(), self.parts(1), self.parts(2)],
            self.block4(self.owned, self.depth, self.cells),
            shaped(fields, self.owned, self.depth, self.cells),
            [pltpu.VMEM((self.cycles, QUAD, self.block, self.cells), jnp.float32)],
            token,
        )

    def filtered(self, own, other, mine, core, chip, token):
        fields = mine.shape[0]

        def kernel(ints, reals, back, own, other, mine, core, chip, *refs):
            (mine_out, core_out, chip_out), waves = refs[:3], refs[3]
            scalars = self.scalars(ints, reals)
            row = lax.broadcasted_iota(jnp.int32, (self.depth, self.cells), 0)
            source = (mine.at[0], core.at[0, 0], chip.at[0, 0], chip.at[1, 0])
            result = (mine_out.at[0], core_out.at[0, 0], chip_out.at[0, 0], chip_out.at[1, 0])
            for j in range(self.owned):
                pair = scalars.rank * self.owned + j
                total = own[0, j] + other[0, j]
                keep = row < scalars.split(pair)
                for a in range(2):
                    waves[2 * j + a] = jnp.dot(
                        back[0, j],
                        jnp.where(keep if a == 0 else jnp.logical_not(keep), total, 0.0),
                        precision=lax.Precision.HIGHEST,
                        preferred_element_type=jnp.float32,
                    ).reshape(QUAD, self.block, self.cells)
                    r = pair + a * self.pairs
                    for k in range(QUAD):
                        result[k][2 * j + a] = (
                            scalars.base(r) * source[k][2 * j + a]
                            + scalars.scale(r) * waves[2 * j + a, scalars.rank ^ k]
                        )

        modes = self.block4(self.owned, self.depth, self.cells)
        return self.table_call(
            kernel,
            "filtered",
            fields,
            [self.reals, self.back, own, other, mine, core, chip],
            [SMEM, self.own_rows(self.back.shape[2:]), modes, modes]
            + [self.part(), self.parts(1), self.parts(2)],
            [self.part(), self.parts(1), self.parts(2)],
            self.quad_shapes(fields),
            [pltpu.VMEM((self.cycles, QUAD, self.block, self.cells), jnp.float32)],
            token,
        )

    def place_near(self, mine, core, chip, held, lo, hi, token):
        carried = [] if held is None else [held]

        def kernel(ints, reals, mine, core, chip, *refs):
            out, stage = refs[-2:]
            rank = self.scalars(ints, reals).rank
            for k, part in enumerate((mine[0], core[0, 0], chip[0, 0], core[1, 0])):
                stage[rank ^ k] = part
            for o in range(QUAD):
                for j in range(self.owned):
                    for a in range(2):
                        out[0, :, o * self.owned + j + a * self.pairs, :] = stage[o, 2 * j + a]

        return call(
            kernel,
            "place_near",
            token,
            (hi - lo,),
            [self.ints, self.reals, mine, core, chip] + carried,
            [SMEM, SMEM, self.part(), self.parts(2), self.parts(1)] + [ANY] * len(carried),
            self.side(lo, 0),
            shaped(*self.shape),
            [pltpu.VMEM((QUAD, self.cycles, self.block, self.cells), jnp.float32)],
            alias={5: 0} if carried else None,
        )

    def place_far(self, local, others, held, lo, hi, token):
        def kernel(ints, reals, local, *refs):
            others, out = refs[: len(refs) - 1 - len(carried)], refs[-1]
            out[0] = sums(self.scalars(ints, reals), local, others)

        carried = [] if held is None else [held]
        return call(
            kernel,
            "place_far",
            token,
            (hi - lo,),
            [self.ints, self.reals, local] + others + carried,
            [SMEM, SMEM, self.side(lo, 1)]
            + [self.side(0, 0)] * len(others)
            + [ANY] * len(carried),
            self.side(lo, 1),
            shaped(*self.shape),
            alias={3 + len(others): 0} if carried else None,
        )


def spans(sizes, total):
    ends = np.cumsum(sizes)
    return [(int(end - size), int(end)) for size, end in zip(sizes, ends)]


def body(adjoint, source, viscosity, kappa, coupling, bc_flags, inst_map):
    slots = lax.axis_size("inst")
    sectors = lax.axis_size("space")
    center = adjoint[0]
    fields, block, cycles, cells = center.shape
    near = cycles // 2
    points = block * sectors
    quads = sectors // QUAD

    def to_partner(x, pick):
        pairs = []
        for i in range(slots):
            for p in range(sectors):
                pairs.append((i * sectors + p, pick(i, p % 2) * sectors + p))
        return lax.ppermute(x, ("inst", "space"), pairs)

    def to_first(x):
        return to_partner(x, lambda i, core: first_partner(i, core, slots))

    def to_later(x, s):
        return to_partner(x, lambda i, core: later_partner(i, core, slots, s))

    def to_sector(x, k):
        return lax.ppermute(x, "space", [(i, i ^ k) for i in range(sectors)])

    def ring(x, step):
        return lax.ppermute(x, "space", [(i, (i + step) % sectors) for i in range(sectors)])

    table, split, base, scale = mode_layout(points, near)
    table = table.reshape(table.shape[0], table.shape[1], quads, QUAD * block).transpose(2, 0, 1, 3)
    here = jnp.stack([lax.axis_index("inst"), lax.axis_index("space")])
    ints = jnp.concatenate([here, inst_map, jnp.asarray(split)])
    reals = jnp.asarray(np.concatenate([spectral_values(slots), base, scale]).astype(np.float32))
    plan = Plan(
        ints,
        reals,
        slots,
        center.shape,
        near,
        jnp.asarray(np.ascontiguousarray(table)),
        jnp.asarray(np.ascontiguousarray(table.transpose(0, 1, 3, 2))),
    )

    groups = [(lo, hi, 0) for lo, hi in spans(NEAR_SIZES, fields)]
    groups += [(lo, hi, 1) for lo, hi in spans(FAR_SIZES, fields)]
    first, others, parts, own, done = {}, {}, {}, {}, {}
    token, local, held, halos = None, None, None, None
    for step, g in ORDER:
        lo, hi, index = groups[g]
        if step == "pack":
            packed = pack(center, viscosity, lo, hi, index, near, halos is None, token)
            token = packed[0]
            first[g] = to_first(packed[0])
            if halos is None:
                halos = ring(packed[1], 1), ring(packed[2], -1)
        elif step == "local":
            local = token = local_part(
                center, source[0], viscosity, kappa, coupling, bc_flags, *halos, token
            )
        elif step == "mix":
            mixed = plan.mix(center, first[g], lo, hi, index, token)
            token = mixed[0]
            others[g] = [first[g]] + [to_later(x, s + 1) for s, x in enumerate(mixed)]
        elif step == "spread":
            mine, core, chip = plan.spread(local, others[g], lo, hi, token)
            token = mine
            parts[g] = mine, to_sector(core, 1), chip
        elif step == "join":
            mine, core, chip = parts[g]
            token = plan.join(chip, core, token)
            parts[g] = mine, core, to_sector(token, 2)
        elif step == "coef":
            part = token = plan.coefficients(*parts[g], token)
            stride = QUAD
            while 2 * stride < sectors:
                part = part + to_sector(part, stride)
                stride = 2 * stride
            other = to_sector(part, stride) if stride < sectors else jnp.zeros_like(part)
            own[g] = part, other
        elif step == "filter":
            mine, core, chip = plan.filtered(*own[g], *parts[g], token)
            token = mine
            done[g] = mine, core, to_sector(chip, 2)
        elif step == "back":
            mine, core, chip = done[g]
            token = plan.join(core, chip, token)
            done[g] = mine, to_sector(token, 1), chip
        elif step == "near":
            held = token = plan.place_near(*done[g], held, lo, hi, None if token is held else token)
        else:
            held = token = plan.place_far(
                local, others[g], held, lo, hi, None if token is held else token
            )
    return held[None]


def solution(mesh):
    return jax.shard_map(
        body,
        mesh=mesh,
        in_specs=(
            P("inst", None, "space", None, None),
            P("inst", None, "space", None, None),
            P("space", None, None),
            P(),
            P(),
            P(),
            P(),
        ),
        out_specs=P("inst", None, "space", None, None),
        check_vma=False,
    )
```

```python
import functools

import jax
import jax.numpy as jnp
import numpy as np
from jax import lax
from jax.experimental import pallas as pl
from jax.experimental.pallas import tpu as pltpu
from jax.sharding import PartitionSpec as P

CORES = 2
NEAR_SIZES = (2, 2, 1)
FAR_SIZES = (3, 2)
ORDER = (
    ("pack", 0),
    ("pack", 1),
    ("local", 0),
    ("mix", 0),
    ("mix", 1),
    ("spread", 0),
    ("pack", 2),
    ("coef", 0),
    ("pack", 3),
    ("mix", 2),
    ("spread", 1),
    ("coef", 1),
    ("mix", 3),
    ("spread", 2),
    ("pack", 4),
    ("coef", 2),
    ("mix", 4),
    ("filter", 0),
    ("near", 0),
    ("filter", 1),
    ("far", 3),
    ("near", 1),
    ("filter", 2),
    ("far", 4),
    ("near", 2),
)
SMEM = pl.BlockSpec(memory_space=pltpu.SMEM)
ANY = pl.BlockSpec(memory_space=pl.ANY)
COST = pl.CostEstimate(flops=0, bytes_accessed=0, transcendentals=0)
PARAMS = pltpu.CompilerParams(vmem_limit_bytes=48 * 1024 * 1024)


def spectral_values(slots):
    offset = np.arange(1 - slots, slots)
    safe = np.where(offset == 0, 1.0, np.sin(np.pi * offset / slots))
    return np.where(offset == 0, 0.0, 0.5 * (1.0 - 2.0 * (np.abs(offset) % 2)) / safe)


def mode_layout(points, near):
    half = points // 2
    pairs = near // 2
    theta = np.arange(points)
    bases, base, scale = [], np.zeros(near), np.zeros(near)
    for r in range(near):
        cutoff = max(4, points * (r + 1) // (2 * near))
        weight = max(1.0 - r / near, 0.0)
        kept = [m for m in range(half + 1) if m < cutoff]
        out = [m for m in range(half + 1) if m >= cutoff]
        count = [sum(1 if m in (0, half) else 2 for m in modes) for modes in (kept, out)]
        low = count[0] <= count[1]
        rows = []
        for m in kept if low else out:
            angle = 2.0 * np.pi * (m * theta % points) / points
            if m in (0, half):
                rows.append(np.cos(angle) / np.sqrt(points))
            else:
                rows.append(np.cos(angle) * np.sqrt(2.0 / points))
                rows.append(np.sin(angle) * np.sqrt(2.0 / points))
        bases.append(rows)
        base[r] = 1.0 - weight if low else 1.0
        scale[r] = weight if low else -weight
    depth = max(len(bases[p]) + len(bases[p + pairs]) for p in range(pairs))
    depth = -(-depth // 8) * 8
    table = np.zeros((pairs, depth, points), np.float32)
    split = np.zeros(pairs, np.int32)
    for p in range(pairs):
        rows = bases[p] + bases[p + pairs]
        table[p, : len(rows)] = np.stack(rows)
        split[p] = len(bases[p])
    return table, split, base, scale


class Scalars:
    def __init__(self, ints, reals, slots, near):
        self.ints, self.reals, self.slots, self.near = ints, reals, slots, near
        self.slot, self.place = ints[0], ints[1]
        self.rank = self.place % CORES

    def weight(self, i, j):
        return self.reals[self.ints[2 + i] - self.ints[2 + j] + self.slots - 1]

    def split(self, pair):
        return self.ints[2 + self.slots + pair]

    def base(self, r):
        return self.reals[2 * self.slots - 1 + r]

    def scale(self, r):
        return self.reals[2 * self.slots - 1 + self.near + r]

    def first(self):
        return first_partner(self.slot, self.place % 2, self.slots)

    def target(self, s):
        return later_partner(self.slot, self.place % 2, self.slots, s)


def first_partner(slot, core, slots):
    if slots == 4:
        return slot ^ (2 - core)
    return slot ^ 1


def later_partner(slot, core, slots, s):
    if slots == 4:
        return slot ^ (1 + core)
    return (slot // 2 + s) % (slots // 2) * 2 + slot % 2


def call(kernel, name, token, grid, inputs, in_specs, out_specs, out_shape, scratch=(), alias=None):
    extra = [] if token is None else [token]
    return pl.pallas_call(
        lambda *refs: kernel(*refs[: len(inputs)], *refs[len(inputs) + len(extra) :]),
        grid=grid,
        in_specs=list(in_specs) + [ANY] * len(extra),
        out_specs=out_specs,
        out_shape=out_shape,
        scratch_shapes=list(scratch),
        input_output_aliases=alias or {},
        compiler_params=PARAMS,
        cost_estimate=COST,
        name=name,
    )(*inputs, *extra)


def shaped(*shape):
    return jax.ShapeDtypeStruct(shape, jnp.float32)


def pack(center, viscosity, lo, hi, index, near, edges, token):
    fields, block, rows, cells = center.shape
    inputs, in_specs = [center], [pl.BlockSpec((1, block, near, cells), lambda i: (lo + i, 0, index, 0))]
    shapes = [shaped(hi - lo, block, near, cells)]
    out_specs = [pl.BlockSpec((1, block, near, cells), lambda i: (i, 0, 0, 0))]
    if edges:
        for start in (block - 1, 0):
            inputs += [center, viscosity]
            in_specs.append(pl.BlockSpec((fields, 1, rows, cells), lambda i, s=start: (0, s, 0, 0)))
            in_specs.append(pl.BlockSpec((1, rows, cells), lambda i, s=start: (s, 0, 0)))
            shapes.append(shaped(fields + 1, 1, rows, cells))
            out_specs.append(pl.BlockSpec((fields + 1, 1, rows, cells), lambda i: (0, 0, 0, 0)))

    def kernel(source, *refs):
        out, rest = refs[len(inputs) - 1], refs[len(inputs) :]
        out[...] = source[...]
        for e, edge in enumerate(rest):
            edge[:fields] = refs[2 * e][...]
            edge[fields] = refs[2 * e + 1][...]

    return call(kernel, "pack", token, (hi - lo,), inputs, in_specs, out_specs, shapes)


def local_kernel(
    coupling, kappa, flags, adj, before, after, src, mu, mu_before, mu_after, low, high, out
):
    fields, planes, rows, cells = adj.shape
    step = pl.program_id(0)
    first = step == 0
    last = step == pl.num_programs(0) - 1
    row = lax.broadcasted_iota(jnp.int32, (rows, cells), 0)
    col = lax.broadcasted_iota(jnp.int32, (rows, cells), 1)
    ring = 0.5 / (row.astype(jnp.float32) + 1.0)

    def pick(source, behind, ahead, f, k):
        if k < 0:
            return jnp.where(first, low[f, 0], behind)
        if k >= planes:
            return jnp.where(last, high[f, 0], ahead)
        return source

    def visc(k):
        return pick(mu[max(0, min(k, planes - 1))], mu_before[0], mu_after[0], fields, k)

    def cell(f, k):
        return pick(adj[f, max(0, min(k, planes - 1))], before[f, 0], after[f, 0], f, k)

    for k in range(planes):
        m = visc(k)
        up = ring * (m + visc(k + 1))
        down = ring * (m + visc(k - 1))
        outer = jnp.where(row < rows - 1, 0.5 * (m + pltpu.roll(m, rows - 1, 0)), 0.0)
        inner = jnp.where(row > 0, 0.5 * (m + pltpu.roll(m, 1, 0)), 0.0)
        east = jnp.where(col < cells - 1, 0.5 * (m + pltpu.roll(m, cells - 1, 1)), 0.0)
        west = jnp.where(col > 0, 0.5 * (m + pltpu.roll(m, 1, 1)), 0.0)
        diag = up + down + outer + inner + east + west
        for f in range(fields):
            p = adj[f, k]
            opens = [(1 - flags[f, i]).astype(jnp.float32) for i in range(3)]
            wall = jnp.where(col == 0, opens[0], 0.0)
            wall = wall + jnp.where(col == cells - 1, opens[1], 0.0)
            wall = wall + jnp.where(row == rows - 1, opens[2], 0.0)
            flux = (diag + wall * m) * p
            flux = flux - up * cell(f, k + 1) - down * cell(f, k - 1)
            flux = flux - outer * pltpu.roll(p, rows - 1, 0) - inner * pltpu.roll(p, 1, 0)
            flux = flux - east * pltpu.roll(p, cells - 1, 1) - west * pltpu.roll(p, 1, 1)
            total = src[f, k] + kappa[f] * flux
            for g in range(fields):
                total = total + coupling[g, f] * adj[g, k]
            out[f, k] = total


def local_part(center, source, viscosity, kappa, coupling, flags, low, high, token):
    fields, block, rows, cells = center.shape
    planes = min(4, block)

    def whole(width, index):
        return pl.BlockSpec((fields, width, rows, cells), lambda i: (0, index(i), 0, 0))

    def plane(width, index):
        return pl.BlockSpec((width, rows, cells), lambda i: (index(i), 0, 0))

    behind = lambda i: jnp.maximum(i * planes - 1, 0)
    ahead = lambda i: jnp.minimum(i * planes + planes, block - 1)
    here = lambda i: i
    halo = pl.BlockSpec((fields + 1, 1, rows, cells), lambda i: (0, 0, 0, 0))
    return call(
        local_kernel,
        "local_part",
        token,
        (block // planes,),
        [coupling, kappa, flags, center, center, center, source, viscosity, viscosity, viscosity, low, high],
        [
            SMEM,
            SMEM,
            SMEM,
            whole(planes, here),
            whole(1, behind),
            whole(1, ahead),
            whole(planes, here),
            plane(planes, here),
            plane(1, behind),
            plane(1, ahead),
            halo,
            halo,
        ],
        whole(planes, here),
        shaped(*center.shape),
    )


def sums(scalars, local, others):
    total = local[0] + scalars.weight(scalars.first(), scalars.slot) * others[0][0]
    for part in others[1:]:
        total = total + part[0]
    return total


class Plan:
    def __init__(self, ints, reals, slots, shape, near, table, back):
        self.ints, self.reals, self.slots, self.near = ints, reals, slots, near
        self.shape, self.table, self.back = shape, table, back
        self.fields, self.block, self.rows, self.cells = shape
        self.pairs = near // 2
        self.owned = self.pairs // CORES
        self.cycles = near // CORES
        self.depth = table.shape[2]

    def scalars(self, ints, reals):
        return Scalars(ints, reals, self.slots, self.near)

    def side(self, first, index):
        return pl.BlockSpec((1, self.block, self.near, self.cells), lambda i: (first + i, 0, index, 0))

    def part(self):
        return pl.BlockSpec((1, self.cycles, self.block, self.cells), lambda i, *_: (i, 0, 0, 0))

    def mix(self, center, first, lo, hi, index, token):
        count = max(1, self.slots // 2 - 1)

        def kernel(ints, reals, own, got, *outs):
            scalars = self.scalars(ints, reals)
            for s in range(count):
                target = scalars.target(s + 1)
                outs[s][0] = (
                    scalars.weight(scalars.slot, target) * own[0]
                    + scalars.weight(scalars.first(), target) * got[0]
                )

        return call(
            kernel,
            "mix",
            token,
            (hi - lo,),
            [self.ints, self.reals, center, first],
            [SMEM, SMEM, self.side(lo, index), self.side(0, 0)],
            [self.side(0, 0)] * count,
            [shaped(hi - lo, self.block, self.near, self.cells)] * count,
        )

    def spread(self, local, others, lo, hi, token):
        def kernel(ints, reals, local, *refs):
            others, (mine, core, flat, stage) = refs[:-4], refs[-4:]
            scalars = self.scalars(ints, reals)
            flat[...] = sums(scalars, local, others).reshape(flat.shape)
            for o in range(CORES):
                for j in range(self.owned):
                    for a in range(2):
                        r = o * self.owned + j + a * self.pairs
                        stage[o, 2 * j + a] = flat[pl.ds(r, self.block, stride=self.near), :]
            mine[0] = stage[scalars.rank]
            core[0] = stage[1 - scalars.rank]

        return call(
            kernel,
            "spread",
            token,
            (hi - lo,),
            [self.ints, self.reals, local] + others,
            [SMEM, SMEM, self.side(lo, 0)] + [self.side(0, 0)] * len(others),
            [self.part()] * 2,
            [shaped(hi - lo, self.cycles, self.block, self.cells)] * 2,
            [
                pltpu.VMEM((self.block * self.near, self.cells), jnp.float32),
                pltpu.VMEM((CORES, self.cycles, self.block, self.cells), jnp.float32),
            ],
        )

    def own_rows(self, shape):
        return pl.BlockSpec(
            (1, self.owned) + shape, lambda i, ints: (ints[1] // CORES, ints[1] % CORES, 0, 0)
        )

    def table_call(self, kernel, name, fields, inputs, in_specs, out_specs, out_shape, scratch, token):
        extra = [] if token is None else [token]
        count = len(inputs)
        return pl.pallas_call(
            lambda *refs: kernel(*refs[: count + 1], *refs[count + 1 + len(extra) :]),
            grid_spec=pltpu.PrefetchScalarGridSpec(
                num_scalar_prefetch=1,
                grid=(fields,),
                in_specs=in_specs + [ANY] * len(extra),
                out_specs=out_specs,
                scratch_shapes=scratch,
            ),
            out_shape=out_shape,
            compiler_params=PARAMS,
            cost_estimate=COST,
            name=name,
        )(self.ints, *inputs, *extra)

    def block4(self, *shape):
        return pl.BlockSpec((1,) + shape, lambda i, ints: (i, 0, 0, 0))

    def coefficients(self, mine, core, token):
        fields = mine.shape[0]

        def kernel(ints, reals, table, mine, core, out, column):
            scalars = self.scalars(ints, reals)
            row = lax.broadcasted_iota(jnp.int32, (self.depth, self.cells), 0)
            column[:, scalars.rank] = mine[0]
            column[:, 1 - scalars.rank] = core[0]
            for j in range(self.owned):
                modes = [
                    jnp.dot(
                        table[0, j],
                        column[2 * j + a].reshape(CORES * self.block, self.cells),
                        precision=lax.Precision.HIGHEST,
                        preferred_element_type=jnp.float32,
                    )
                    for a in range(2)
                ]
                split = scalars.split(scalars.rank * self.owned + j)
                out[0, j] = jnp.where(row < split, modes[0], modes[1])

        return self.table_call(
            kernel,
            "coefficients",
            fields,
            [self.reals, self.table, mine, core],
            [SMEM, self.own_rows(self.table.shape[2:]), self.part(), self.part()],
            self.block4(self.owned, self.depth, self.cells),
            shaped(fields, self.owned, self.depth, self.cells),
            [pltpu.VMEM((self.cycles, CORES, self.block, self.cells), jnp.float32)],
            token,
        )

    def filtered(self, total, mine, core, token):
        fields = mine.shape[0]

        def kernel(ints, reals, back, total, mine, core, mine_out, core_out, waves):
            scalars = self.scalars(ints, reals)
            row = lax.broadcasted_iota(jnp.int32, (self.depth, self.cells), 0)
            for j in range(self.owned):
                pair = scalars.rank * self.owned + j
                keep = row < scalars.split(pair)
                for a in range(2):
                    c = 2 * j + a
                    waves[c] = jnp.dot(
                        back[0, j],
                        jnp.where(keep if a == 0 else jnp.logical_not(keep), total[0, j], 0.0),
                        precision=lax.Precision.HIGHEST,
                        preferred_element_type=jnp.float32,
                    ).reshape(CORES, self.block, self.cells)
                    base = scalars.base(pair + a * self.pairs)
                    scale = scalars.scale(pair + a * self.pairs)
                    mine_out[0, c] = base * mine[0, c] + scale * waves[c, scalars.rank]
                    core_out[0, c] = base * core[0, c] + scale * waves[c, 1 - scalars.rank]

        return self.table_call(
            kernel,
            "filtered",
            fields,
            [self.reals, self.back, total, mine, core],
            [SMEM, self.own_rows(self.back.shape[2:])]
            + [self.block4(self.owned, self.depth, self.cells), self.part(), self.part()],
            [self.part()] * 2,
            [shaped(*mine.shape)] * 2,
            [pltpu.VMEM((self.cycles, CORES, self.block, self.cells), jnp.float32)],
            token,
        )

    def place_near(self, mine, core, held, lo, hi, token):
        carried = [] if held is None else [held]

        def kernel(ints, reals, mine, core, *refs):
            out, stage = refs[-2:]
            rank = self.scalars(ints, reals).rank
            stage[rank] = mine[0]
            stage[1 - rank] = core[0]
            for o in range(CORES):
                for j in range(self.owned):
                    for a in range(2):
                        out[0, :, o * self.owned + j + a * self.pairs, :] = stage[o, 2 * j + a]

        return call(
            kernel,
            "place_near",
            token,
            (hi - lo,),
            [self.ints, self.reals, mine, core] + carried,
            [SMEM, SMEM, self.part(), self.part()] + [ANY] * len(carried),
            self.side(lo, 0),
            shaped(*self.shape),
            [pltpu.VMEM((CORES, self.cycles, self.block, self.cells), jnp.float32)],
            alias={4: 0} if carried else None,
        )

    def place_far(self, local, others, held, lo, hi, token):
        def kernel(ints, reals, local, *refs):
            others, out = refs[: len(refs) - 1 - len(carried)], refs[-1]
            out[0] = sums(self.scalars(ints, reals), local, others)

        carried = [] if held is None else [held]
        return call(
            kernel,
            "place_far",
            token,
            (hi - lo,),
            [self.ints, self.reals, local] + others + carried,
            [SMEM, SMEM, self.side(lo, 1)]
            + [self.side(0, 0)] * len(others)
            + [ANY] * len(carried),
            self.side(lo, 1),
            shaped(*self.shape),
            alias={3 + len(others): 0} if carried else None,
        )


def spans(sizes, total):
    ends = np.cumsum(sizes)
    return [(int(end - size), int(end)) for size, end in zip(sizes, ends)]


def body(adjoint, source, viscosity, kappa, coupling, bc_flags, inst_map):
    slots = lax.axis_size("inst")
    sectors = lax.axis_size("space")
    center = adjoint[0]
    fields, block, cycles, cells = center.shape
    near = cycles // 2
    points = block * sectors
    chips = sectors // CORES
    lines = [[c * CORES + i for c in range(chips)] for i in range(CORES)]

    def to_partner(x, pick):
        pairs = []
        for i in range(slots):
            for p in range(sectors):
                pairs.append((i * sectors + p, pick(i, p % 2) * sectors + p))
        return lax.ppermute(x, ("inst", "space"), pairs)

    def to_first(x):
        return to_partner(x, lambda i, core: first_partner(i, core, slots))

    def to_later(x, s):
        return to_partner(x, lambda i, core: later_partner(i, core, slots, s))

    def to_core(x):
        return lax.ppermute(x, "space", [(i, i ^ 1) for i in range(sectors)])

    def ring(x, step):
        return lax.ppermute(x, "space", [(i, (i + step) % sectors) for i in range(sectors)])

    def line_order(g):
        flipped = lines[::-1] if g % 2 else lines
        return [line[::-1] for line in flipped] if g // 2 % 2 else flipped

    table, split, base, scale = mode_layout(points, near)
    table = table.reshape(table.shape[0], table.shape[1], chips, CORES * block).transpose(2, 0, 1, 3)
    here = jnp.stack([lax.axis_index("inst"), lax.axis_index("space")])
    ints = jnp.concatenate([here, inst_map, jnp.asarray(split)])
    reals = jnp.asarray(np.concatenate([spectral_values(slots), base, scale]).astype(np.float32))
    plan = Plan(
        ints,
        reals,
        slots,
        center.shape,
        near,
        jnp.asarray(np.ascontiguousarray(table)),
        jnp.asarray(np.ascontiguousarray(table.transpose(0, 1, 3, 2))),
    )

    groups = [(lo, hi, 0) for lo, hi in spans(NEAR_SIZES, fields)]
    groups += [(lo, hi, 1) for lo, hi in spans(FAR_SIZES, fields)]
    first, others, parts, totals, done = {}, {}, {}, {}, {}
    token, local, held, halos = None, None, None, None
    for step, g in ORDER:
        lo, hi, index = groups[g]
        if step == "pack":
            packed = pack(center, viscosity, lo, hi, index, near, halos is None, token)
            token = packed[0]
            first[g] = to_first(packed[0])
            if halos is None:
                halos = ring(packed[1], 1), ring(packed[2], -1)
        elif step == "local":
            local = token = local_part(
                center, source[0], viscosity, kappa, coupling, bc_flags, *halos, token
            )
        elif step == "mix":
            mixed = plan.mix(center, first[g], lo, hi, index, token)
            token = mixed[0]
            others[g] = [first[g]] + [to_later(x, s + 1) for s, x in enumerate(mixed)]
        elif step == "spread":
            mine, core = plan.spread(local, others[g], lo, hi, token)
            token = mine
            parts[g] = mine, to_core(core)
        elif step == "coef":
            token = plan.coefficients(*parts[g], token)
            totals[g] = lax.psum(token, "space", axis_index_groups=line_order(g))
        elif step == "filter":
            mine, core = plan.filtered(totals[g], *parts[g], token)
            token = mine
            done[g] = mine, to_core(core)
        elif step == "near":
            held = token = plan.place_near(*done[g], held, lo, hi, None if token is held else token)
        else:
            held = token = plan.place_far(
                local, others[g], held, lo, hi, None if token is held else token
            )
    return held[None]


def solution(mesh):
    return jax.shard_map(
        body,
        mesh=mesh,
        in_specs=(
            P("inst", None, "space", None, None),
            P("inst", None, "space", None, None),
            P("space", None, None),
            P(),
            P(),
            P(),
            P(),
        ),
        out_specs=P("inst", None, "space", None, None),
        check_vma=False,
    )
```

```python
import functools

import jax
import jax.numpy as jnp
import numpy as np
from jax import lax
from jax.experimental import pallas as pl
from jax.experimental.pallas import tpu as pltpu
from jax.sharding import PartitionSpec as P

QUAD = 4
NEAR_SIZES = (2, 2, 1)
FAR_SIZES = (3, 2)
ORDER = (
    ("pack", 0),
    ("pack", 1),
    ("local", 0),
    ("mix", 0),
    ("mix", 1),
    ("spread", 0),
    ("pack", 2),
    ("join", 0),
    ("spread", 1),
    ("pack", 3),
    ("coef", 0),
    ("join", 1),
    ("mix", 2),
    ("spread", 2),
    ("pack", 4),
    ("filter", 0),
    ("coef", 1),
    ("join", 2),
    ("mix", 3),
    ("back", 0),
    ("coef", 2),
    ("near", 0),
    ("filter", 1),
    ("mix", 4),
    ("back", 1),
    ("near", 1),
    ("filter", 2),
    ("far", 3),
    ("back", 2),
    ("near", 2),
    ("far", 4),
)
DEPTH = 99
CROSS = 99
FREE = ("join", "back", "near")
SMEM = pl.BlockSpec(memory_space=pltpu.SMEM)
ANY = pl.BlockSpec(memory_space=pl.ANY)
COST = pl.CostEstimate(flops=0, bytes_accessed=0, transcendentals=0)
PARAMS = pltpu.CompilerParams(vmem_limit_bytes=48 * 1024 * 1024)


def spectral_values(slots):
    offset = np.arange(1 - slots, slots)
    safe = np.where(offset == 0, 1.0, np.sin(np.pi * offset / slots))
    return np.where(offset == 0, 0.0, 0.5 * (1.0 - 2.0 * (np.abs(offset) % 2)) / safe)


def mode_layout(points, near):
    half = points // 2
    pairs = near // 2
    theta = np.arange(points)
    bases, base, scale = [], np.zeros(near), np.zeros(near)
    for r in range(near):
        cutoff = max(4, points * (r + 1) // (2 * near))
        weight = max(1.0 - r / near, 0.0)
        kept = [m for m in range(half + 1) if m < cutoff]
        out = [m for m in range(half + 1) if m >= cutoff]
        count = [sum(1 if m in (0, half) else 2 for m in modes) for modes in (kept, out)]
        low = count[0] <= count[1]
        rows = []
        for m in kept if low else out:
            angle = 2.0 * np.pi * (m * theta % points) / points
            if m in (0, half):
                rows.append(np.cos(angle) / np.sqrt(points))
            else:
                rows.append(np.cos(angle) * np.sqrt(2.0 / points))
                rows.append(np.sin(angle) * np.sqrt(2.0 / points))
        bases.append(rows)
        base[r] = 1.0 - weight if low else 1.0
        scale[r] = weight if low else -weight
    depth = max(len(bases[p]) + len(bases[p + pairs]) for p in range(pairs))
    depth = -(-depth // 8) * 8
    table = np.zeros((pairs, depth, points), np.float32)
    split = np.zeros(pairs, np.int32)
    for p in range(pairs):
        rows = bases[p] + bases[p + pairs]
        table[p, : len(rows)] = np.stack(rows)
        split[p] = len(bases[p])
    return table, split, base, scale


class Scalars:
    def __init__(self, ints, reals, slots, near):
        self.ints, self.reals, self.slots, self.near = ints, reals, slots, near
        self.slot, self.place = ints[0], ints[1]
        self.rank = self.place % QUAD

    def weight(self, i, j):
        return self.reals[self.ints[2 + i] - self.ints[2 + j] + self.slots - 1]

    def split(self, pair):
        return self.ints[2 + self.slots + pair]

    def base(self, r):
        return self.reals[2 * self.slots - 1 + r]

    def scale(self, r):
        return self.reals[2 * self.slots - 1 + self.near + r]

    def first(self):
        return first_partner(self.slot, self.place % 2, self.slots)

    def target(self, s):
        return later_partner(self.slot, self.place % 2, self.slots, s)


def first_partner(slot, core, slots):
    if slots == 4:
        return slot ^ (2 - core)
    return slot ^ 1


def later_partner(slot, core, slots, s):
    if slots == 4:
        return slot ^ (1 + core)
    return (slot // 2 + s) % (slots // 2) * 2 + slot % 2


def call(kernel, name, token, grid, inputs, in_specs, out_specs, out_shape, scratch=(), alias=None):
    extra = [t for t in token or () if all(t is not x for x in inputs)]
    return pl.pallas_call(
        lambda *refs: kernel(*refs[: len(inputs)], *refs[len(inputs) + len(extra) :]),
        grid=grid,
        in_specs=list(in_specs) + [ANY] * len(extra),
        out_specs=out_specs,
        out_shape=out_shape,
        scratch_shapes=list(scratch),
        input_output_aliases=alias or {},
        compiler_params=PARAMS,
        cost_estimate=COST,
        name=name,
    )(*inputs, *extra)


def shaped(*shape):
    return jax.ShapeDtypeStruct(shape, jnp.float32)


def pack(center, viscosity, lo, hi, index, near, edges, token):
    fields, block, rows, cells = center.shape
    inputs, in_specs = [center], [pl.BlockSpec((1, block, near, cells), lambda i: (lo + i, 0, index, 0))]
    shapes = [shaped(hi - lo, block, near, cells)]
    out_specs = [pl.BlockSpec((1, block, near, cells), lambda i: (i, 0, 0, 0))]
    if edges:
        for start in (block - 1, 0):
            inputs += [center, viscosity]
            in_specs.append(pl.BlockSpec((fields, 1, rows, cells), lambda i, s=start: (0, s, 0, 0)))
            in_specs.append(pl.BlockSpec((1, rows, cells), lambda i, s=start: (s, 0, 0)))
            shapes.append(shaped(fields + 1, 1, rows, cells))
            out_specs.append(pl.BlockSpec((fields + 1, 1, rows, cells), lambda i: (0, 0, 0, 0)))

    def kernel(source, *refs):
        out, rest = refs[len(inputs) - 1], refs[len(inputs) :]
        out[...] = source[...]
        for e, edge in enumerate(rest):
            edge[:fields] = refs[2 * e][...]
            edge[fields] = refs[2 * e + 1][...]

    return call(kernel, "pack", token, (hi - lo,), inputs, in_specs, out_specs, shapes)


def local_kernel(
    coupling, kappa, flags, adj, before, after, src, mu, mu_before, mu_after, low, high, out
):
    fields, planes, rows, cells = adj.shape
    step = pl.program_id(0)
    first = step == 0
    last = step == pl.num_programs(0) - 1
    row = lax.broadcasted_iota(jnp.int32, (rows, cells), 0)
    col = lax.broadcasted_iota(jnp.int32, (rows, cells), 1)
    ring = 0.5 / (row.astype(jnp.float32) + 1.0)

    def pick(source, behind, ahead, f, k):
        if k < 0:
            return jnp.where(first, low[f, 0], behind)
        if k >= planes:
            return jnp.where(last, high[f, 0], ahead)
        return source

    def visc(k):
        return pick(mu[max(0, min(k, planes - 1))], mu_before[0], mu_after[0], fields, k)

    def cell(f, k):
        return pick(adj[f, max(0, min(k, planes - 1))], before[f, 0], after[f, 0], f, k)

    for k in range(planes):
        m = visc(k)
        up = ring * (m + visc(k + 1))
        down = ring * (m + visc(k - 1))
        outer = jnp.where(row < rows - 1, 0.5 * (m + pltpu.roll(m, rows - 1, 0)), 0.0)
        inner = jnp.where(row > 0, 0.5 * (m + pltpu.roll(m, 1, 0)), 0.0)
        east = jnp.where(col < cells - 1, 0.5 * (m + pltpu.roll(m, cells - 1, 1)), 0.0)
        west = jnp.where(col > 0, 0.5 * (m + pltpu.roll(m, 1, 1)), 0.0)
        diag = up + down + outer + inner + east + west
        for f in range(fields):
            p = adj[f, k]
            opens = [(1 - flags[f, i]).astype(jnp.float32) for i in range(3)]
            wall = jnp.where(col == 0, opens[0], 0.0)
            wall = wall + jnp.where(col == cells - 1, opens[1], 0.0)
            wall = wall + jnp.where(row == rows - 1, opens[2], 0.0)
            flux = (diag + wall * m) * p
            flux = flux - up * cell(f, k + 1) - down * cell(f, k - 1)
            flux = flux - outer * pltpu.roll(p, rows - 1, 0) - inner * pltpu.roll(p, 1, 0)
            flux = flux - east * pltpu.roll(p, cells - 1, 1) - west * pltpu.roll(p, 1, 1)
            total = src[f, k] + kappa[f] * flux
            for g in range(fields):
                total = total + coupling[g, f] * adj[g, k]
            out[f, k] = total


def local_part(center, source, viscosity, kappa, coupling, flags, low, high, token):
    fields, block, rows, cells = center.shape
    planes = min(4, block)

    def whole(width, index):
        return pl.BlockSpec((fields, width, rows, cells), lambda i: (0, index(i), 0, 0))

    def plane(width, index):
        return pl.BlockSpec((width, rows, cells), lambda i: (index(i), 0, 0))

    behind = lambda i: jnp.maximum(i * planes - 1, 0)
    ahead = lambda i: jnp.minimum(i * planes + planes, block - 1)
    here = lambda i: i
    halo = pl.BlockSpec((fields + 1, 1, rows, cells), lambda i: (0, 0, 0, 0))
    return call(
        local_kernel,
        "local_part",
        token,
        (block // planes,),
        [coupling, kappa, flags, center, center, center, source, viscosity, viscosity, viscosity, low, high],
        [
            SMEM,
            SMEM,
            SMEM,
            whole(planes, here),
            whole(1, behind),
            whole(1, ahead),
            whole(planes, here),
            plane(planes, here),
            plane(1, behind),
            plane(1, ahead),
            halo,
            halo,
        ],
        whole(planes, here),
        shaped(*center.shape),
    )


def sums(scalars, local, others):
    total = local[0] + scalars.weight(scalars.first(), scalars.slot) * others[0][0]
    for part in others[1:]:
        total = total + part[0]
    return total


class Plan:
    def __init__(self, ints, reals, slots, shape, near, table, back):
        self.ints, self.reals, self.slots, self.near = ints, reals, slots, near
        self.shape, self.table, self.back = shape, table, back
        self.fields, self.block, self.rows, self.cells = shape
        self.pairs = near // 2
        self.owned = self.pairs // QUAD
        self.cycles = near // QUAD
        self.depth = table.shape[2]

    def scalars(self, ints, reals):
        return Scalars(ints, reals, self.slots, self.near)

    def side(self, first, index):
        return pl.BlockSpec((1, self.block, self.near, self.cells), lambda i: (first + i, 0, index, 0))

    def part(self):
        return pl.BlockSpec((1, self.cycles, self.block, self.cells), lambda i, *_: (i, 0, 0, 0))

    def parts(self, count, first=0):
        shape = (count, 1, self.cycles, self.block, self.cells)
        return pl.BlockSpec(shape, lambda i, *_: (first, i, 0, 0, 0))

    def quad_shapes(self, fields):
        one = (fields, self.cycles, self.block, self.cells)
        return [shaped(*one), shaped(2, *one), shaped(2, *one)]

    def mix(self, center, first, lo, hi, index, token):
        count = max(1, self.slots // 2 - 1)

        def kernel(ints, reals, own, got, *outs):
            scalars = self.scalars(ints, reals)
            for s in range(count):
                target = scalars.target(s + 1)
                outs[s][0] = (
                    scalars.weight(scalars.slot, target) * own[0]
                    + scalars.weight(scalars.first(), target) * got[0]
                )

        return call(
            kernel,
            "mix",
            token,
            (hi - lo,),
            [self.ints, self.reals, center, first],
            [SMEM, SMEM, self.side(lo, index), self.side(0, 0)],
            [self.side(0, 0)] * count,
            [shaped(hi - lo, self.block, self.near, self.cells)] * count,
        )

    def spread(self, local, others, lo, hi, token):
        def kernel(ints, reals, local, *refs):
            others, (mine, core, chip), (flat, stage) = refs[:-5], refs[-5:-2], refs[-2:]
            scalars = self.scalars(ints, reals)
            flat[...] = sums(scalars, local, others).reshape(flat.shape)
            for o in range(QUAD):
                for j in range(self.owned):
                    for a in range(2):
                        r = o * self.owned + j + a * self.pairs
                        stage[o, 2 * j + a] = flat[pl.ds(r, self.block, stride=self.near), :]
            mine[0] = stage[scalars.rank]
            core[0, 0] = stage[scalars.rank ^ 1]
            core[1, 0] = stage[scalars.rank ^ 3]
            chip[0, 0] = stage[scalars.rank ^ 2]

        return call(
            kernel,
            "spread",
            token,
            (hi - lo,),
            [self.ints, self.reals, local] + others,
            [SMEM, SMEM, self.side(lo, 0)] + [self.side(0, 0)] * len(others),
            [self.part(), self.parts(2), self.parts(1)],
            self.quad_shapes(hi - lo),
            [
                pltpu.VMEM((self.block * self.near, self.cells), jnp.float32),
                pltpu.VMEM((QUAD, self.cycles, self.block, self.cells), jnp.float32),
            ],
        )

    def join(self, held, new, token):
        def kernel(held, new, out):
            out[...] = new[...]

        return call(
            kernel,
            "join",
            token,
            (held.shape[1],),
            [held, new],
            [ANY, self.parts(1, 1)],
            self.parts(1, 1),
            shaped(*held.shape),
            alias={0: 0},
        )

    def own_rows(self, shape):
        return pl.BlockSpec(
            (1, self.owned) + shape, lambda i, ints: (ints[1] // QUAD, ints[1] % QUAD, 0, 0)
        )

    def table_call(self, kernel, name, fields, inputs, in_specs, out_specs, out_shape, scratch, token):
        extra = [t for t in token or () if all(t is not x for x in inputs)]
        count = len(inputs)
        return pl.pallas_call(
            lambda *refs: kernel(*refs[: count + 1], *refs[count + 1 + len(extra) :]),
            grid_spec=pltpu.PrefetchScalarGridSpec(
                num_scalar_prefetch=1,
                grid=(fields,),
                in_specs=in_specs + [ANY] * len(extra),
                out_specs=out_specs,
                scratch_shapes=scratch,
            ),
            out_shape=out_shape,
            compiler_params=PARAMS,
            cost_estimate=COST,
            name=name,
        )(self.ints, *inputs, *extra)

    def block4(self, *shape):
        return pl.BlockSpec((1,) + shape, lambda i, ints: (i, 0, 0, 0))

    def coefficients(self, mine, core, chip, token):
        fields = mine.shape[0]

        def kernel(ints, reals, table, mine, core, chip, out, column):
            scalars = self.scalars(ints, reals)
            row = lax.broadcasted_iota(jnp.int32, (self.depth, self.cells), 0)
            for k, part in enumerate((mine[0], core[0, 0], chip[0, 0], chip[1, 0])):
                column[:, scalars.rank ^ k] = part
            for j in range(self.owned):
                modes = [
                    jnp.dot(
                        table[0, j],
                        column[2 * j + a].reshape(QUAD * self.block, self.cells),
                        precision=lax.Precision.HIGHEST,
                        preferred_element_type=jnp.float32,
                    )
                    for a in range(2)
                ]
                split = scalars.split(scalars.rank * self.owned + j)
                out[0, j] = jnp.where(row < split, modes[0], modes[1])

        return self.table_call(
            kernel,
            "coefficients",
            fields,
            [self.reals, self.table, mine, core, chip],
            [SMEM, self.own_rows(self.table.shape[2:]), self.part(), self.parts(1), self.parts(2)],
            self.block4(self.owned, self.depth, self.cells),
            shaped(fields, self.owned, self.depth, self.cells),
            [pltpu.VMEM((self.cycles, QUAD, self.block, self.cells), jnp.float32)],
            token,
        )

    def filtered(self, own, other, mine, core, chip, token):
        fields = mine.shape[0]

        def kernel(ints, reals, back, own, other, mine, core, chip, *refs):
            (mine_out, core_out, chip_out), waves = refs[:3], refs[3]
            scalars = self.scalars(ints, reals)
            row = lax.broadcasted_iota(jnp.int32, (self.depth, self.cells), 0)
            source = (mine.at[0], core.at[0, 0], chip.at[0, 0], chip.at[1, 0])
            result = (mine_out.at[0], core_out.at[0, 0], chip_out.at[0, 0], chip_out.at[1, 0])
            for j in range(self.owned):
                pair = scalars.rank * self.owned + j
                total = own[0, j] + other[0, j]
                keep = row < scalars.split(pair)
                for a in range(2):
                    waves[2 * j + a] = jnp.dot(
                        back[0, j],
                        jnp.where(keep if a == 0 else jnp.logical_not(keep), total, 0.0),
                        precision=lax.Precision.HIGHEST,
                        preferred_element_type=jnp.float32,
                    ).reshape(QUAD, self.block, self.cells)
                    r = pair + a * self.pairs
                    for k in range(QUAD):
                        result[k][2 * j + a] = (
                            scalars.base(r) * source[k][2 * j + a]
                            + scalars.scale(r) * waves[2 * j + a, scalars.rank ^ k]
                        )

        modes = self.block4(self.owned, self.depth, self.cells)
        return self.table_call(
            kernel,
            "filtered",
            fields,
            [self.reals, self.back, own, other, mine, core, chip],
            [SMEM, self.own_rows(self.back.shape[2:]), modes, modes]
            + [self.part(), self.parts(1), self.parts(2)],
            [self.part(), self.parts(1), self.parts(2)],
            self.quad_shapes(fields),
            [pltpu.VMEM((self.cycles, QUAD, self.block, self.cells), jnp.float32)],
            token,
        )

    def place_near(self, mine, core, chip, held, lo, hi, token):
        carried = [] if held is None else [held]

        def kernel(ints, reals, mine, core, chip, *refs):
            out, stage = refs[-2:]
            rank = self.scalars(ints, reals).rank
            for k, part in enumerate((mine[0], core[0, 0], chip[0, 0], core[1, 0])):
                stage[rank ^ k] = part
            for o in range(QUAD):
                for j in range(self.owned):
                    for a in range(2):
                        out[0, :, o * self.owned + j + a * self.pairs, :] = stage[o, 2 * j + a]

        return call(
            kernel,
            "place_near",
            token,
            (hi - lo,),
            [self.ints, self.reals, mine, core, chip] + carried,
            [SMEM, SMEM, self.part(), self.parts(2), self.parts(1)] + [ANY] * len(carried),
            self.side(lo, 0),
            shaped(*self.shape),
            [pltpu.VMEM((QUAD, self.cycles, self.block, self.cells), jnp.float32)],
            alias={5: 0} if carried else None,
        )

    def place_far(self, local, others, held, lo, hi, token):
        def kernel(ints, reals, local, *refs):
            others, out = refs[: len(refs) - 1 - len(carried)], refs[-1]
            out[0] = sums(self.scalars(ints, reals), local, others)

        carried = [] if held is None else [held]
        return call(
            kernel,
            "place_far",
            token,
            (hi - lo,),
            [self.ints, self.reals, local] + others + carried,
            [SMEM, SMEM, self.side(lo, 1)]
            + [self.side(0, 0)] * len(others)
            + [ANY] * len(carried),
            self.side(lo, 1),
            shaped(*self.shape),
            alias={3 + len(others): 0} if carried else None,
        )


def spans(sizes, total):
    ends = np.cumsum(sizes)
    return [(int(end - size), int(end)) for size, end in zip(sizes, ends)]


def body(adjoint, source, viscosity, kappa, coupling, bc_flags, inst_map):
    slots = lax.axis_size("inst")
    sectors = lax.axis_size("space")
    center = adjoint[0]
    fields, block, cycles, cells = center.shape
    near = cycles // 2
    points = block * sectors
    quads = sectors // QUAD

    def to_partner(x, pick):
        pairs = []
        for i in range(slots):
            for p in range(sectors):
                pairs.append((i * sectors + p, pick(i, p % 2) * sectors + p))
        return lax.ppermute(x, ("inst", "space"), pairs)

    def to_first(x):
        return to_partner(x, lambda i, core: first_partner(i, core, slots))

    def to_later(x, s):
        return to_partner(x, lambda i, core: later_partner(i, core, slots, s))

    def to_sector(x, k):
        return lax.ppermute(x, "space", [(i, i ^ k) for i in range(sectors)])

    def ring(x, step):
        return lax.ppermute(x, "space", [(i, (i + step) % sectors) for i in range(sectors)])

    table, split, base, scale = mode_layout(points, near)
    table = table.reshape(table.shape[0], table.shape[1], quads, QUAD * block).transpose(2, 0, 1, 3)
    here = jnp.stack([lax.axis_index("inst"), lax.axis_index("space")])
    ints = jnp.concatenate([here, inst_map, jnp.asarray(split)])
    reals = jnp.asarray(np.concatenate([spectral_values(slots), base, scale]).astype(np.float32))
    plan = Plan(
        ints,
        reals,
        slots,
        center.shape,
        near,
        jnp.asarray(np.ascontiguousarray(table)),
        jnp.asarray(np.ascontiguousarray(table.transpose(0, 1, 3, 2))),
    )

    groups = [(lo, hi, 0) for lo, hi in spans(NEAR_SIZES, fields)]
    groups += [(lo, hi, 1) for lo, hi in spans(FAR_SIZES, fields)]
    first, others, parts, own, done = {}, {}, {}, {}, {}
    last, local, held, halos = None, None, None, None
    sent, crossed = [], []
    for step, g in ORDER:
        lo, hi, index = groups[g]
        before = last
        token = [] if last is None or step in FREE else [last]
        if step in ("pack", "mix"):
            token += sent[-DEPTH : len(sent) - DEPTH + 1] if len(sent) >= DEPTH else []
        if step in ("join", "coef", "filter"):
            token += crossed[-CROSS : len(crossed) - CROSS + 1] if len(crossed) >= CROSS else []
        if step == "pack":
            packed = pack(center, viscosity, lo, hi, index, near, halos is None, token)
            last = packed[0]
            first[g] = to_first(packed[0])
            sent.append(first[g])
            if halos is None:
                halos = ring(packed[1], 1), ring(packed[2], -1)
        elif step == "local":
            local = last = local_part(
                center, source[0], viscosity, kappa, coupling, bc_flags, *halos, token
            )
        elif step == "mix":
            mixed = plan.mix(center, first[g], lo, hi, index, token)
            last = mixed[0]
            others[g] = [first[g]] + [to_later(x, s + 1) for s, x in enumerate(mixed)]
            sent.append(others[g][-1])
        elif step == "spread":
            mine, core, chip = plan.spread(local, others[g], lo, hi, token)
            last = mine
            parts[g] = mine, to_sector(core, 1), chip
        elif step == "join":
            mine, core, chip = parts[g]
            last = plan.join(chip, core, token)
            parts[g] = mine, core, to_sector(last, 2)
            crossed.append(parts[g][2])
        elif step == "coef":
            part = last = plan.coefficients(*parts[g], token)
            stride = QUAD
            while 2 * stride < sectors:
                part = part + to_sector(part, stride)
                stride = 2 * stride
            other = to_sector(part, stride) if stride < sectors else jnp.zeros_like(part)
            own[g] = part, other
            crossed.append(other)
        elif step == "filter":
            mine, core, chip = plan.filtered(*own[g], *parts[g], token)
            last = mine
            done[g] = mine, core, to_sector(chip, 2)
            crossed.append(done[g][2])
        elif step == "back":
            mine, core, chip = done[g]
            last = plan.join(core, chip, token)
            done[g] = mine, to_sector(last, 1), chip
        elif step == "near":
            held = last = plan.place_near(*done[g], held, lo, hi, token)
        else:
            held = last = plan.place_far(local, others[g], held, lo, hi, token)
        if step in FREE:
            last = before
    return held[None]


def solution(mesh):
    return jax.shard_map(
        body,
        mesh=mesh,
        in_specs=(
            P("inst", None, "space", None, None),
            P("inst", None, "space", None, None),
            P("space", None, None),
            P(),
            P(),
            P(),
            P(),
        ),
        out_specs=P("inst", None, "space", None, None),
        check_vma=False,
    )
```

```python
import functools

import jax
import jax.numpy as jnp
import numpy as np
from jax import lax
from jax.experimental import pallas as pl
from jax.experimental.pallas import tpu as pltpu
from jax.sharding import PartitionSpec as P

QUAD = 4
NEAR_SIZES = (1, 2, 1, 1)
FAR_SIZES = (2, 1, 2)
ORDER = (
    ("pack", 0),
    ("pack", 1),
    ("pack", 2),
    ("local", 0),
    ("mix", 0),
    ("mix", 1),
    ("mix", 2),
    ("pack", 6),
    ("spread", 0),
    ("pack", 3),
    ("join", 0),
    ("pack", 4),
    ("spread", 1),
    ("coef", 0),
    ("join", 1),
    ("mix", 4),
    ("mix", 3),
    ("pack", 5),
    ("spread", 2),
    ("filter", 0),
    ("join", 2),
    ("coef", 1),
    ("spread", 3),
    ("mix", 6),
    ("back", 0),
    ("join", 3),
    ("coef", 2),
    ("filter", 1),
    ("mix", 5),
    ("far", 4),
    ("coef", 3),
    ("filter", 2),
    ("near", 0),
    ("filter", 3),
    ("back", 2),
    ("back", 1),
    ("far", 5),
    ("near", 2),
    ("far", 6),
    ("near", 1),
    ("back", 3),
    ("near", 3),
)
EDGES = tuple(zip(ORDER[:-1], ORDER[1:]))
SMEM = pl.BlockSpec(memory_space=pltpu.SMEM)
ANY = pl.BlockSpec(memory_space=pl.ANY)
COST = pl.CostEstimate(flops=0, bytes_accessed=0, transcendentals=0)
PARAMS = pltpu.CompilerParams(vmem_limit_bytes=48 * 1024 * 1024)


def spectral_values(slots):
    offset = np.arange(1 - slots, slots)
    safe = np.where(offset == 0, 1.0, np.sin(np.pi * offset / slots))
    return np.where(offset == 0, 0.0, 0.5 * (1.0 - 2.0 * (np.abs(offset) % 2)) / safe)


def mode_layout(points, near):
    half = points // 2
    pairs = near // 2
    theta = np.arange(points)
    bases, base, scale = [], np.zeros(near), np.zeros(near)
    for r in range(near):
        cutoff = max(4, points * (r + 1) // (2 * near))
        weight = max(1.0 - r / near, 0.0)
        kept = [m for m in range(half + 1) if m < cutoff]
        out = [m for m in range(half + 1) if m >= cutoff]
        count = [sum(1 if m in (0, half) else 2 for m in modes) for modes in (kept, out)]
        low = count[0] <= count[1]
        rows = []
        for m in kept if low else out:
            angle = 2.0 * np.pi * (m * theta % points) / points
            if m in (0, half):
                rows.append(np.cos(angle) / np.sqrt(points))
            else:
                rows.append(np.cos(angle) * np.sqrt(2.0 / points))
                rows.append(np.sin(angle) * np.sqrt(2.0 / points))
        bases.append(rows)
        base[r] = 1.0 - weight if low else 1.0
        scale[r] = weight if low else -weight
    depth = max(len(bases[p]) + len(bases[p + pairs]) for p in range(pairs))
    depth = -(-depth // 8) * 8
    table = np.zeros((pairs, depth, points), np.float32)
    split = np.zeros(pairs, np.int32)
    for p in range(pairs):
        rows = bases[p] + bases[p + pairs]
        table[p, : len(rows)] = np.stack(rows)
        split[p] = len(bases[p])
    return table, split, base, scale


class Scalars:
    def __init__(self, ints, reals, slots, near):
        self.ints, self.reals, self.slots, self.near = ints, reals, slots, near
        self.slot, self.place = ints[0], ints[1]
        self.rank = self.place % QUAD

    def weight(self, i, j):
        return self.reals[self.ints[2 + i] - self.ints[2 + j] + self.slots - 1]

    def split(self, pair):
        return self.ints[2 + self.slots + pair]

    def base(self, r):
        return self.reals[2 * self.slots - 1 + r]

    def scale(self, r):
        return self.reals[2 * self.slots - 1 + self.near + r]

    def first(self):
        return first_partner(self.slot, self.place % 2, self.slots)

    def target(self, s):
        return later_partner(self.slot, self.place % 2, self.slots, s)


def first_partner(slot, core, slots):
    if slots == 4:
        return slot ^ (2 - core)
    return slot ^ 1


def later_partner(slot, core, slots, s):
    if slots == 4:
        return slot ^ (1 + core)
    return (slot // 2 + s) % (slots // 2) * 2 + slot % 2


def call(kernel, name, token, grid, inputs, in_specs, out_specs, out_shape, scratch=(), alias=None):
    extra = [t for t in token or () if all(t is not x for x in inputs)]
    return pl.pallas_call(
        lambda *refs: kernel(*refs[: len(inputs)], *refs[len(inputs) + len(extra) :]),
        grid=grid,
        in_specs=list(in_specs) + [ANY] * len(extra),
        out_specs=out_specs,
        out_shape=out_shape,
        scratch_shapes=list(scratch),
        input_output_aliases=alias or {},
        compiler_params=PARAMS,
        cost_estimate=COST,
        name=name,
    )(*inputs, *extra)


def shaped(*shape):
    return jax.ShapeDtypeStruct(shape, jnp.float32)


def pack(center, viscosity, lo, hi, index, near, edges, token):
    fields, block, rows, cells = center.shape
    inputs, in_specs = [center], [pl.BlockSpec((1, block, near, cells), lambda i: (lo + i, 0, index, 0))]
    shapes = [shaped(hi - lo, block, near, cells)]
    out_specs = [pl.BlockSpec((1, block, near, cells), lambda i: (i, 0, 0, 0))]
    if edges:
        for start in (block - 1, 0):
            inputs += [center, viscosity]
            in_specs.append(pl.BlockSpec((fields, 1, rows, cells), lambda i, s=start: (0, s, 0, 0)))
            in_specs.append(pl.BlockSpec((1, rows, cells), lambda i, s=start: (s, 0, 0)))
            shapes.append(shaped(fields + 1, 1, rows, cells))
            out_specs.append(pl.BlockSpec((fields + 1, 1, rows, cells), lambda i: (0, 0, 0, 0)))

    def kernel(source, *refs):
        out, rest = refs[len(inputs) - 1], refs[len(inputs) :]
        out[...] = source[...]
        for e, edge in enumerate(rest):
            edge[:fields] = refs[2 * e][...]
            edge[fields] = refs[2 * e + 1][...]

    return call(kernel, "pack", token, (hi - lo,), inputs, in_specs, out_specs, shapes)


def local_kernel(
    coupling, kappa, flags, adj, before, after, src, mu, mu_before, mu_after, low, high, out
):
    fields, planes, rows, cells = adj.shape
    step = pl.program_id(0)
    first = step == 0
    last = step == pl.num_programs(0) - 1
    row = lax.broadcasted_iota(jnp.int32, (rows, cells), 0)
    col = lax.broadcasted_iota(jnp.int32, (rows, cells), 1)
    ring = 0.5 / (row.astype(jnp.float32) + 1.0)

    def pick(source, behind, ahead, f, k):
        if k < 0:
            return jnp.where(first, low[f, 0], behind)
        if k >= planes:
            return jnp.where(last, high[f, 0], ahead)
        return source

    def visc(k):
        return pick(mu[max(0, min(k, planes - 1))], mu_before[0], mu_after[0], fields, k)

    def cell(f, k):
        return pick(adj[f, max(0, min(k, planes - 1))], before[f, 0], after[f, 0], f, k)

    walls = []
    for f in range(fields):
        opens = [(1 - flags[f, i]).astype(jnp.float32) for i in range(3)]
        wall = jnp.where(col == 0, opens[0], 0.0)
        wall = wall + jnp.where(col == cells - 1, opens[1], 0.0)
        walls.append(wall + jnp.where(row == rows - 1, opens[2], 0.0))

    for k in range(planes):
        m = visc(k)
        up = ring * (m + visc(k + 1))
        down = ring * (m + visc(k - 1))
        outer = jnp.where(row < rows - 1, 0.5 * (m + pltpu.roll(m, rows - 1, 0)), 0.0)
        inner = jnp.where(row > 0, 0.5 * (m + pltpu.roll(m, 1, 0)), 0.0)
        east = jnp.where(col < cells - 1, 0.5 * (m + pltpu.roll(m, cells - 1, 1)), 0.0)
        west = jnp.where(col > 0, 0.5 * (m + pltpu.roll(m, 1, 1)), 0.0)
        diag = up + down + outer + inner + east + west
        for f in range(fields):
            p = adj[f, k]
            flux = (diag + walls[f] * m) * p
            flux = flux - up * cell(f, k + 1) - down * cell(f, k - 1)
            flux = flux - outer * pltpu.roll(p, rows - 1, 0) - inner * pltpu.roll(p, 1, 0)
            flux = flux - east * pltpu.roll(p, cells - 1, 1) - west * pltpu.roll(p, 1, 1)
            total = src[f, k] + kappa[f] * flux
            for g in range(fields):
                total = total + coupling[g, f] * adj[g, k]
            out[f, k] = total


def local_part(center, source, viscosity, kappa, coupling, flags, low, high, token):
    fields, block, rows, cells = center.shape
    planes = min(4, block)

    def whole(width, index):
        return pl.BlockSpec((fields, width, rows, cells), lambda i: (0, index(i), 0, 0))

    def plane(width, index):
        return pl.BlockSpec((width, rows, cells), lambda i: (index(i), 0, 0))

    behind = lambda i: jnp.maximum(i * planes - 1, 0)
    ahead = lambda i: jnp.minimum(i * planes + planes, block - 1)
    here = lambda i: i
    halo = pl.BlockSpec((fields + 1, 1, rows, cells), lambda i: (0, 0, 0, 0))
    return call(
        local_kernel,
        "local_part",
        token,
        (block // planes,),
        [coupling, kappa, flags, center, center, center, source, viscosity, viscosity, viscosity, low, high],
        [
            SMEM,
            SMEM,
            SMEM,
            whole(planes, here),
            whole(1, behind),
            whole(1, ahead),
            whole(planes, here),
            plane(planes, here),
            plane(1, behind),
            plane(1, ahead),
            halo,
            halo,
        ],
        whole(planes, here),
        shaped(*center.shape),
    )


def sums(scalars, local, others):
    total = local[0] + scalars.weight(scalars.first(), scalars.slot) * others[0][0]
    for part in others[1:]:
        total = total + part[0]
    return total


class Plan:
    def __init__(self, ints, reals, slots, shape, near, table, back):
        self.ints, self.reals, self.slots, self.near = ints, reals, slots, near
        self.shape, self.table, self.back = shape, table, back
        self.fields, self.block, self.rows, self.cells = shape
        self.pairs = near // 2
        self.owned = self.pairs // QUAD
        self.cycles = near // QUAD
        self.depth = table.shape[2]

    def scalars(self, ints, reals):
        return Scalars(ints, reals, self.slots, self.near)

    def side(self, first, index):
        return pl.BlockSpec((1, self.block, self.near, self.cells), lambda i: (first + i, 0, index, 0))

    def part(self):
        return pl.BlockSpec((1, self.cycles, self.block, self.cells), lambda i, *_: (i, 0, 0, 0))

    def parts(self, count, first=0):
        shape = (count, 1, self.cycles, self.block, self.cells)
        return pl.BlockSpec(shape, lambda i, *_: (first, i, 0, 0, 0))

    def quad_shapes(self, fields):
        one = (fields, self.cycles, self.block, self.cells)
        return [shaped(*one), shaped(2, *one), shaped(2, *one)]

    def mix(self, center, first, lo, hi, index, token):
        count = max(1, self.slots // 2 - 1)

        def kernel(ints, reals, own, got, *outs):
            scalars = self.scalars(ints, reals)
            for s in range(count):
                target = scalars.target(s + 1)
                outs[s][0] = (
                    scalars.weight(scalars.slot, target) * own[0]
                    + scalars.weight(scalars.first(), target) * got[0]
                )

        return call(
            kernel,
            "mix",
            token,
            (hi - lo,),
            [self.ints, self.reals, center, first],
            [SMEM, SMEM, self.side(lo, index), self.side(0, 0)],
            [self.side(0, 0)] * count,
            [shaped(hi - lo, self.block, self.near, self.cells)] * count,
        )

    def spread(self, local, others, lo, hi, token):
        def kernel(ints, reals, local, *refs):
            others, (mine, core, chip), (flat, stage) = refs[:-5], refs[-5:-2], refs[-2:]
            scalars = self.scalars(ints, reals)
            flat[...] = sums(scalars, local, others).reshape(flat.shape)
            for o in range(QUAD):
                for j in range(self.owned):
                    for a in range(2):
                        r = o * self.owned + j + a * self.pairs
                        stage[o, 2 * j + a] = flat[pl.ds(r, self.block, stride=self.near), :]
            mine[0] = stage[scalars.rank]
            core[0, 0] = stage[scalars.rank ^ 1]
            core[1, 0] = stage[scalars.rank ^ 3]
            chip[0, 0] = stage[scalars.rank ^ 2]

        return call(
            kernel,
            "spread",
            token,
            (hi - lo,),
            [self.ints, self.reals, local] + others,
            [SMEM, SMEM, self.side(lo, 0)] + [self.side(0, 0)] * len(others),
            [self.part(), self.parts(2), self.parts(1)],
            self.quad_shapes(hi - lo),
            [
                pltpu.VMEM((self.block * self.near, self.cells), jnp.float32),
                pltpu.VMEM((QUAD, self.cycles, self.block, self.cells), jnp.float32),
            ],
        )

    def join(self, held, new, token):
        def kernel(held, new, out):
            out[...] = new[...]

        return call(
            kernel,
            "join",
            token,
            (held.shape[1],),
            [held, new],
            [ANY, self.parts(1, 1)],
            self.parts(1, 1),
            shaped(*held.shape),
            alias={0: 0},
        )

    def own_rows(self, shape):
        return pl.BlockSpec(
            (1, self.owned) + shape, lambda i, ints: (ints[1] // QUAD, ints[1] % QUAD, 0, 0)
        )

    def table_call(self, kernel, name, fields, inputs, in_specs, out_specs, out_shape, scratch, token):
        extra = [t for t in token or () if all(t is not x for x in inputs)]
        count = len(inputs)
        return pl.pallas_call(
            lambda *refs: kernel(*refs[: count + 1], *refs[count + 1 + len(extra) :]),
            grid_spec=pltpu.PrefetchScalarGridSpec(
                num_scalar_prefetch=1,
                grid=(fields,),
                in_specs=in_specs + [ANY] * len(extra),
                out_specs=out_specs,
                scratch_shapes=scratch,
            ),
            out_shape=out_shape,
            compiler_params=PARAMS,
            cost_estimate=COST,
            name=name,
        )(self.ints, *inputs, *extra)

    def block4(self, *shape):
        return pl.BlockSpec((1,) + shape, lambda i, ints: (i, 0, 0, 0))

    def coefficients(self, mine, core, chip, token):
        fields = mine.shape[0]

        def kernel(ints, reals, table, mine, core, chip, out, column):
            scalars = self.scalars(ints, reals)
            row = lax.broadcasted_iota(jnp.int32, (self.depth, self.cells), 0)
            for k, part in enumerate((mine[0], core[0, 0], chip[0, 0], chip[1, 0])):
                column[:, scalars.rank ^ k] = part
            for j in range(self.owned):
                modes = [
                    jnp.dot(
                        table[0, j],
                        column[2 * j + a].reshape(QUAD * self.block, self.cells),
                        precision=lax.Precision.HIGHEST,
                        preferred_element_type=jnp.float32,
                    )
                    for a in range(2)
                ]
                split = scalars.split(scalars.rank * self.owned + j)
                out[0, j] = jnp.where(row < split, modes[0], modes[1])

        return self.table_call(
            kernel,
            "coefficients",
            fields,
            [self.reals, self.table, mine, core, chip],
            [SMEM, self.own_rows(self.table.shape[2:]), self.part(), self.parts(1), self.parts(2)],
            self.block4(self.owned, self.depth, self.cells),
            shaped(fields, self.owned, self.depth, self.cells),
            [pltpu.VMEM((self.cycles, QUAD, self.block, self.cells), jnp.float32)],
            token,
        )

    def filtered(self, own, other, mine, core, chip, token):
        fields = mine.shape[0]

        def kernel(ints, reals, back, own, other, mine, core, chip, *refs):
            (mine_out, core_out, chip_out), waves = refs[:3], refs[3]
            scalars = self.scalars(ints, reals)
            row = lax.broadcasted_iota(jnp.int32, (self.depth, self.cells), 0)
            source = (mine.at[0], core.at[0, 0], chip.at[0, 0], chip.at[1, 0])
            result = (mine_out.at[0], core_out.at[0, 0], chip_out.at[0, 0], chip_out.at[1, 0])
            for j in range(self.owned):
                pair = scalars.rank * self.owned + j
                total = own[0, j] + other[0, j]
                keep = row < scalars.split(pair)
                for a in range(2):
                    waves[2 * j + a] = jnp.dot(
                        back[0, j],
                        jnp.where(keep if a == 0 else jnp.logical_not(keep), total, 0.0),
                        precision=lax.Precision.HIGHEST,
                        preferred_element_type=jnp.float32,
                    ).reshape(QUAD, self.block, self.cells)
                    r = pair + a * self.pairs
                    for k in range(QUAD):
                        result[k][2 * j + a] = (
                            scalars.base(r) * source[k][2 * j + a]
                            + scalars.scale(r) * waves[2 * j + a, scalars.rank ^ k]
                        )

        modes = self.block4(self.owned, self.depth, self.cells)
        return self.table_call(
            kernel,
            "filtered",
            fields,
            [self.reals, self.back, own, other, mine, core, chip],
            [SMEM, self.own_rows(self.back.shape[2:]), modes, modes]
            + [self.part(), self.parts(1), self.parts(2)],
            [self.part(), self.parts(1), self.parts(2)],
            self.quad_shapes(fields),
            [pltpu.VMEM((self.cycles, QUAD, self.block, self.cells), jnp.float32)],
            token,
        )

    def place_near(self, mine, core, chip, held, lo, hi, token):
        carried = [] if held is None else [held]

        def kernel(ints, reals, mine, core, chip, *refs):
            out, stage = refs[-2:]
            rank = self.scalars(ints, reals).rank
            for k, part in enumerate((mine[0], core[0, 0], chip[0, 0], core[1, 0])):
                stage[rank ^ k] = part
            for o in range(QUAD):
                for j in range(self.owned):
                    for a in range(2):
                        out[0, :, o * self.owned + j + a * self.pairs, :] = stage[o, 2 * j + a]

        return call(
            kernel,
            "place_near",
            token,
            (hi - lo,),
            [self.ints, self.reals, mine, core, chip] + carried,
            [SMEM, SMEM, self.part(), self.parts(2), self.parts(1)] + [ANY] * len(carried),
            self.side(lo, 0),
            shaped(*self.shape),
            [pltpu.VMEM((QUAD, self.cycles, self.block, self.cells), jnp.float32)],
            alias={5: 0} if carried else None,
        )

    def place_far(self, local, others, held, lo, hi, token):
        def kernel(ints, reals, local, *refs):
            others, out = refs[: len(refs) - 1 - len(carried)], refs[-1]
            out[0] = sums(self.scalars(ints, reals), local, others)

        carried = [] if held is None else [held]
        return call(
            kernel,
            "place_far",
            token,
            (hi - lo,),
            [self.ints, self.reals, local] + others + carried,
            [SMEM, SMEM, self.side(lo, 1)]
            + [self.side(0, 0)] * len(others)
            + [ANY] * len(carried),
            self.side(lo, 1),
            shaped(*self.shape),
            alias={3 + len(others): 0} if carried else None,
        )


def spans(sizes, total):
    ends = np.cumsum(sizes)
    return [(int(end - size), int(end)) for size, end in zip(sizes, ends)]


def body(adjoint, source, viscosity, kappa, coupling, bc_flags, inst_map):
    slots = lax.axis_size("inst")
    sectors = lax.axis_size("space")
    center = adjoint[0]
    fields, block, cycles, cells = center.shape
    near = cycles // 2
    points = block * sectors
    quads = sectors // QUAD

    def to_partner(x, pick):
        pairs = []
        for i in range(slots):
            for p in range(sectors):
                pairs.append((i * sectors + p, pick(i, p % 2) * sectors + p))
        return lax.ppermute(x, ("inst", "space"), pairs)

    def to_first(x):
        return to_partner(x, lambda i, core: first_partner(i, core, slots))

    def to_later(x, s):
        return to_partner(x, lambda i, core: later_partner(i, core, slots, s))

    def to_sector(x, k):
        return lax.ppermute(x, "space", [(i, i ^ k) for i in range(sectors)])

    def ring(x, step):
        return lax.ppermute(x, "space", [(i, (i + step) % sectors) for i in range(sectors)])

    table, split, base, scale = mode_layout(points, near)
    table = table.reshape(table.shape[0], table.shape[1], quads, QUAD * block).transpose(2, 0, 1, 3)
    here = jnp.stack([lax.axis_index("inst"), lax.axis_index("space")])
    ints = jnp.concatenate([here, inst_map, jnp.asarray(split)])
    reals = jnp.asarray(np.concatenate([spectral_values(slots), base, scale]).astype(np.float32))
    plan = Plan(
        ints,
        reals,
        slots,
        center.shape,
        near,
        jnp.asarray(np.ascontiguousarray(table)),
        jnp.asarray(np.ascontiguousarray(table.transpose(0, 1, 3, 2))),
    )

    groups = [(lo, hi, 0) for lo, hi in spans(NEAR_SIZES, fields)]
    groups += [(lo, hi, 1) for lo, hi in spans(FAR_SIZES, fields)]
    first, others, parts, own, done = {}, {}, {}, {}, {}
    made, local, held, halos = {}, None, None, None
    for step, g in ORDER:
        lo, hi, index = groups[g]
        token = [made[before] for before, after in EDGES if after == (step, g)]
        if step == "pack":
            packed = pack(center, viscosity, lo, hi, index, near, halos is None, token)
            made[step, g] = packed[0]
            first[g] = to_first(packed[0])
            if halos is None:
                halos = ring(packed[1], 1), ring(packed[2], -1)
        elif step == "local":
            local = made[step, g] = local_part(
                center, source[0], viscosity, kappa, coupling, bc_flags, *halos, token
            )
        elif step == "mix":
            mixed = plan.mix(center, first[g], lo, hi, index, token)
            made[step, g] = mixed[0]
            others[g] = [first[g]] + [to_later(x, s + 1) for s, x in enumerate(mixed)]
        elif step == "spread":
            mine, core, chip = plan.spread(local, others[g], lo, hi, token)
            made[step, g] = mine
            parts[g] = mine, to_sector(core, 1), chip
        elif step == "join":
            mine, core, chip = parts[g]
            made[step, g] = plan.join(chip, core, token)
            parts[g] = mine, core, to_sector(made[step, g], 2)
        elif step == "coef":
            part = made[step, g] = plan.coefficients(*parts[g], token)
            stride = QUAD
            while 2 * stride < sectors:
                part = part + to_sector(part, stride)
                stride = 2 * stride
            other = to_sector(part, stride) if stride < sectors else jnp.zeros_like(part)
            own[g] = part, other
        elif step == "filter":
            mine, core, chip = plan.filtered(*own[g], *parts[g], token)
            made[step, g] = mine
            done[g] = mine, core, to_sector(chip, 2)
        elif step == "back":
            mine, core, chip = done[g]
            made[step, g] = plan.join(core, chip, token)
            done[g] = mine, to_sector(made[step, g], 1), chip
        elif step == "near":
            held = made[step, g] = plan.place_near(*done[g], held, lo, hi, token)
        else:
            held = made[step, g] = plan.place_far(local, others[g], held, lo, hi, token)
    return held[None]


def solution(mesh):
    return jax.shard_map(
        body,
        mesh=mesh,
        in_specs=(
            P("inst", None, "space", None, None),
            P("inst", None, "space", None, None),
            P("space", None, None),
            P(),
            P(),
            P(),
            P(),
        ),
        out_specs=P("inst", None, "space", None, None),
        check_vma=False,
    )
```

```python
import functools

import jax
import jax.numpy as jnp
import numpy as np
from jax import lax
from jax.experimental import pallas as pl
from jax.experimental.pallas import tpu as pltpu
from jax.sharding import PartitionSpec as P

QUAD = 4
NEAR_SIZES = (1, 1, 2, 1)
FAR_SIZES = (2, 1, 1, 1)
ORDER = (
    ("pack", 0),
    ("pack", 2),
    ("pack", 1),
    ("local", 0),
    ("mix", 2),
    ("mix", 1),
    ("pack", 5),
    ("pack", 6),
    ("pack", 4),
    ("spread", 1),
    ("join", 1),
    ("pack", 3),
    ("spread", 2),
    ("coef", 1),
    ("mix", 0),
    ("mix", 3),
    ("join", 2),
    ("pack", 7),
    ("spread", 0),
    ("filter", 1),
    ("join", 0),
    ("mix", 6),
    ("coef", 2),
    ("spread", 3),
    ("coef", 0),
    ("join", 3),
    ("mix", 7),
    ("local", 1),
    ("mix", 4),
    ("filter", 2),
    ("back", 1),
    ("mix", 5),
    ("coef", 3),
    ("filter", 0),
    ("near", 1),
    ("far", 6),
    ("back", 2),
    ("far", 7),
    ("filter", 3),
    ("back", 0),
    ("near", 0),
    ("near", 2),
    ("far", 4),
    ("back", 3),
    ("far", 5),
    ("near", 3),
)
EDGES = tuple(zip(ORDER[:-1], ORDER[1:]))
SMEM = pl.BlockSpec(memory_space=pltpu.SMEM)
STAMP = pl.BlockSpec((8, 128), lambda i: (0, 0))
ANY = pl.BlockSpec(memory_space=pl.ANY)
COST = pl.CostEstimate(flops=0, bytes_accessed=0, transcendentals=0)
PARAMS = pltpu.CompilerParams(vmem_limit_bytes=48 * 1024 * 1024)


def spectral_values(slots):
    offset = np.arange(1 - slots, slots)
    safe = np.where(offset == 0, 1.0, np.sin(np.pi * offset / slots))
    return np.where(offset == 0, 0.0, 0.5 * (1.0 - 2.0 * (np.abs(offset) % 2)) / safe)


def mode_layout(points, near):
    half = points // 2
    pairs = near // 2
    theta = np.arange(points)
    bases, base, scale = [], np.zeros(near), np.zeros(near)
    for r in range(near):
        cutoff = max(4, points * (r + 1) // (2 * near))
        weight = max(1.0 - r / near, 0.0)
        kept = [m for m in range(half + 1) if m < cutoff]
        out = [m for m in range(half + 1) if m >= cutoff]
        count = [sum(1 if m in (0, half) else 2 for m in modes) for modes in (kept, out)]
        low = count[0] <= count[1]
        rows = []
        for m in kept if low else out:
            angle = 2.0 * np.pi * (m * theta % points) / points
            if m in (0, half):
                rows.append(np.cos(angle) / np.sqrt(points))
            else:
                rows.append(np.cos(angle) * np.sqrt(2.0 / points))
                rows.append(np.sin(angle) * np.sqrt(2.0 / points))
        bases.append(rows)
        base[r] = 1.0 - weight if low else 1.0
        scale[r] = weight if low else -weight
    depth = max(len(bases[p]) + len(bases[p + pairs]) for p in range(pairs))
    depth = -(-depth // 8) * 8
    table = np.zeros((pairs, depth, points), np.float32)
    split = np.zeros(pairs, np.int32)
    for p in range(pairs):
        rows = bases[p] + bases[p + pairs]
        table[p, : len(rows)] = np.stack(rows)
        split[p] = len(bases[p])
    return table, split, base, scale


class Scalars:
    def __init__(self, ints, reals, slots, near):
        self.ints, self.reals, self.slots, self.near = ints, reals, slots, near
        self.slot, self.place = ints[0], ints[1]
        self.rank = self.place % QUAD

    def weight(self, i, j):
        return self.reals[self.ints[2 + i] - self.ints[2 + j] + self.slots - 1]

    def split(self, pair):
        return self.ints[2 + self.slots + pair]

    def base(self, r):
        return self.reals[2 * self.slots - 1 + r]

    def scale(self, r):
        return self.reals[2 * self.slots - 1 + self.near + r]

    def first(self):
        return first_partner(self.slot, self.place % 2, self.slots)

    def target(self, s):
        return later_partner(self.slot, self.place % 2, self.slots, s)


def first_partner(slot, core, slots):
    if slots == 4:
        return slot ^ (2 - core)
    return slot ^ 1


def later_partner(slot, core, slots, s):
    if slots == 4:
        return slot ^ (1 + core)
    return (slot // 2 + s) % (slots // 2) * 2 + slot % 2


def call(kernel, name, token, grid, inputs, in_specs, out_specs, out_shape, scratch=(), alias=None):
    extra = [t for t in token or () if all(t is not x for x in inputs)]
    return pl.pallas_call(
        lambda *refs: kernel(*refs[: len(inputs)], *refs[len(inputs) + len(extra) :]),
        grid=grid,
        in_specs=list(in_specs) + [ANY] * len(extra),
        out_specs=out_specs,
        out_shape=out_shape,
        scratch_shapes=list(scratch),
        input_output_aliases=alias or {},
        compiler_params=PARAMS,
        cost_estimate=COST,
        name=name,
    )(*inputs, *extra)


def shaped(*shape):
    return jax.ShapeDtypeStruct(shape, jnp.float32)


def pack(center, viscosity, lo, hi, index, near, edges, token):
    fields, block, rows, cells = center.shape
    inputs, in_specs = [center], [pl.BlockSpec((1, block, near, cells), lambda i: (lo + i, 0, index, 0))]
    shapes = [shaped(hi - lo, block, near, cells)]
    out_specs = [pl.BlockSpec((1, block, near, cells), lambda i: (i, 0, 0, 0))]
    if edges:
        for start in (block - 1, 0):
            inputs += [center, viscosity]
            in_specs.append(pl.BlockSpec((fields, 1, rows, cells), lambda i, s=start: (0, s, 0, 0)))
            in_specs.append(pl.BlockSpec((1, rows, cells), lambda i, s=start: (s, 0, 0)))
            shapes.append(shaped(fields + 1, 1, rows, cells))
            out_specs.append(pl.BlockSpec((fields + 1, 1, rows, cells), lambda i: (0, 0, 0, 0)))

    def kernel(source, *refs):
        out, rest = refs[len(inputs) - 1], refs[len(inputs) :]
        out[...] = source[...]
        for e, edge in enumerate(rest):
            edge[:fields] = refs[2 * e][...]
            edge[fields] = refs[2 * e + 1][...]

    return call(kernel, "pack", token, (hi - lo,), inputs, in_specs, out_specs, shapes)


def local_kernel(
    far, coupling, kappa, flags, adj, before, after, next_to, src, mu, mu_before, mu_after, mu_next, low, high, out, stamp
):
    fields, planes, rows, cells = adj.shape
    step = pl.program_id(0)
    first = step == 0
    last = step == pl.num_programs(0) - 1
    row = lax.broadcasted_iota(jnp.int32, (rows, cells), 0)
    col = lax.broadcasted_iota(jnp.int32, (rows, cells), 1)
    ring = 0.5 / ((row + rows * far).astype(jnp.float32) + 1.0)
    stamp[...] = jnp.zeros_like(stamp)

    def pick(source, behind, ahead, f, k):
        if k < 0:
            return jnp.where(first, low[f, 0], behind)
        if k >= planes:
            return jnp.where(last, high[f, 0], ahead)
        return source

    def visc(k):
        return pick(mu[max(0, min(k, planes - 1))], mu_before[0], mu_after[0], fields, k)

    def cell(f, k):
        return pick(adj[f, max(0, min(k, planes - 1))], before[f, 0], after[f, 0], f, k)

    def outward(x, edge):
        moved = pltpu.roll(x, rows - 1, 0)
        return moved if far else jnp.where(row == rows - 1, edge[:1], moved)

    def inward(x, edge):
        moved = pltpu.roll(x, 1, 0)
        return jnp.where(row == 0, edge[-1:], moved) if far else moved

    walls = []
    for f in range(fields):
        opens = [(1 - flags[f, i]).astype(jnp.float32) for i in range(3)]
        wall = jnp.where(col == 0, opens[0], 0.0)
        wall = wall + jnp.where(col == cells - 1, opens[1], 0.0)
        walls.append(wall + jnp.where(row == rows - 1, opens[2], 0.0) if far else wall)

    for k in range(planes):
        m = visc(k)
        up = ring * (m + visc(k + 1))
        down = ring * (m + visc(k - 1))
        outer = 0.5 * (m + outward(m, mu_next[k]))
        inner = 0.5 * (m + inward(m, mu_next[k]))
        if far:
            outer = jnp.where(row < rows - 1, outer, 0.0)
        else:
            inner = jnp.where(row > 0, inner, 0.0)
        east = jnp.where(col < cells - 1, 0.5 * (m + pltpu.roll(m, cells - 1, 1)), 0.0)
        west = jnp.where(col > 0, 0.5 * (m + pltpu.roll(m, 1, 1)), 0.0)
        diag = up + down + outer + inner + east + west
        for f in range(fields):
            p = adj[f, k]
            flux = (diag + walls[f] * m) * p
            flux = flux - up * cell(f, k + 1) - down * cell(f, k - 1)
            flux = flux - outer * outward(p, next_to[f, k]) - inner * inward(p, next_to[f, k])
            flux = flux - east * pltpu.roll(p, cells - 1, 1) - west * pltpu.roll(p, 1, 1)
            total = src[f, k] + kappa[f] * flux
            for g in range(fields):
                total = total + coupling[g, f] * adj[g, k]
            out[f, k] = total


def local_part(far, center, source, viscosity, kappa, coupling, flags, low, high, token):
    fields, block, rows, cells = center.shape
    half = rows // 2
    planes = min(4, block)
    edge = half // 8 - 1 if far else half // 8

    def whole(width, index):
        return pl.BlockSpec((fields, width, half, cells), lambda i: (0, index(i), far, 0))

    def plane(width, index):
        return pl.BlockSpec((width, half, cells), lambda i: (index(i), far, 0))

    behind = lambda i: jnp.maximum(i * planes - 1, 0)
    ahead = lambda i: jnp.minimum(i * planes + planes, block - 1)
    here = lambda i: i
    halo = pl.BlockSpec((fields + 1, 1, half, cells), lambda i: (0, 0, far, 0))
    return call(
        functools.partial(local_kernel, far),
        "local_part",
        token,
        (block // planes,),
        [coupling, kappa, flags, center, center, center, center, source]
        + [viscosity, viscosity, viscosity, viscosity, low, high],
        [
            SMEM,
            SMEM,
            SMEM,
            whole(planes, here),
            whole(1, behind),
            whole(1, ahead),
            pl.BlockSpec((fields, planes, 8, cells), lambda i: (0, i, edge, 0)),
            whole(planes, here),
            plane(planes, here),
            plane(1, behind),
            plane(1, ahead),
            pl.BlockSpec((planes, 8, cells), lambda i: (i, edge, 0)),
            halo,
            halo,
        ],
        [pl.BlockSpec((fields, planes, half, cells), lambda i: (0, i, 0, 0)), STAMP],
        [shaped(fields, block, half, cells), shaped(8, 128)],
    )


def sums(scalars, local, others):
    total = local[0] + scalars.weight(scalars.first(), scalars.slot) * others[0][0]
    for part in others[1:]:
        total = total + part[0]
    return total


class Plan:
    def __init__(self, ints, reals, slots, shape, near, table, back):
        self.ints, self.reals, self.slots, self.near = ints, reals, slots, near
        self.shape, self.table, self.back = shape, table, back
        self.fields, self.block, self.rows, self.cells = shape
        self.pairs = near // 2
        self.owned = self.pairs // QUAD
        self.cycles = near // QUAD
        self.depth = table.shape[2]

    def scalars(self, ints, reals):
        return Scalars(ints, reals, self.slots, self.near)

    def side(self, first, index):
        return pl.BlockSpec((1, self.block, self.near, self.cells), lambda i: (first + i, 0, index, 0))

    def part(self):
        return pl.BlockSpec((1, self.cycles, self.block, self.cells), lambda i, *_: (i, 0, 0, 0))

    def parts(self, count, first=0):
        shape = (count, 1, self.cycles, self.block, self.cells)
        return pl.BlockSpec(shape, lambda i, *_: (first, i, 0, 0, 0))

    def quad_shapes(self, fields):
        one = (fields, self.cycles, self.block, self.cells)
        return [shaped(*one), shaped(2, *one), shaped(2, *one)]

    def mix(self, center, first, lo, hi, index, token):
        count = max(1, self.slots // 2 - 1)

        def kernel(ints, reals, own, got, *outs):
            scalars = self.scalars(ints, reals)
            for s in range(count):
                target = scalars.target(s + 1)
                outs[s][0] = (
                    scalars.weight(scalars.slot, target) * own[0]
                    + scalars.weight(scalars.first(), target) * got[0]
                )

        return call(
            kernel,
            "mix",
            token,
            (hi - lo,),
            [self.ints, self.reals, center, first],
            [SMEM, SMEM, self.side(lo, index), self.side(0, 0)],
            [self.side(0, 0)] * count,
            [shaped(hi - lo, self.block, self.near, self.cells)] * count,
        )

    def spread(self, local, others, lo, hi, token):
        def kernel(ints, reals, local, *refs):
            others, (mine, core, chip), (flat, stage) = refs[:-5], refs[-5:-2], refs[-2:]
            scalars = self.scalars(ints, reals)
            flat[...] = sums(scalars, local, others).reshape(flat.shape)
            for o in range(QUAD):
                for j in range(self.owned):
                    for a in range(2):
                        r = o * self.owned + j + a * self.pairs
                        stage[o, 2 * j + a] = flat[pl.ds(r, self.block, stride=self.near), :]
            mine[0] = stage[scalars.rank]
            core[0, 0] = stage[scalars.rank ^ 1]
            core[1, 0] = stage[scalars.rank ^ 3]
            chip[0, 0] = stage[scalars.rank ^ 2]

        return call(
            kernel,
            "spread",
            token,
            (hi - lo,),
            [self.ints, self.reals, local] + others,
            [SMEM, SMEM, self.side(lo, 0)] + [self.side(0, 0)] * len(others),
            [self.part(), self.parts(2), self.parts(1)],
            self.quad_shapes(hi - lo),
            [
                pltpu.VMEM((self.block * self.near, self.cells), jnp.float32),
                pltpu.VMEM((QUAD, self.cycles, self.block, self.cells), jnp.float32),
            ],
        )

    def join(self, held, new, token):
        def kernel(held, new, out):
            out[...] = new[...]

        return call(
            kernel,
            "join",
            token,
            (held.shape[1],),
            [held, new],
            [ANY, self.parts(1, 1)],
            self.parts(1, 1),
            shaped(*held.shape),
            alias={0: 0},
        )

    def own_rows(self, shape):
        return pl.BlockSpec(
            (1, self.owned) + shape, lambda i, ints: (ints[1] // QUAD, ints[1] % QUAD, 0, 0)
        )

    def table_call(self, kernel, name, fields, inputs, in_specs, out_specs, out_shape, scratch, token):
        extra = [t for t in token or () if all(t is not x for x in inputs)]
        count = len(inputs)
        return pl.pallas_call(
            lambda *refs: kernel(*refs[: count + 1], *refs[count + 1 + len(extra) :]),
            grid_spec=pltpu.PrefetchScalarGridSpec(
                num_scalar_prefetch=1,
                grid=(fields,),
                in_specs=in_specs + [ANY] * len(extra),
                out_specs=out_specs,
                scratch_shapes=scratch,
            ),
            out_shape=out_shape,
            compiler_params=PARAMS,
            cost_estimate=COST,
            name=name,
        )(self.ints, *inputs, *extra)

    def block4(self, *shape):
        return pl.BlockSpec((1,) + shape, lambda i, ints: (i, 0, 0, 0))

    def coefficients(self, mine, core, chip, token):
        fields = mine.shape[0]

        def kernel(ints, reals, table, mine, core, chip, out, column):
            scalars = self.scalars(ints, reals)
            row = lax.broadcasted_iota(jnp.int32, (self.depth, self.cells), 0)
            for k, part in enumerate((mine[0], core[0, 0], chip[0, 0], chip[1, 0])):
                column[:, scalars.rank ^ k] = part
            for j in range(self.owned):
                modes = [
                    jnp.dot(
                        table[0, j],
                        column[2 * j + a].reshape(QUAD * self.block, self.cells),
                        precision=lax.Precision.HIGHEST,
                        preferred_element_type=jnp.float32,
                    )
                    for a in range(2)
                ]
                split = scalars.split(scalars.rank * self.owned + j)
                out[0, j] = jnp.where(row < split, modes[0], modes[1])

        return self.table_call(
            kernel,
            "coefficients",
            fields,
            [self.reals, self.table, mine, core, chip],
            [SMEM, self.own_rows(self.table.shape[2:]), self.part(), self.parts(1), self.parts(2)],
            self.block4(self.owned, self.depth, self.cells),
            shaped(fields, self.owned, self.depth, self.cells),
            [pltpu.VMEM((self.cycles, QUAD, self.block, self.cells), jnp.float32)],
            token,
        )

    def filtered(self, own, other, mine, core, chip, token):
        fields = mine.shape[0]

        def kernel(ints, reals, back, own, other, mine, core, chip, *refs):
            (mine_out, core_out, chip_out), waves = refs[:3], refs[3]
            scalars = self.scalars(ints, reals)
            row = lax.broadcasted_iota(jnp.int32, (self.depth, self.cells), 0)
            source = (mine.at[0], core.at[0, 0], chip.at[0, 0], chip.at[1, 0])
            result = (mine_out.at[0], core_out.at[0, 0], chip_out.at[0, 0], chip_out.at[1, 0])
            for j in range(self.owned):
                pair = scalars.rank * self.owned + j
                total = own[0, j] + other[0, j]
                keep = row < scalars.split(pair)
                for a in range(2):
                    waves[2 * j + a] = jnp.dot(
                        back[0, j],
                        jnp.where(keep if a == 0 else jnp.logical_not(keep), total, 0.0),
                        precision=lax.Precision.HIGHEST,
                        preferred_element_type=jnp.float32,
                    ).reshape(QUAD, self.block, self.cells)
                    r = pair + a * self.pairs
                    for k in range(QUAD):
                        result[k][2 * j + a] = (
                            scalars.base(r) * source[k][2 * j + a]
                            + scalars.scale(r) * waves[2 * j + a, scalars.rank ^ k]
                        )

        modes = self.block4(self.owned, self.depth, self.cells)
        return self.table_call(
            kernel,
            "filtered",
            fields,
            [self.reals, self.back, own, other, mine, core, chip],
            [SMEM, self.own_rows(self.back.shape[2:]), modes, modes]
            + [self.part(), self.parts(1), self.parts(2)],
            [self.part(), self.parts(1), self.parts(2)],
            self.quad_shapes(fields),
            [pltpu.VMEM((self.cycles, QUAD, self.block, self.cells), jnp.float32)],
            token,
        )

    def place_near(self, mine, core, chip, held, lo, hi, token):
        carried = [] if held is None else [held]

        def kernel(ints, reals, mine, core, chip, *refs):
            out, stamp, stage = refs[-3:]
            stamp[...] = jnp.zeros_like(stamp)
            rank = self.scalars(ints, reals).rank
            for k, part in enumerate((mine[0], core[0, 0], chip[0, 0], core[1, 0])):
                stage[rank ^ k] = part
            for o in range(QUAD):
                for j in range(self.owned):
                    for a in range(2):
                        out[0, :, o * self.owned + j + a * self.pairs, :] = stage[o, 2 * j + a]

        return call(
            kernel,
            "place_near",
            token,
            (hi - lo,),
            [self.ints, self.reals, mine, core, chip] + carried,
            [SMEM, SMEM, self.part(), self.parts(2), self.parts(1)] + [ANY] * len(carried),
            [self.side(lo, 0), STAMP],
            [shaped(*self.shape), shaped(8, 128)],
            [pltpu.VMEM((QUAD, self.cycles, self.block, self.cells), jnp.float32)],
            alias={5: 0} if carried else None,
        )

    def place_far(self, local, others, held, lo, hi, token):
        def kernel(ints, reals, local, *refs):
            others, (out, stamp) = refs[: len(refs) - 2 - len(carried)], refs[-2:]
            stamp[...] = jnp.zeros_like(stamp)
            out[0] = sums(self.scalars(ints, reals), local, others)

        carried = [] if held is None else [held]
        return call(
            kernel,
            "place_far",
            token,
            (hi - lo,),
            [self.ints, self.reals, local] + others + carried,
            [SMEM, SMEM, self.side(lo, 0)]
            + [self.side(0, 0)] * len(others)
            + [ANY] * len(carried),
            [self.side(lo, 1), STAMP],
            [shaped(*self.shape), shaped(8, 128)],
            alias={3 + len(others): 0} if carried else None,
        )


def spans(sizes, total):
    ends = np.cumsum(sizes)
    return [(int(end - size), int(end)) for size, end in zip(sizes, ends)]


def body(adjoint, source, viscosity, kappa, coupling, bc_flags, inst_map):
    slots = lax.axis_size("inst")
    sectors = lax.axis_size("space")
    center = adjoint[0]
    fields, block, cycles, cells = center.shape
    near = cycles // 2
    points = block * sectors
    quads = sectors // QUAD

    def to_partner(x, pick):
        pairs = []
        for i in range(slots):
            for p in range(sectors):
                pairs.append((i * sectors + p, pick(i, p % 2) * sectors + p))
        return lax.ppermute(x, ("inst", "space"), pairs)

    def to_first(x):
        return to_partner(x, lambda i, core: first_partner(i, core, slots))

    def to_later(x, s):
        return to_partner(x, lambda i, core: later_partner(i, core, slots, s))

    def to_sector(x, k):
        return lax.ppermute(x, "space", [(i, i ^ k) for i in range(sectors)])

    def ring(x, step):
        return lax.ppermute(x, "space", [(i, (i + step) % sectors) for i in range(sectors)])

    table, split, base, scale = mode_layout(points, near)
    table = table.reshape(table.shape[0], table.shape[1], quads, QUAD * block).transpose(2, 0, 1, 3)
    here = jnp.stack([lax.axis_index("inst"), lax.axis_index("space")])
    ints = jnp.concatenate([here, inst_map, jnp.asarray(split)])
    reals = jnp.asarray(np.concatenate([spectral_values(slots), base, scale]).astype(np.float32))
    plan = Plan(
        ints,
        reals,
        slots,
        center.shape,
        near,
        jnp.asarray(np.ascontiguousarray(table)),
        jnp.asarray(np.ascontiguousarray(table.transpose(0, 1, 3, 2))),
    )

    groups = [(lo, hi, 0) for lo, hi in spans(NEAR_SIZES, fields)]
    groups += [(lo, hi, 1) for lo, hi in spans(FAR_SIZES, fields)]
    first, others, parts, own, done = {}, {}, {}, {}, {}
    made, local, held, halos = {}, {}, None, None
    for step, g in ORDER:
        lo, hi, index = groups[g]
        token = [made[before] for before, after in EDGES if after == (step, g)]
        if step == "pack":
            packed = pack(center, viscosity, lo, hi, index, near, halos is None, token)
            made[step, g] = packed[0]
            first[g] = to_first(packed[0])
            if halos is None:
                halos = ring(packed[1], 1), ring(packed[2], -1)
        elif step == "local":
            local[g], made[step, g] = local_part(
                g, center, source[0], viscosity, kappa, coupling, bc_flags, *halos, token
            )
        elif step == "mix":
            mixed = plan.mix(center, first[g], lo, hi, index, token)
            made[step, g] = mixed[0]
            others[g] = [first[g]] + [to_later(x, s + 1) for s, x in enumerate(mixed)]
        elif step == "spread":
            mine, core, chip = plan.spread(local[0], others[g], lo, hi, token)
            made[step, g] = mine
            parts[g] = mine, to_sector(core, 1), chip
        elif step == "join":
            mine, core, chip = parts[g]
            made[step, g] = plan.join(chip, core, token)
            parts[g] = mine, core, to_sector(made[step, g], 2)
        elif step == "coef":
            part = made[step, g] = plan.coefficients(*parts[g], token)
            stride = QUAD
            while 2 * stride < sectors:
                part = part + to_sector(part, stride)
                stride = 2 * stride
            other = to_sector(part, stride) if stride < sectors else jnp.zeros_like(part)
            own[g] = part, other
        elif step == "filter":
            mine, core, chip = plan.filtered(*own[g], *parts[g], token)
            made[step, g] = mine
            done[g] = mine, core, to_sector(chip, 2)
        elif step == "back":
            mine, core, chip = done[g]
            made[step, g] = plan.join(core, chip, token)
            done[g] = mine, to_sector(made[step, g], 1), chip
        elif step == "near":
            held, made[step, g] = plan.place_near(*done[g], held, lo, hi, token)
        else:
            held, made[step, g] = plan.place_far(local[1], others[g], held, lo, hi, token)
    return held[None]


def solution(mesh):
    return jax.shard_map(
        body,
        mesh=mesh,
        in_specs=(
            P("inst", None, "space", None, None),
            P("inst", None, "space", None, None),
            P("space", None, None),
            P(),
            P(),
            P(),
            P(),
        ),
        out_specs=P("inst", None, "space", None, None),
        check_vma=False,
    )
```

```python
import functools

import jax
import jax.numpy as jnp
import numpy as np
from jax import lax
from jax.experimental import pallas as pl
from jax.experimental.pallas import tpu as pltpu
from jax.sharding import PartitionSpec as P

QUAD = 4
NEAR_SIZES = (2, 2, 1)
FAR_SIZES = (1, 2, 2)
ORDER = (
    ("pack", 0),
    ("pack", 3),
    ("pack", 1),
    ("pack", 4),
    ("local", 0),
    ("pack", 2),
    ("mix", 0),
    ("mix", 1),
    ("spread", 0),
    ("join", 0),
    ("spread", 1),
    ("pack", 5),
    ("mix", 2),
    ("coef", 0),
    ("join", 1),
    ("spread", 2),
    ("coef", 1),
    ("mix", 5),
    ("join", 2),
    ("filter", 0),
    ("mix", 3),
    ("local", 1),
    ("coef", 2),
    ("mix", 4),
    ("filter", 1),
    ("back", 0),
    ("filter", 2),
    ("far", 5),
    ("near", 0),
    ("back", 1),
    ("far", 3),
    ("far", 4),
    ("back", 2),
    ("near", 2),
    ("near", 1),
)
EDGES = tuple(zip(ORDER[:-1], ORDER[1:]))
SMEM = pl.BlockSpec(memory_space=pltpu.SMEM)
STAMP = pl.BlockSpec((8, 128), lambda i: (0, 0))
ANY = pl.BlockSpec(memory_space=pl.ANY)
COST = pl.CostEstimate(flops=0, bytes_accessed=0, transcendentals=0)
PARAMS = pltpu.CompilerParams(vmem_limit_bytes=24 * 1024 * 1024)


def spectral_values(slots):
    offset = np.arange(1 - slots, slots)
    safe = np.where(offset == 0, 1.0, np.sin(np.pi * offset / slots))
    return np.where(offset == 0, 0.0, 0.5 * (1.0 - 2.0 * (np.abs(offset) % 2)) / safe)


def mode_layout(points, near):
    half = points // 2
    pairs = near // 2
    theta = np.arange(points)
    bases, base, scale = [], np.zeros(near), np.zeros(near)
    for r in range(near):
        cutoff = max(4, points * (r + 1) // (2 * near))
        weight = max(1.0 - r / near, 0.0)
        kept = [m for m in range(half + 1) if m < cutoff]
        out = [m for m in range(half + 1) if m >= cutoff]
        count = [sum(1 if m in (0, half) else 2 for m in modes) for modes in (kept, out)]
        low = count[0] <= count[1]
        rows = []
        for m in kept if low else out:
            angle = 2.0 * np.pi * (m * theta % points) / points
            if m in (0, half):
                rows.append(np.cos(angle) / np.sqrt(points))
            else:
                rows.append(np.cos(angle) * np.sqrt(2.0 / points))
                rows.append(np.sin(angle) * np.sqrt(2.0 / points))
        bases.append(rows)
        base[r] = 1.0 - weight if low else 1.0
        scale[r] = weight if low else -weight
    depth = max(len(bases[p]) + len(bases[p + pairs]) for p in range(pairs))
    depth = -(-depth // 8) * 8
    table = np.zeros((pairs, depth, points), np.float32)
    split = np.zeros(pairs, np.int32)
    for p in range(pairs):
        rows = bases[p] + bases[p + pairs]
        table[p, : len(rows)] = np.stack(rows)
        split[p] = len(bases[p])
    return table, split, base, scale


class Scalars:
    def __init__(self, ints, reals, slots, near):
        self.ints, self.reals, self.slots, self.near = ints, reals, slots, near
        self.slot, self.place = ints[0], ints[1]
        self.rank = self.place % QUAD

    def weight(self, i, j):
        return self.reals[self.ints[2 + i] - self.ints[2 + j] + self.slots - 1]

    def split(self, pair):
        return self.ints[2 + self.slots + pair]

    def base(self, r):
        return self.reals[2 * self.slots - 1 + r]

    def scale(self, r):
        return self.reals[2 * self.slots - 1 + self.near + r]

    def first(self):
        return first_partner(self.slot, self.place % 2, self.slots)

    def target(self, s):
        return later_partner(self.slot, self.place % 2, self.slots, s)


def first_partner(slot, core, slots):
    if slots == 4:
        return slot ^ (2 - core)
    return slot ^ 1


def later_partner(slot, core, slots, s):
    if slots == 4:
        return slot ^ (1 + core)
    return (slot // 2 + s) % (slots // 2) * 2 + slot % 2


def call(kernel, name, token, grid, inputs, in_specs, out_specs, out_shape, scratch=(), alias=None):
    extra = [t for t in token or () if all(t is not x for x in inputs)]
    return pl.pallas_call(
        lambda *refs: kernel(*refs[: len(inputs)], *refs[len(inputs) + len(extra) :]),
        grid=grid,
        in_specs=list(in_specs) + [ANY] * len(extra),
        out_specs=out_specs,
        out_shape=out_shape,
        scratch_shapes=list(scratch),
        input_output_aliases=alias or {},
        compiler_params=PARAMS,
        cost_estimate=COST,
        name=name,
    )(*inputs, *extra)


def shaped(*shape):
    return jax.ShapeDtypeStruct(shape, jnp.float32)


def pack(center, viscosity, lo, hi, index, near, edges, token):
    fields, block, rows, cells = center.shape
    inputs, in_specs = [center], [pl.BlockSpec((1, block, near, cells), lambda i: (lo + i, 0, index, 0))]
    shapes = [shaped(hi - lo, block, near, cells)]
    out_specs = [pl.BlockSpec((1, block, near, cells), lambda i: (i, 0, 0, 0))]
    if edges:
        for start in (block - 1, 0):
            inputs += [center, viscosity]
            in_specs.append(pl.BlockSpec((fields, 1, rows, cells), lambda i, s=start: (0, s, 0, 0)))
            in_specs.append(pl.BlockSpec((1, rows, cells), lambda i, s=start: (s, 0, 0)))
            shapes.append(shaped(fields + 1, 1, rows, cells))
            out_specs.append(pl.BlockSpec((fields + 1, 1, rows, cells), lambda i: (0, 0, 0, 0)))

    def kernel(source, *refs):
        out, rest = refs[len(inputs) - 1], refs[len(inputs) :]
        out[...] = source[...]
        for e, edge in enumerate(rest):
            edge[:fields] = refs[2 * e][...]
            edge[fields] = refs[2 * e + 1][...]

    return call(kernel, "pack", token, (hi - lo,), inputs, in_specs, out_specs, shapes)


def local_kernel(
    far, coupling, kappa, flags, adj, before, after, next_to, src, mu, mu_before, mu_after, mu_next, low, high, out, stamp
):
    fields, planes, rows, cells = adj.shape
    step = pl.program_id(0)
    first = step == 0
    last = step == pl.num_programs(0) - 1
    row = lax.broadcasted_iota(jnp.int32, (rows, cells), 0)
    col = lax.broadcasted_iota(jnp.int32, (rows, cells), 1)
    ring = 0.5 / ((row + rows * far).astype(jnp.float32) + 1.0)
    stamp[...] = jnp.zeros_like(stamp)

    def pick(source, behind, ahead, f, k):
        if k < 0:
            return jnp.where(first, low[f, 0], behind)
        if k >= planes:
            return jnp.where(last, high[f, 0], ahead)
        return source

    def visc(k):
        return pick(mu[max(0, min(k, planes - 1))], mu_before[0], mu_after[0], fields, k)

    def cell(f, k):
        return pick(adj[f, max(0, min(k, planes - 1))], before[f, 0], after[f, 0], f, k)

    def outward(x, edge):
        moved = pltpu.roll(x, rows - 1, 0)
        return moved if far else jnp.where(row == rows - 1, edge[:1], moved)

    def inward(x, edge):
        moved = pltpu.roll(x, 1, 0)
        return jnp.where(row == 0, edge[-1:], moved) if far else moved

    walls = []
    for f in range(fields):
        opens = [(1 - flags[f, i]).astype(jnp.float32) for i in range(3)]
        wall = jnp.where(col == 0, opens[0], 0.0)
        wall = wall + jnp.where(col == cells - 1, opens[1], 0.0)
        walls.append(wall + jnp.where(row == rows - 1, opens[2], 0.0) if far else wall)

    for k in range(planes):
        m = visc(k)
        up = ring * (m + visc(k + 1))
        down = ring * (m + visc(k - 1))
        outer = 0.5 * (m + outward(m, mu_next[k]))
        inner = 0.5 * (m + inward(m, mu_next[k]))
        if far:
            outer = jnp.where(row < rows - 1, outer, 0.0)
        else:
            inner = jnp.where(row > 0, inner, 0.0)
        east = jnp.where(col < cells - 1, 0.5 * (m + pltpu.roll(m, cells - 1, 1)), 0.0)
        west = jnp.where(col > 0, 0.5 * (m + pltpu.roll(m, 1, 1)), 0.0)
        diag = up + down + outer + inner + east + west
        for f in range(fields):
            p = adj[f, k]
            flux = (diag + walls[f] * m) * p
            flux = flux - up * cell(f, k + 1) - down * cell(f, k - 1)
            flux = flux - outer * outward(p, next_to[f, k]) - inner * inward(p, next_to[f, k])
            flux = flux - east * pltpu.roll(p, cells - 1, 1) - west * pltpu.roll(p, 1, 1)
            total = src[f, k] + kappa[f] * flux
            for g in range(fields):
                total = total + coupling[g, f] * adj[g, k]
            out[f, k] = total


def local_part(far, center, source, viscosity, kappa, coupling, flags, low, high, token):
    fields, block, rows, cells = center.shape
    half = rows // 2
    planes = min(4, block)
    edge = half // 8 - 1 if far else half // 8

    def whole(width, index):
        return pl.BlockSpec((fields, width, half, cells), lambda i: (0, index(i), far, 0))

    def plane(width, index):
        return pl.BlockSpec((width, half, cells), lambda i: (index(i), far, 0))

    behind = lambda i: jnp.maximum(i * planes - 1, 0)
    ahead = lambda i: jnp.minimum(i * planes + planes, block - 1)
    here = lambda i: i
    halo = pl.BlockSpec((fields + 1, 1, half, cells), lambda i: (0, 0, far, 0))
    return call(
        functools.partial(local_kernel, far),
        "local_part",
        token,
        (block // planes,),
        [coupling, kappa, flags, center, center, center, center, source]
        + [viscosity, viscosity, viscosity, viscosity, low, high],
        [
            SMEM,
            SMEM,
            SMEM,
            whole(planes, here),
            whole(1, behind),
            whole(1, ahead),
            pl.BlockSpec((fields, planes, 8, cells), lambda i: (0, i, edge, 0)),
            whole(planes, here),
            plane(planes, here),
            plane(1, behind),
            plane(1, ahead),
            pl.BlockSpec((planes, 8, cells), lambda i: (i, edge, 0)),
            halo,
            halo,
        ],
        [pl.BlockSpec((fields, planes, half, cells), lambda i: (0, i, 0, 0)), STAMP],
        [shaped(fields, block, half, cells), shaped(8, 128)],
    )


def sums(scalars, local, others):
    total = local[0] + scalars.weight(scalars.first(), scalars.slot) * others[0][0]
    for part in others[1:]:
        total = total + part[0]
    return total


class Plan:
    def __init__(self, ints, reals, slots, shape, near, table, back):
        self.ints, self.reals, self.slots, self.near = ints, reals, slots, near
        self.shape, self.table, self.back = shape, table, back
        self.fields, self.block, self.rows, self.cells = shape
        self.pairs = near // 2
        self.owned = self.pairs // QUAD
        self.cycles = near // QUAD
        self.depth = table.shape[2]

    def scalars(self, ints, reals):
        return Scalars(ints, reals, self.slots, self.near)

    def side(self, first, index):
        return pl.BlockSpec((1, self.block, self.near, self.cells), lambda i: (first + i, 0, index, 0))

    def part(self):
        return pl.BlockSpec((1, self.cycles, self.block, self.cells), lambda i, *_: (i, 0, 0, 0))

    def parts(self, count, first=0):
        shape = (count, 1, self.cycles, self.block, self.cells)
        return pl.BlockSpec(shape, lambda i, *_: (first, i, 0, 0, 0))

    def quad_shapes(self, fields):
        one = (fields, self.cycles, self.block, self.cells)
        return [shaped(*one), shaped(2, *one), shaped(2, *one)]

    def mix(self, center, first, lo, hi, index, token):
        count = max(1, self.slots // 2 - 1)

        def kernel(ints, reals, own, got, *outs):
            scalars = self.scalars(ints, reals)
            for s in range(count):
                target = scalars.target(s + 1)
                outs[s][0] = (
                    scalars.weight(scalars.slot, target) * own[0]
                    + scalars.weight(scalars.first(), target) * got[0]
                )

        return call(
            kernel,
            "mix",
            token,
            (hi - lo,),
            [self.ints, self.reals, center, first],
            [SMEM, SMEM, self.side(lo, index), self.side(0, 0)],
            [self.side(0, 0)] * count,
            [shaped(hi - lo, self.block, self.near, self.cells)] * count,
        )

    def spread(self, local, others, lo, hi, token):
        def kernel(ints, reals, local, *refs):
            others, (mine, core, chip), (flat, stage) = refs[:-5], refs[-5:-2], refs[-2:]
            scalars = self.scalars(ints, reals)
            flat[...] = sums(scalars, local, others).reshape(flat.shape)
            for o in range(QUAD):
                for j in range(self.owned):
                    for a in range(2):
                        r = o * self.owned + j + a * self.pairs
                        stage[o, 2 * j + a] = flat[pl.ds(r, self.block, stride=self.near), :]
            mine[0] = stage[scalars.rank]
            core[0, 0] = stage[scalars.rank ^ 1]
            core[1, 0] = stage[scalars.rank ^ 3]
            chip[0, 0] = stage[scalars.rank ^ 2]

        return call(
            kernel,
            "spread",
            token,
            (hi - lo,),
            [self.ints, self.reals, local] + others,
            [SMEM, SMEM, self.side(lo, 0)] + [self.side(0, 0)] * len(others),
            [self.part(), self.parts(2), self.parts(1)],
            self.quad_shapes(hi - lo),
            [
                pltpu.VMEM((self.block * self.near, self.cells), jnp.float32),
                pltpu.VMEM((QUAD, self.cycles, self.block, self.cells), jnp.float32),
            ],
        )

    def join(self, held, new, token):
        def kernel(held, new, out):
            out[...] = new[...]

        return call(
            kernel,
            "join",
            token,
            (held.shape[1],),
            [held, new],
            [ANY, self.parts(1, 1)],
            self.parts(1, 1),
            shaped(*held.shape),
            alias={0: 0},
        )

    def own_rows(self, shape):
        return pl.BlockSpec(
            (1, self.owned) + shape, lambda i, ints: (ints[1] // QUAD, ints[1] % QUAD, 0, 0)
        )

    def table_call(self, kernel, name, fields, inputs, in_specs, out_specs, out_shape, scratch, token):
        extra = [t for t in token or () if all(t is not x for x in inputs)]
        count = len(inputs)
        return pl.pallas_call(
            lambda *refs: kernel(*refs[: count + 1], *refs[count + 1 + len(extra) :]),
            grid_spec=pltpu.PrefetchScalarGridSpec(
                num_scalar_prefetch=1,
                grid=(fields,),
                in_specs=in_specs + [ANY] * len(extra),
                out_specs=out_specs,
                scratch_shapes=scratch,
            ),
            out_shape=out_shape,
            compiler_params=PARAMS,
            cost_estimate=COST,
            name=name,
        )(self.ints, *inputs, *extra)

    def block4(self, *shape):
        return pl.BlockSpec((1,) + shape, lambda i, ints: (i, 0, 0, 0))

    def coefficients(self, mine, core, chip, token):
        fields = mine.shape[0]

        def kernel(ints, reals, table, mine, core, chip, out, column):
            scalars = self.scalars(ints, reals)
            row = lax.broadcasted_iota(jnp.int32, (self.depth, self.cells), 0)
            for k, part in enumerate((mine[0], core[0, 0], chip[0, 0], chip[1, 0])):
                column[:, scalars.rank ^ k] = part
            for j in range(self.owned):
                modes = [
                    jnp.dot(
                        table[0, j],
                        column[2 * j + a].reshape(QUAD * self.block, self.cells),
                        precision=lax.Precision.HIGHEST,
                        preferred_element_type=jnp.float32,
                    )
                    for a in range(2)
                ]
                split = scalars.split(scalars.rank * self.owned + j)
                out[0, j] = jnp.where(row < split, modes[0], modes[1])

        return self.table_call(
            kernel,
            "coefficients",
            fields,
            [self.reals, self.table, mine, core, chip],
            [SMEM, self.own_rows(self.table.shape[2:]), self.part(), self.parts(1), self.parts(2)],
            self.block4(self.owned, self.depth, self.cells),
            shaped(fields, self.owned, self.depth, self.cells),
            [pltpu.VMEM((self.cycles, QUAD, self.block, self.cells), jnp.float32)],
            token,
        )

    def filtered(self, own, other, mine, core, chip, token):
        fields = mine.shape[0]

        def kernel(ints, reals, back, own, other, mine, core, chip, *refs):
            (mine_out, core_out, chip_out), waves = refs[:3], refs[3]
            scalars = self.scalars(ints, reals)
            row = lax.broadcasted_iota(jnp.int32, (self.depth, self.cells), 0)
            source = (mine.at[0], core.at[0, 0], chip.at[0, 0], chip.at[1, 0])
            result = (mine_out.at[0], core_out.at[0, 0], chip_out.at[0, 0], chip_out.at[1, 0])
            for j in range(self.owned):
                pair = scalars.rank * self.owned + j
                total = own[0, j] + other[0, j]
                keep = row < scalars.split(pair)
                for a in range(2):
                    waves[2 * j + a] = jnp.dot(
                        back[0, j],
                        jnp.where(keep if a == 0 else jnp.logical_not(keep), total, 0.0),
                        precision=lax.Precision.HIGHEST,
                        preferred_element_type=jnp.float32,
                    ).reshape(QUAD, self.block, self.cells)
                    r = pair + a * self.pairs
                    for k in range(QUAD):
                        result[k][2 * j + a] = (
                            scalars.base(r) * source[k][2 * j + a]
                            + scalars.scale(r) * waves[2 * j + a, scalars.rank ^ k]
                        )

        modes = self.block4(self.owned, self.depth, self.cells)
        return self.table_call(
            kernel,
            "filtered",
            fields,
            [self.reals, self.back, own, other, mine, core, chip],
            [SMEM, self.own_rows(self.back.shape[2:]), modes, modes]
            + [self.part(), self.parts(1), self.parts(2)],
            [self.part(), self.parts(1), self.parts(2)],
            self.quad_shapes(fields),
            [pltpu.VMEM((self.cycles, QUAD, self.block, self.cells), jnp.float32)],
            token,
        )

    def place_near(self, mine, core, chip, held, lo, hi, token):
        carried = [] if held is None else [held]

        def kernel(ints, reals, mine, core, chip, *refs):
            out, stamp, stage = refs[-3:]
            stamp[...] = jnp.zeros_like(stamp)
            rank = self.scalars(ints, reals).rank
            for k, part in enumerate((mine[0], core[0, 0], chip[0, 0], core[1, 0])):
                stage[rank ^ k] = part
            for o in range(QUAD):
                for j in range(self.owned):
                    for a in range(2):
                        out[0, :, o * self.owned + j + a * self.pairs, :] = stage[o, 2 * j + a]

        return call(
            kernel,
            "place_near",
            token,
            (hi - lo,),
            [self.ints, self.reals, mine, core, chip] + carried,
            [SMEM, SMEM, self.part(), self.parts(2), self.parts(1)] + [ANY] * len(carried),
            [self.side(lo, 0), STAMP],
            [shaped(*self.shape), shaped(8, 128)],
            [pltpu.VMEM((QUAD, self.cycles, self.block, self.cells), jnp.float32)],
            alias={5: 0} if carried else None,
        )

    def place_far(self, local, others, held, lo, hi, token):
        def kernel(ints, reals, local, *refs):
            others, (out, stamp) = refs[: len(refs) - 2 - len(carried)], refs[-2:]
            stamp[...] = jnp.zeros_like(stamp)
            out[0] = sums(self.scalars(ints, reals), local, others)

        carried = [] if held is None else [held]
        return call(
            kernel,
            "place_far",
            token,
            (hi - lo,),
            [self.ints, self.reals, local] + others + carried,
            [SMEM, SMEM, self.side(lo, 0)]
            + [self.side(0, 0)] * len(others)
            + [ANY] * len(carried),
            [self.side(lo, 1), STAMP],
            [shaped(*self.shape), shaped(8, 128)],
            alias={3 + len(others): 0} if carried else None,
        )


def spans(sizes, total):
    ends = np.cumsum(sizes)
    return [(int(end - size), int(end)) for size, end in zip(sizes, ends)]


def body(adjoint, source, viscosity, kappa, coupling, bc_flags, inst_map):
    slots = lax.axis_size("inst")
    sectors = lax.axis_size("space")
    center = adjoint[0]
    fields, block, cycles, cells = center.shape
    near = cycles // 2
    points = block * sectors
    quads = sectors // QUAD

    def to_partner(x, pick):
        pairs = []
        for i in range(slots):
            for p in range(sectors):
                pairs.append((i * sectors + p, pick(i, p % 2) * sectors + p))
        return lax.ppermute(x, ("inst", "space"), pairs)

    def to_first(x):
        return to_partner(x, lambda i, core: first_partner(i, core, slots))

    def to_later(x, s):
        return to_partner(x, lambda i, core: later_partner(i, core, slots, s))

    def to_sector(x, k):
        return lax.ppermute(x, "space", [(i, i ^ k) for i in range(sectors)])

    def ring(x, step):
        return lax.ppermute(x, "space", [(i, (i + step) % sectors) for i in range(sectors)])

    table, split, base, scale = mode_layout(points, near)
    table = table.reshape(table.shape[0], table.shape[1], quads, QUAD * block).transpose(2, 0, 1, 3)
    here = jnp.stack([lax.axis_index("inst"), lax.axis_index("space")])
    ints = jnp.concatenate([here, inst_map, jnp.asarray(split)])
    reals = jnp.asarray(np.concatenate([spectral_values(slots), base, scale]).astype(np.float32))
    plan = Plan(
        ints,
        reals,
        slots,
        center.shape,
        near,
        jnp.asarray(np.ascontiguousarray(table)),
        jnp.asarray(np.ascontiguousarray(table.transpose(0, 1, 3, 2))),
    )

    groups = [(lo, hi, 0) for lo, hi in spans(NEAR_SIZES, fields)]
    groups += [(lo, hi, 1) for lo, hi in spans(FAR_SIZES, fields)]
    first, others, parts, own, done = {}, {}, {}, {}, {}
    made, local, held, halos = {}, {}, None, None
    for step, g in ORDER:
        lo, hi, index = groups[g]
        token = [made[before] for before, after in EDGES if after == (step, g)]
        if step == "pack":
            packed = pack(center, viscosity, lo, hi, index, near, halos is None, token)
            made[step, g] = packed[0]
            first[g] = to_first(packed[0])
            if halos is None:
                halos = ring(packed[1], 1), ring(packed[2], -1)
        elif step == "local":
            local[g], made[step, g] = local_part(
                g, center, source[0], viscosity, kappa, coupling, bc_flags, *halos, token
            )
        elif step == "mix":
            mixed = plan.mix(center, first[g], lo, hi, index, token)
            made[step, g] = mixed[0]
            others[g] = [first[g]] + [to_later(x, s + 1) for s, x in enumerate(mixed)]
        elif step == "spread":
            mine, core, chip = plan.spread(local[0], others[g], lo, hi, token)
            made[step, g] = mine
            parts[g] = mine, to_sector(core, 1), chip
        elif step == "join":
            mine, core, chip = parts[g]
            made[step, g] = plan.join(chip, core, token)
            parts[g] = mine, core, to_sector(made[step, g], 2)
        elif step == "coef":
            part = made[step, g] = plan.coefficients(*parts[g], token)
            stride = QUAD
            while 2 * stride < sectors:
                part = part + to_sector(part, stride)
                stride = 2 * stride
            other = to_sector(part, stride) if stride < sectors else jnp.zeros_like(part)
            own[g] = part, other
        elif step == "filter":
            mine, core, chip = plan.filtered(*own[g], *parts[g], token)
            made[step, g] = mine
            done[g] = mine, core, to_sector(chip, 2)
        elif step == "back":
            mine, core, chip = done[g]
            made[step, g] = plan.join(core, chip, token)
            done[g] = mine, to_sector(made[step, g], 1), chip
        elif step == "near":
            held, made[step, g] = plan.place_near(*done[g], held, lo, hi, token)
        else:
            held, made[step, g] = plan.place_far(local[1], others[g], held, lo, hi, token)
    return held[None]


def solution(mesh):
    return jax.shard_map(
        body,
        mesh=mesh,
        in_specs=(
            P("inst", None, "space", None, None),
            P("inst", None, "space", None, None),
            P("space", None, None),
            P(),
            P(),
            P(),
            P(),
        ),
        out_specs=P("inst", None, "space", None, None),
        check_vma=False,
    )
```

```python
import functools

import jax
import jax.numpy as jnp
import numpy as np
from jax import lax
from jax.experimental import pallas as pl
from jax.experimental.pallas import tpu as pltpu
from jax.sharding import PartitionSpec as P

QUAD = 4
NEAR_SIZES = (1, 2, 1, 1)
FAR_SIZES = (2, 2, 1)
ORDER = (
    ("pack", 0),
    ("pack", 1),
    ("mix", 0),
    ("pack", 3),
    ("local", 0),
    ("mix", 3),
    ("mix", 1),
    ("spread", 0),
    ("pack", 6),
    ("pack", 4),
    ("join", 0),
    ("spread", 3),
    ("pack", 5),
    ("join", 3),
    ("pack", 2),
    ("spread", 1),
    ("coef", 3),
    ("mix", 2),
    ("coef", 0),
    ("join", 1),
    ("filter", 3),
    ("spread", 2),
    ("mix", 4),
    ("mix", 6),
    ("coef", 1),
    ("join", 2),
    ("filter", 0),
    ("back", 3),
    ("coef", 2),
    ("mix", 5),
    ("local", 1),
    ("near", 3),
    ("filter", 1),
    ("far", 6),
    ("filter", 2),
    ("back", 0),
    ("near", 0),
    ("back", 1),
    ("far", 4),
    ("back", 2),
    ("far", 5),
    ("near", 2),
    ("near", 1),
)
EDGES = tuple(zip(ORDER[:-1], ORDER[1:]))
PACK = 60
LOCAL = 52
SMEM = pl.BlockSpec(memory_space=pltpu.SMEM)
ANY = pl.BlockSpec(memory_space=pl.ANY)
COST = pl.CostEstimate(flops=0, bytes_accessed=0, transcendentals=0)
MIB = 1024 * 1024


def spectral_values(slots):
    offset = np.arange(1 - slots, slots)
    safe = np.where(offset == 0, 1.0, np.sin(np.pi * offset / slots))
    return np.where(offset == 0, 0.0, 0.5 * (1.0 - 2.0 * (np.abs(offset) % 2)) / safe)


def mode_layout(points, near):
    half = points // 2
    pairs = near // 2
    theta = np.arange(points)
    bases, base, scale = [], np.zeros(near), np.zeros(near)
    for r in range(near):
        cutoff = max(4, points * (r + 1) // (2 * near))
        weight = max(1.0 - r / near, 0.0)
        kept = [m for m in range(half + 1) if m < cutoff]
        out = [m for m in range(half + 1) if m >= cutoff]
        count = [sum(1 if m in (0, half) else 2 for m in modes) for modes in (kept, out)]
        low = count[0] <= count[1]
        rows = []
        for m in kept if low else out:
            angle = 2.0 * np.pi * (m * theta % points) / points
            if m in (0, half):
                rows.append(np.cos(angle) / np.sqrt(points))
            else:
                rows.append(np.cos(angle) * np.sqrt(2.0 / points))
                rows.append(np.sin(angle) * np.sqrt(2.0 / points))
        bases.append(rows)
        base[r] = 1.0 - weight if low else 1.0
        scale[r] = weight if low else -weight
    depth = max(len(bases[p]) + len(bases[p + pairs]) for p in range(pairs))
    depth = -(-depth // 8) * 8
    table = np.zeros((pairs, depth, points), np.float32)
    split = np.zeros(pairs, np.int32)
    for p in range(pairs):
        rows = bases[p] + bases[p + pairs]
        table[p, : len(rows)] = np.stack(rows)
        split[p] = len(bases[p])
    return table, split, base, scale


class Scalars:
    def __init__(self, ints, reals, slots, near):
        self.ints, self.reals, self.slots, self.near = ints, reals, slots, near
        self.slot, self.place = ints[0], ints[1]
        self.rank = self.place % QUAD

    def weight(self, i, j):
        return self.reals[self.ints[2 + i] - self.ints[2 + j] + self.slots - 1]

    def split(self, pair):
        return self.ints[2 + self.slots + pair]

    def base(self, r):
        return self.reals[2 * self.slots - 1 + r]

    def scale(self, r):
        return self.reals[2 * self.slots - 1 + self.near + r]

    def first(self):
        return first_partner(self.slot, self.place % 2, self.slots)

    def target(self, s):
        return later_partner(self.slot, self.place % 2, self.slots, s)


def first_partner(slot, core, slots):
    if slots == 4:
        return slot ^ (2 - core)
    return slot ^ 1


def later_partner(slot, core, slots, s):
    if slots == 4:
        return slot ^ (1 + core)
    return (slot // 2 + s) % (slots // 2) * 2 + slot % 2


def stamped(kernel, inputs, extra, out_specs, out_shape):
    out_specs = out_specs if isinstance(out_specs, list) else [out_specs]
    out_shape = out_shape if isinstance(out_shape, list) else [out_shape]
    skip, end = inputs + extra, inputs + extra + len(out_shape)

    def body(*refs):
        refs[end][...] = jnp.zeros_like(refs[end])
        kernel(*refs[:inputs], *refs[skip:end], *refs[end + 1 :])

    stamp = pl.BlockSpec((8, 128), lambda i, *_: (0, 0))
    return body, out_specs + [stamp], out_shape + [shaped(8, 128)]


def call(kernel, name, token, grid, inputs, in_specs, out_specs, out_shape, scratch=(), alias=None, grant=24):
    extra = list(token)
    kernel, out_specs, out_shape = stamped(kernel, len(inputs), len(extra), out_specs, out_shape)
    return pl.pallas_call(
        kernel,
        grid=grid,
        in_specs=list(in_specs) + [ANY] * len(extra),
        out_specs=out_specs,
        out_shape=out_shape,
        scratch_shapes=list(scratch),
        input_output_aliases=alias or {},
        compiler_params=pltpu.CompilerParams(vmem_limit_bytes=grant * MIB),
        cost_estimate=COST,
        name=name,
    )(*inputs, *extra)


def shaped(*shape):
    return jax.ShapeDtypeStruct(shape, jnp.float32)


def pack(center, viscosity, lo, hi, index, near, edges, token, early):
    fields, block, rows, cells = center.shape
    inputs, in_specs = [center], [pl.BlockSpec((1, block, near, cells), lambda i: (lo + i, 0, index, 0))]
    shapes = [shaped(hi - lo, block, near, cells)]
    out_specs = [pl.BlockSpec((1, block, near, cells), lambda i: (i, 0, 0, 0))]
    if edges:
        for start in (block - 1, 0):
            inputs += [center, viscosity]
            in_specs.append(pl.BlockSpec((fields, 1, rows, cells), lambda i, s=start: (0, s, 0, 0)))
            in_specs.append(pl.BlockSpec((1, rows, cells), lambda i, s=start: (s, 0, 0)))
            shapes.append(shaped(fields + 1, 1, rows, cells))
            out_specs.append(pl.BlockSpec((fields + 1, 1, rows, cells), lambda i: (0, 0, 0, 0)))

    def kernel(source, *refs):
        out, rest = refs[len(inputs) - 1], refs[len(inputs) :]
        out[...] = source[...]
        for e, edge in enumerate(rest):
            edge[:fields] = refs[2 * e][...]
            edge[fields] = refs[2 * e + 1][...]

    return call(kernel, "pack", token, (hi - lo,), inputs, in_specs, out_specs, shapes, grant=PACK if early else 24)


def local_kernel(
    far, coupling, kappa, flags, adj, before, after, next_to, src, mu, mu_before, mu_after, mu_next, low, high, out
):
    fields, planes, rows, cells = adj.shape
    step = pl.program_id(0)
    first = step == 0
    last = step == pl.num_programs(0) - 1
    row = lax.broadcasted_iota(jnp.int32, (rows, cells), 0)
    col = lax.broadcasted_iota(jnp.int32, (rows, cells), 1)
    ring = 0.5 / ((row + rows * far).astype(jnp.float32) + 1.0)

    def pick(source, behind, ahead, f, k):
        if k < 0:
            return jnp.where(first, low[f, 0], behind)
        if k >= planes:
            return jnp.where(last, high[f, 0], ahead)
        return source

    def visc(k):
        return pick(mu[max(0, min(k, planes - 1))], mu_before[0], mu_after[0], fields, k)

    def cell(f, k):
        return pick(adj[f, max(0, min(k, planes - 1))], before[f, 0], after[f, 0], f, k)

    def outward(x, edge):
        moved = pltpu.roll(x, rows - 1, 0)
        return moved if far else jnp.where(row == rows - 1, edge[:1], moved)

    def inward(x, edge):
        moved = pltpu.roll(x, 1, 0)
        return jnp.where(row == 0, edge[-1:], moved) if far else moved

    walls = []
    for f in range(fields):
        opens = [(1 - flags[f, i]).astype(jnp.float32) for i in range(3)]
        wall = jnp.where(col == 0, opens[0], 0.0)
        wall = wall + jnp.where(col == cells - 1, opens[1], 0.0)
        walls.append(wall + jnp.where(row == rows - 1, opens[2], 0.0) if far else wall)

    for k in range(planes):
        m = visc(k)
        up = ring * (m + visc(k + 1))
        down = ring * (m + visc(k - 1))
        outer = 0.5 * (m + outward(m, mu_next[k]))
        inner = 0.5 * (m + inward(m, mu_next[k]))
        if far:
            outer = jnp.where(row < rows - 1, outer, 0.0)
        else:
            inner = jnp.where(row > 0, inner, 0.0)
        east = jnp.where(col < cells - 1, 0.5 * (m + pltpu.roll(m, cells - 1, 1)), 0.0)
        west = jnp.where(col > 0, 0.5 * (m + pltpu.roll(m, 1, 1)), 0.0)
        diag = up + down + outer + inner + east + west
        for f in range(fields):
            p = adj[f, k]
            flux = (diag + walls[f] * m) * p
            flux = flux - up * cell(f, k + 1) - down * cell(f, k - 1)
            flux = flux - outer * outward(p, next_to[f, k]) - inner * inward(p, next_to[f, k])
            flux = flux - east * pltpu.roll(p, cells - 1, 1) - west * pltpu.roll(p, 1, 1)
            total = src[f, k] + kappa[f] * flux
            for g in range(fields):
                total = total + coupling[g, f] * adj[g, k]
            out[f, k] = total


def local_part(far, center, source, viscosity, kappa, coupling, flags, low, high, token):
    fields, block, rows, cells = center.shape
    half = rows // 2
    planes = min(4, block)
    edge = half // 8 - 1 if far else half // 8

    def whole(width, index):
        return pl.BlockSpec((fields, width, half, cells), lambda i: (0, index(i), far, 0))

    def plane(width, index):
        return pl.BlockSpec((width, half, cells), lambda i: (index(i), far, 0))

    behind = lambda i: jnp.maximum(i * planes - 1, 0)
    ahead = lambda i: jnp.minimum(i * planes + planes, block - 1)
    here = lambda i: i
    halo = pl.BlockSpec((fields + 1, 1, half, cells), lambda i: (0, 0, far, 0))
    return call(
        functools.partial(local_kernel, far),
        "local_part",
        token,
        (block // planes,),
        [coupling, kappa, flags, center, center, center, center, source]
        + [viscosity, viscosity, viscosity, viscosity, low, high],
        [
            SMEM,
            SMEM,
            SMEM,
            whole(planes, here),
            whole(1, behind),
            whole(1, ahead),
            pl.BlockSpec((fields, planes, 8, cells), lambda i: (0, i, edge, 0)),
            whole(planes, here),
            plane(planes, here),
            plane(1, behind),
            plane(1, ahead),
            pl.BlockSpec((planes, 8, cells), lambda i: (i, edge, 0)),
            halo,
            halo,
        ],
        pl.BlockSpec((fields, planes, half, cells), lambda i: (0, i, 0, 0)),
        shaped(fields, block, half, cells),
        grant=24 if far else LOCAL,
    )


def sums(scalars, local, others):
    total = local[0] + scalars.weight(scalars.first(), scalars.slot) * others[0][0]
    for part in others[1:]:
        total = total + part[0]
    return total


class Plan:
    def __init__(self, ints, reals, slots, shape, near, table, back):
        self.ints, self.reals, self.slots, self.near = ints, reals, slots, near
        self.shape, self.table, self.back = shape, table, back
        self.fields, self.block, self.rows, self.cells = shape
        self.pairs = near // 2
        self.owned = self.pairs // QUAD
        self.cycles = near // QUAD
        self.depth = table.shape[2]

    def scalars(self, ints, reals):
        return Scalars(ints, reals, self.slots, self.near)

    def side(self, first, index):
        return pl.BlockSpec((1, self.block, self.near, self.cells), lambda i: (first + i, 0, index, 0))

    def part(self):
        return pl.BlockSpec((1, self.cycles, self.block, self.cells), lambda i, *_: (i, 0, 0, 0))

    def parts(self, count, first=0):
        shape = (count, 1, self.cycles, self.block, self.cells)
        return pl.BlockSpec(shape, lambda i, *_: (first, i, 0, 0, 0))

    def quad_shapes(self, fields):
        one = (fields, self.cycles, self.block, self.cells)
        return [shaped(*one), shaped(2, *one), shaped(2, *one)]

    def mix(self, center, first, lo, hi, index, token):
        count = max(1, self.slots // 2 - 1)

        def kernel(ints, reals, own, got, *outs):
            scalars = self.scalars(ints, reals)
            for s in range(count):
                target = scalars.target(s + 1)
                outs[s][0] = (
                    scalars.weight(scalars.slot, target) * own[0]
                    + scalars.weight(scalars.first(), target) * got[0]
                )

        return call(
            kernel,
            "mix",
            token,
            (hi - lo,),
            [self.ints, self.reals, center, first],
            [SMEM, SMEM, self.side(lo, index), self.side(0, 0)],
            [self.side(0, 0)] * count,
            [shaped(hi - lo, self.block, self.near, self.cells)] * count,
        )

    def spread(self, local, others, lo, hi, token):
        def kernel(ints, reals, local, *refs):
            others, (mine, core, chip), (flat, stage) = refs[:-5], refs[-5:-2], refs[-2:]
            scalars = self.scalars(ints, reals)
            flat[...] = sums(scalars, local, others).reshape(flat.shape)
            for o in range(QUAD):
                for j in range(self.owned):
                    for a in range(2):
                        r = o * self.owned + j + a * self.pairs
                        stage[o, 2 * j + a] = flat[pl.ds(r, self.block, stride=self.near), :]
            mine[0] = stage[scalars.rank]
            core[0, 0] = stage[scalars.rank ^ 1]
            core[1, 0] = stage[scalars.rank ^ 3]
            chip[0, 0] = stage[scalars.rank ^ 2]

        return call(
            kernel,
            "spread",
            token,
            (hi - lo,),
            [self.ints, self.reals, local] + others,
            [SMEM, SMEM, self.side(lo, 0)] + [self.side(0, 0)] * len(others),
            [self.part(), self.parts(2), self.parts(1)],
            self.quad_shapes(hi - lo),
            [
                pltpu.VMEM((self.block * self.near, self.cells), jnp.float32),
                pltpu.VMEM((QUAD, self.cycles, self.block, self.cells), jnp.float32),
            ],
        )

    def join(self, held, new, token):
        def kernel(held, new, out):
            out[...] = new[...]

        return call(
            kernel,
            "join",
            token,
            (held.shape[1],),
            [held, new],
            [ANY, self.parts(1, 1)],
            self.parts(1, 1),
            shaped(*held.shape),
            alias={0: 0},
        )

    def own_rows(self, shape):
        return pl.BlockSpec(
            (1, self.owned) + shape, lambda i, ints: (ints[1] // QUAD, ints[1] % QUAD, 0, 0)
        )

    def table_call(self, kernel, name, fields, inputs, in_specs, out_specs, out_shape, scratch, token):
        extra = list(token)
        kernel, out_specs, out_shape = stamped(kernel, 1 + len(inputs), len(extra), out_specs, out_shape)
        return pl.pallas_call(
            kernel,
            grid_spec=pltpu.PrefetchScalarGridSpec(
                num_scalar_prefetch=1,
                grid=(fields,),
                in_specs=in_specs + [ANY] * len(extra),
                out_specs=out_specs,
                scratch_shapes=scratch,
            ),
            out_shape=out_shape,
            compiler_params=pltpu.CompilerParams(vmem_limit_bytes=24 * MIB),
            cost_estimate=COST,
            name=name,
        )(self.ints, *inputs, *extra)

    def block4(self, *shape):
        return pl.BlockSpec((1,) + shape, lambda i, ints: (i, 0, 0, 0))

    def coefficients(self, mine, core, chip, token):
        fields = mine.shape[0]

        def kernel(ints, reals, table, mine, core, chip, out, column):
            scalars = self.scalars(ints, reals)
            row = lax.broadcasted_iota(jnp.int32, (self.depth, self.cells), 0)
            for k, part in enumerate((mine[0], core[0, 0], chip[0, 0], chip[1, 0])):
                column[:, scalars.rank ^ k] = part
            for j in range(self.owned):
                modes = [
                    jnp.dot(
                        table[0, j],
                        column[2 * j + a].reshape(QUAD * self.block, self.cells),
                        precision=lax.Precision.HIGHEST,
                        preferred_element_type=jnp.float32,
                    )
                    for a in range(2)
                ]
                split = scalars.split(scalars.rank * self.owned + j)
                out[0, j] = jnp.where(row < split, modes[0], modes[1])

        return self.table_call(
            kernel,
            "coefficients",
            fields,
            [self.reals, self.table, mine, core, chip],
            [SMEM, self.own_rows(self.table.shape[2:]), self.part(), self.parts(1), self.parts(2)],
            self.block4(self.owned, self.depth, self.cells),
            shaped(fields, self.owned, self.depth, self.cells),
            [pltpu.VMEM((self.cycles, QUAD, self.block, self.cells), jnp.float32)],
            token,
        )

    def filtered(self, own, other, mine, core, chip, token):
        fields = mine.shape[0]

        def kernel(ints, reals, back, own, other, mine, core, chip, *refs):
            (mine_out, core_out, chip_out), waves = refs[:3], refs[3]
            scalars = self.scalars(ints, reals)
            row = lax.broadcasted_iota(jnp.int32, (self.depth, self.cells), 0)
            source = (mine.at[0], core.at[0, 0], chip.at[0, 0], chip.at[1, 0])
            result = (mine_out.at[0], core_out.at[0, 0], chip_out.at[0, 0], chip_out.at[1, 0])
            for j in range(self.owned):
                pair = scalars.rank * self.owned + j
                total = own[0, j] + other[0, j]
                keep = row < scalars.split(pair)
                for a in range(2):
                    waves[2 * j + a] = jnp.dot(
                        back[0, j],
                        jnp.where(keep if a == 0 else jnp.logical_not(keep), total, 0.0),
                        precision=lax.Precision.HIGHEST,
                        preferred_element_type=jnp.float32,
                    ).reshape(QUAD, self.block, self.cells)
                    r = pair + a * self.pairs
                    for k in range(QUAD):
                        result[k][2 * j + a] = (
                            scalars.base(r) * source[k][2 * j + a]
                            + scalars.scale(r) * waves[2 * j + a, scalars.rank ^ k]
                        )

        modes = self.block4(self.owned, self.depth, self.cells)
        return self.table_call(
            kernel,
            "filtered",
            fields,
            [self.reals, self.back, own, other, mine, core, chip],
            [SMEM, self.own_rows(self.back.shape[2:]), modes, modes]
            + [self.part(), self.parts(1), self.parts(2)],
            [self.part(), self.parts(1), self.parts(2)],
            self.quad_shapes(fields),
            [pltpu.VMEM((self.cycles, QUAD, self.block, self.cells), jnp.float32)],
            token,
        )

    def place_near(self, mine, core, chip, held, lo, hi, token):
        carried = [] if held is None else [held]

        def kernel(ints, reals, mine, core, chip, *refs):
            out, stage = refs[-2:]
            rank = self.scalars(ints, reals).rank
            for k, part in enumerate((mine[0], core[0, 0], chip[0, 0], core[1, 0])):
                stage[rank ^ k] = part
            for o in range(QUAD):
                for j in range(self.owned):
                    for a in range(2):
                        out[0, :, o * self.owned + j + a * self.pairs, :] = stage[o, 2 * j + a]

        return call(
            kernel,
            "place_near",
            token,
            (hi - lo,),
            [self.ints, self.reals, mine, core, chip] + carried,
            [SMEM, SMEM, self.part(), self.parts(2), self.parts(1)] + [ANY] * len(carried),
            self.side(lo, 0),
            shaped(*self.shape),
            [pltpu.VMEM((QUAD, self.cycles, self.block, self.cells), jnp.float32)],
            alias={5: 0} if carried else None,
        )

    def place_far(self, local, others, held, lo, hi, token):
        def kernel(ints, reals, local, *refs):
            others, out = refs[: len(refs) - 1 - len(carried)], refs[-1]
            out[0] = sums(self.scalars(ints, reals), local, others)

        carried = [] if held is None else [held]
        return call(
            kernel,
            "place_far",
            token,
            (hi - lo,),
            [self.ints, self.reals, local] + others + carried,
            [SMEM, SMEM, self.side(lo, 0)]
            + [self.side(0, 0)] * len(others)
            + [ANY] * len(carried),
            self.side(lo, 1),
            shaped(*self.shape),
            alias={3 + len(others): 0} if carried else None,
        )


def spans(sizes, total):
    ends = np.cumsum(sizes)
    return [(int(end - size), int(end)) for size, end in zip(sizes, ends)]


def body(adjoint, source, viscosity, kappa, coupling, bc_flags, inst_map):
    slots = lax.axis_size("inst")
    sectors = lax.axis_size("space")
    center = adjoint[0]
    fields, block, cycles, cells = center.shape
    near = cycles // 2
    points = block * sectors
    quads = sectors // QUAD

    def to_partner(x, pick):
        pairs = []
        for i in range(slots):
            for p in range(sectors):
                pairs.append((i * sectors + p, pick(i, p % 2) * sectors + p))
        return lax.ppermute(x, ("inst", "space"), pairs)

    def to_first(x):
        return to_partner(x, lambda i, core: first_partner(i, core, slots))

    def to_later(x, s):
        return to_partner(x, lambda i, core: later_partner(i, core, slots, s))

    def to_sector(x, k):
        return lax.ppermute(x, "space", [(i, i ^ k) for i in range(sectors)])

    def ring(x, step):
        return lax.ppermute(x, "space", [(i, (i + step) % sectors) for i in range(sectors)])

    table, split, base, scale = mode_layout(points, near)
    table = table.reshape(table.shape[0], table.shape[1], quads, QUAD * block).transpose(2, 0, 1, 3)
    here = jnp.stack([lax.axis_index("inst"), lax.axis_index("space")])
    ints = jnp.concatenate([here, inst_map, jnp.asarray(split)])
    reals = jnp.asarray(np.concatenate([spectral_values(slots), base, scale]).astype(np.float32))
    plan = Plan(
        ints,
        reals,
        slots,
        center.shape,
        near,
        jnp.asarray(np.ascontiguousarray(table)),
        jnp.asarray(np.ascontiguousarray(table.transpose(0, 1, 3, 2))),
    )

    groups = [(lo, hi, 0) for lo, hi in spans(NEAR_SIZES, fields)]
    groups += [(lo, hi, 1) for lo, hi in spans(FAR_SIZES, fields)]
    first, others, parts, own, done = {}, {}, {}, {}, {}
    made, local, held, halos = {}, {}, None, None
    for step, g in ORDER:
        lo, hi, index = groups[g]
        token = [made[before] for before, after in EDGES if after == (step, g)]
        if step == "pack":
            early = 0 not in local
            *packed, stamp = pack(center, viscosity, lo, hi, index, near, halos is None, token, early)
            first[g] = to_first(packed[0])
            if halos is None:
                halos = ring(packed[1], 1), ring(packed[2], -1)
        elif step == "local":
            local[g], stamp = local_part(
                g, center, source[0], viscosity, kappa, coupling, bc_flags, *halos, token
            )
        elif step == "mix":
            *mixed, stamp = plan.mix(center, first[g], lo, hi, index, token)
            others[g] = [first[g]] + [to_later(x, s + 1) for s, x in enumerate(mixed)]
        elif step == "spread":
            mine, core, chip, stamp = plan.spread(local[0], others[g], lo, hi, token)
            parts[g] = mine, to_sector(core, 1), chip
        elif step == "join":
            mine, core, chip = parts[g]
            chip, stamp = plan.join(chip, core, token)
            parts[g] = mine, core, to_sector(chip, 2)
        elif step == "coef":
            part, stamp = plan.coefficients(*parts[g], token)
            stride = QUAD
            while 2 * stride < sectors:
                part = part + to_sector(part, stride)
                stride = 2 * stride
            other = to_sector(part, stride) if stride < sectors else jnp.zeros_like(part)
            own[g] = part, other
        elif step == "filter":
            mine, core, chip, stamp = plan.filtered(*own[g], *parts[g], token)
            done[g] = mine, core, to_sector(chip, 2)
        elif step == "back":
            mine, core, chip = done[g]
            core, stamp = plan.join(core, chip, token)
            done[g] = mine, to_sector(core, 1), chip
        elif step == "near":
            held, stamp = plan.place_near(*done[g], held, lo, hi, token)
        else:
            held, stamp = plan.place_far(local[1], others[g], held, lo, hi, token)
        made[step, g] = stamp
    return held[None]


def solution(mesh):
    return jax.shard_map(
        body,
        mesh=mesh,
        in_specs=(
            P("inst", None, "space", None, None),
            P("inst", None, "space", None, None),
            P("space", None, None),
            P(),
            P(),
            P(),
            P(),
        ),
        out_specs=P("inst", None, "space", None, None),
        check_vma=False,
    )
```

```python
import functools

import jax
import jax.numpy as jnp
import numpy as np
from jax import lax
from jax.experimental import pallas as pl
from jax.experimental.pallas import tpu as pltpu
from jax.sharding import PartitionSpec as P

QUAD = 4
NEAR_SIZES = (2, 2, 1)
FAR_SIZES = (1, 2, 2)
ORDER = (
    ("pack", 0),
    ("pack", 3),
    ("pack", 1),
    ("pack", 4),
    ("local", 0),
    ("pack", 2),
    ("mix", 0),
    ("mix", 1),
    ("spread", 0),
    ("join", 0),
    ("spread", 1),
    ("pack", 5),
    ("mix", 2),
    ("coef", 0),
    ("join", 1),
    ("spread", 2),
    ("coef", 1),
    ("mix", 5),
    ("join", 2),
    ("filter", 0),
    ("mix", 3),
    ("local", 1),
    ("coef", 2),
    ("mix", 4),
    ("filter", 1),
    ("back", 0),
    ("filter", 2),
    ("far", 5),
    ("near", 0),
    ("back", 1),
    ("far", 3),
    ("far", 4),
    ("back", 2),
    ("near", 2),
    ("near", 1),
)
EDGES = tuple(zip(ORDER[:-1], ORDER[1:]))
PACK = 60
LOCAL = 52
SMEM = pl.BlockSpec(memory_space=pltpu.SMEM)
ANY = pl.BlockSpec(memory_space=pl.ANY)
COST = pl.CostEstimate(flops=0, bytes_accessed=0, transcendentals=0)
MIB = 1024 * 1024


def spectral_values(slots):
    offset = np.arange(1 - slots, slots)
    safe = np.where(offset == 0, 1.0, np.sin(np.pi * offset / slots))
    return np.where(offset == 0, 0.0, 0.5 * (1.0 - 2.0 * (np.abs(offset) % 2)) / safe)


def mode_layout(points, near):
    half = points // 2
    pairs = near // 2
    theta = np.arange(points)
    bases, base, scale = [], np.zeros(near), np.zeros(near)
    for r in range(near):
        cutoff = max(4, points * (r + 1) // (2 * near))
        weight = max(1.0 - r / near, 0.0)
        kept = [m for m in range(half + 1) if m < cutoff]
        out = [m for m in range(half + 1) if m >= cutoff]
        count = [sum(1 if m in (0, half) else 2 for m in modes) for modes in (kept, out)]
        low = count[0] <= count[1]
        rows = []
        for m in kept if low else out:
            angle = 2.0 * np.pi * (m * theta % points) / points
            if m in (0, half):
                rows.append(np.cos(angle) / np.sqrt(points))
            else:
                rows.append(np.cos(angle) * np.sqrt(2.0 / points))
                rows.append(np.sin(angle) * np.sqrt(2.0 / points))
        bases.append(rows)
        base[r] = 1.0 - weight if low else 1.0
        scale[r] = weight if low else -weight
    depth = max(len(bases[p]) + len(bases[p + pairs]) for p in range(pairs))
    depth = -(-depth // 8) * 8
    table = np.zeros((pairs, depth, points), np.float32)
    split = np.zeros(pairs, np.int32)
    for p in range(pairs):
        rows = bases[p] + bases[p + pairs]
        table[p, : len(rows)] = np.stack(rows)
        split[p] = len(bases[p])
    return table, split, base, scale


class Scalars:
    def __init__(self, ints, reals, slots, near):
        self.ints, self.reals, self.slots, self.near = ints, reals, slots, near
        self.slot, self.place = ints[0], ints[1]
        self.rank = self.place % QUAD

    def weight(self, i, j):
        return self.reals[self.ints[2 + i] - self.ints[2 + j] + self.slots - 1]

    def split(self, pair):
        return self.ints[2 + self.slots + pair]

    def base(self, r):
        return self.reals[2 * self.slots - 1 + r]

    def scale(self, r):
        return self.reals[2 * self.slots - 1 + self.near + r]

    def first(self):
        return first_partner(self.slot, self.place % 2, self.slots)

    def target(self, s):
        return later_partner(self.slot, self.place % 2, self.slots, s)


def first_partner(slot, core, slots):
    if slots == 4:
        return slot ^ (2 - core)
    return slot ^ 1


def later_partner(slot, core, slots, s):
    if slots == 4:
        return slot ^ (1 + core)
    return (slot // 2 + s) % (slots // 2) * 2 + slot % 2


def stamped(kernel, inputs, extra, out_specs, out_shape):
    out_specs = out_specs if isinstance(out_specs, list) else [out_specs]
    out_shape = out_shape if isinstance(out_shape, list) else [out_shape]
    skip, end = inputs + extra, inputs + extra + len(out_shape)

    def body(*refs):
        refs[end][...] = jnp.zeros_like(refs[end])
        kernel(*refs[:inputs], *refs[skip:end], *refs[end + 1 :])

    stamp = pl.BlockSpec((8, 128), lambda i, *_: (0, 0))
    return body, out_specs + [stamp], out_shape + [shaped(8, 128)]


def call(kernel, name, token, grid, inputs, in_specs, out_specs, out_shape, scratch=(), alias=None, grant=24):
    extra = list(token)
    kernel, out_specs, out_shape = stamped(kernel, len(inputs), len(extra), out_specs, out_shape)
    return pl.pallas_call(
        kernel,
        grid=grid,
        in_specs=list(in_specs) + [ANY] * len(extra),
        out_specs=out_specs,
        out_shape=out_shape,
        scratch_shapes=list(scratch),
        input_output_aliases=alias or {},
        compiler_params=pltpu.CompilerParams(vmem_limit_bytes=grant * MIB),
        cost_estimate=COST,
        name=name,
    )(*inputs, *extra)


def shaped(*shape):
    return jax.ShapeDtypeStruct(shape, jnp.float32)


def pack(center, viscosity, lo, hi, index, near, edges, token, early):
    fields, block, rows, cells = center.shape
    inputs, in_specs = [center], [pl.BlockSpec((1, block, near, cells), lambda i: (lo + i, 0, index, 0))]
    shapes = [shaped(hi - lo, block, near, cells)]
    out_specs = [pl.BlockSpec((1, block, near, cells), lambda i: (i, 0, 0, 0))]
    if edges:
        for start in (block - 1, 0):
            inputs += [center, viscosity]
            in_specs.append(pl.BlockSpec((fields, 1, rows, cells), lambda i, s=start: (0, s, 0, 0)))
            in_specs.append(pl.BlockSpec((1, rows, cells), lambda i, s=start: (s, 0, 0)))
            shapes.append(shaped(fields + 1, 1, rows, cells))
            out_specs.append(pl.BlockSpec((fields + 1, 1, rows, cells), lambda i: (0, 0, 0, 0)))

    def kernel(source, *refs):
        out, rest = refs[len(inputs) - 1], refs[len(inputs) :]
        out[...] = source[...]
        for e, edge in enumerate(rest):
            edge[:fields] = refs[2 * e][...]
            edge[fields] = refs[2 * e + 1][...]

    return call(kernel, "pack", token, (hi - lo,), inputs, in_specs, out_specs, shapes, grant=PACK if early else 24)


def local_kernel(
    far, coupling, kappa, flags, adj, before, after, next_to, src, mu, mu_before, mu_after, mu_next, low, high, out
):
    fields, planes, rows, cells = adj.shape
    step = pl.program_id(0)
    first = step == 0
    last = step == pl.num_programs(0) - 1
    row = lax.broadcasted_iota(jnp.int32, (rows, cells), 0)
    col = lax.broadcasted_iota(jnp.int32, (rows, cells), 1)
    ring = 0.5 / ((row + rows * far).astype(jnp.float32) + 1.0)

    def pick(source, behind, ahead, f, k):
        if k < 0:
            return jnp.where(first, low[f, 0], behind)
        if k >= planes:
            return jnp.where(last, high[f, 0], ahead)
        return source

    def visc(k):
        return pick(mu[max(0, min(k, planes - 1))], mu_before[0], mu_after[0], fields, k)

    def cell(f, k):
        return pick(adj[f, max(0, min(k, planes - 1))], before[f, 0], after[f, 0], f, k)

    def outward(x, edge):
        moved = pltpu.roll(x, rows - 1, 0)
        return moved if far else jnp.where(row == rows - 1, edge[:1], moved)

    def inward(x, edge):
        moved = pltpu.roll(x, 1, 0)
        return jnp.where(row == 0, edge[-1:], moved) if far else moved

    walls = []
    for f in range(fields):
        opens = [(1 - flags[f, i]).astype(jnp.float32) for i in range(3)]
        wall = jnp.where(col == 0, opens[0], 0.0)
        wall = wall + jnp.where(col == cells - 1, opens[1], 0.0)
        walls.append(wall + jnp.where(row == rows - 1, opens[2], 0.0) if far else wall)

    for k in range(planes):
        m = visc(k)
        up = ring * (m + visc(k + 1))
        down = ring * (m + visc(k - 1))
        outer = 0.5 * (m + outward(m, mu_next[k]))
        inner = 0.5 * (m + inward(m, mu_next[k]))
        if far:
            outer = jnp.where(row < rows - 1, outer, 0.0)
        else:
            inner = jnp.where(row > 0, inner, 0.0)
        east = jnp.where(col < cells - 1, 0.5 * (m + pltpu.roll(m, cells - 1, 1)), 0.0)
        west = jnp.where(col > 0, 0.5 * (m + pltpu.roll(m, 1, 1)), 0.0)
        diag = up + down + outer + inner + east + west
        for f in range(fields):
            p = adj[f, k]
            flux = (diag + walls[f] * m) * p
            flux = flux - up * cell(f, k + 1) - down * cell(f, k - 1)
            flux = flux - outer * outward(p, next_to[f, k]) - inner * inward(p, next_to[f, k])
            flux = flux - east * pltpu.roll(p, cells - 1, 1) - west * pltpu.roll(p, 1, 1)
            total = src[f, k] + kappa[f] * flux
            for g in range(fields):
                total = total + coupling[g, f] * adj[g, k]
            out[f, k] = total


def local_part(far, center, source, viscosity, kappa, coupling, flags, low, high, token):
    fields, block, rows, cells = center.shape
    half = rows // 2
    planes = min(4, block)
    edge = half // 8 - 1 if far else half // 8

    def whole(width, index):
        return pl.BlockSpec((fields, width, half, cells), lambda i: (0, index(i), far, 0))

    def plane(width, index):
        return pl.BlockSpec((width, half, cells), lambda i: (index(i), far, 0))

    behind = lambda i: jnp.maximum(i * planes - 1, 0)
    ahead = lambda i: jnp.minimum(i * planes + planes, block - 1)
    here = lambda i: i
    halo = pl.BlockSpec((fields + 1, 1, half, cells), lambda i: (0, 0, far, 0))
    return call(
        functools.partial(local_kernel, far),
        "local_part",
        token,
        (block // planes,),
        [coupling, kappa, flags, center, center, center, center, source]
        + [viscosity, viscosity, viscosity, viscosity, low, high],
        [
            SMEM,
            SMEM,
            SMEM,
            whole(planes, here),
            whole(1, behind),
            whole(1, ahead),
            pl.BlockSpec((fields, planes, 8, cells), lambda i: (0, i, edge, 0)),
            whole(planes, here),
            plane(planes, here),
            plane(1, behind),
            plane(1, ahead),
            pl.BlockSpec((planes, 8, cells), lambda i: (i, edge, 0)),
            halo,
            halo,
        ],
        pl.BlockSpec((fields, planes, half, cells), lambda i: (0, i, 0, 0)),
        shaped(fields, block, half, cells),
        grant=24 if far else LOCAL,
    )


def sums(scalars, local, others):
    total = local[0] + scalars.weight(scalars.first(), scalars.slot) * others[0][0]
    for part in others[1:]:
        total = total + part[0]
    return total


class Plan:
    def __init__(self, ints, reals, slots, shape, near, table, back):
        self.ints, self.reals, self.slots, self.near = ints, reals, slots, near
        self.shape, self.table, self.back = shape, table, back
        self.fields, self.block, self.rows, self.cells = shape
        self.pairs = near // 2
        self.owned = self.pairs // QUAD
        self.cycles = near // QUAD
        self.depth = table.shape[2]

    def scalars(self, ints, reals):
        return Scalars(ints, reals, self.slots, self.near)

    def side(self, first, index):
        return pl.BlockSpec((1, self.block, self.near, self.cells), lambda i: (first + i, 0, index, 0))

    def part(self):
        return pl.BlockSpec((1, self.cycles, self.block, self.cells), lambda i, *_: (i, 0, 0, 0))

    def parts(self, count, first=0):
        shape = (count, 1, self.cycles, self.block, self.cells)
        return pl.BlockSpec(shape, lambda i, *_: (first, i, 0, 0, 0))

    def quad_shapes(self, fields):
        one = (fields, self.cycles, self.block, self.cells)
        return [shaped(*one), shaped(2, *one), shaped(2, *one)]

    def mix(self, center, first, lo, hi, index, token):
        count = max(1, self.slots // 2 - 1)

        def kernel(ints, reals, own, got, *outs):
            scalars = self.scalars(ints, reals)
            for s in range(count):
                target = scalars.target(s + 1)
                outs[s][0] = (
                    scalars.weight(scalars.slot, target) * own[0]
                    + scalars.weight(scalars.first(), target) * got[0]
                )

        return call(
            kernel,
            "mix",
            token,
            (hi - lo,),
            [self.ints, self.reals, center, first],
            [SMEM, SMEM, self.side(lo, index), self.side(0, 0)],
            [self.side(0, 0)] * count,
            [shaped(hi - lo, self.block, self.near, self.cells)] * count,
        )

    def spread(self, local, others, lo, hi, token):
        def kernel(ints, reals, local, *refs):
            others, (mine, core, chip), (flat, stage) = refs[:-5], refs[-5:-2], refs[-2:]
            scalars = self.scalars(ints, reals)
            flat[...] = sums(scalars, local, others).reshape(flat.shape)
            for o in range(QUAD):
                for j in range(self.owned):
                    for a in range(2):
                        r = o * self.owned + j + a * self.pairs
                        stage[o, 2 * j + a] = flat[pl.ds(r, self.block, stride=self.near), :]
            mine[0] = stage[scalars.rank]
            core[0, 0] = stage[scalars.rank ^ 1]
            core[1, 0] = stage[scalars.rank ^ 3]
            chip[0, 0] = stage[scalars.rank ^ 2]

        return call(
            kernel,
            "spread",
            token,
            (hi - lo,),
            [self.ints, self.reals, local] + others,
            [SMEM, SMEM, self.side(lo, 0)] + [self.side(0, 0)] * len(others),
            [self.part(), self.parts(2), self.parts(1)],
            self.quad_shapes(hi - lo),
            [
                pltpu.VMEM((self.block * self.near, self.cells), jnp.float32),
                pltpu.VMEM((QUAD, self.cycles, self.block, self.cells), jnp.float32),
            ],
        )

    def join(self, held, new, token):
        def kernel(held, new, out):
            out[...] = new[...]

        return call(
            kernel,
            "join",
            token,
            (held.shape[1],),
            [held, new],
            [ANY, self.parts(1, 1)],
            self.parts(1, 1),
            shaped(*held.shape),
            alias={0: 0},
        )

    def own_rows(self, shape):
        return pl.BlockSpec(
            (1, self.owned) + shape, lambda i, ints: (ints[1] // QUAD, ints[1] % QUAD, 0, 0)
        )

    def table_call(self, kernel, name, fields, inputs, in_specs, out_specs, out_shape, scratch, token):
        extra = list(token)
        kernel, out_specs, out_shape = stamped(kernel, 1 + len(inputs), len(extra), out_specs, out_shape)
        return pl.pallas_call(
            kernel,
            grid_spec=pltpu.PrefetchScalarGridSpec(
                num_scalar_prefetch=1,
                grid=(fields,),
                in_specs=in_specs + [ANY] * len(extra),
                out_specs=out_specs,
                scratch_shapes=scratch,
            ),
            out_shape=out_shape,
            compiler_params=pltpu.CompilerParams(vmem_limit_bytes=24 * MIB),
            cost_estimate=COST,
            name=name,
        )(self.ints, *inputs, *extra)

    def block4(self, *shape):
        return pl.BlockSpec((1,) + shape, lambda i, ints: (i, 0, 0, 0))

    def coefficients(self, mine, core, chip, token):
        fields = mine.shape[0]

        def kernel(ints, reals, table, mine, core, chip, out, column):
            scalars = self.scalars(ints, reals)
            row = lax.broadcasted_iota(jnp.int32, (self.depth, self.cells), 0)
            for k, part in enumerate((mine[0], core[0, 0], chip[0, 0], chip[1, 0])):
                column[:, scalars.rank ^ k] = part
            for j in range(self.owned):
                modes = [
                    jnp.dot(
                        table[0, j],
                        column[2 * j + a].reshape(QUAD * self.block, self.cells),
                        precision=lax.Precision.HIGHEST,
                        preferred_element_type=jnp.float32,
                    )
                    for a in range(2)
                ]
                split = scalars.split(scalars.rank * self.owned + j)
                out[0, j] = jnp.where(row < split, modes[0], modes[1])

        return self.table_call(
            kernel,
            "coefficients",
            fields,
            [self.reals, self.table, mine, core, chip],
            [SMEM, self.own_rows(self.table.shape[2:]), self.part(), self.parts(1), self.parts(2)],
            self.block4(self.owned, self.depth, self.cells),
            shaped(fields, self.owned, self.depth, self.cells),
            [pltpu.VMEM((self.cycles, QUAD, self.block, self.cells), jnp.float32)],
            token,
        )

    def filtered(self, own, other, mine, core, chip, token):
        fields = mine.shape[0]

        def kernel(ints, reals, back, own, other, mine, core, chip, *refs):
            (mine_out, core_out, chip_out), waves = refs[:3], refs[3]
            scalars = self.scalars(ints, reals)
            row = lax.broadcasted_iota(jnp.int32, (self.depth, self.cells), 0)
            source = (mine.at[0], core.at[0, 0], chip.at[0, 0], chip.at[1, 0])
            result = (mine_out.at[0], core_out.at[0, 0], chip_out.at[0, 0], chip_out.at[1, 0])
            for j in range(self.owned):
                pair = scalars.rank * self.owned + j
                total = own[0, j] + other[0, j]
                keep = row < scalars.split(pair)
                for a in range(2):
                    waves[2 * j + a] = jnp.dot(
                        back[0, j],
                        jnp.where(keep if a == 0 else jnp.logical_not(keep), total, 0.0),
                        precision=lax.Precision.HIGHEST,
                        preferred_element_type=jnp.float32,
                    ).reshape(QUAD, self.block, self.cells)
                    r = pair + a * self.pairs
                    for k in range(QUAD):
                        result[k][2 * j + a] = (
                            scalars.base(r) * source[k][2 * j + a]
                            + scalars.scale(r) * waves[2 * j + a, scalars.rank ^ k]
                        )

        modes = self.block4(self.owned, self.depth, self.cells)
        return self.table_call(
            kernel,
            "filtered",
            fields,
            [self.reals, self.back, own, other, mine, core, chip],
            [SMEM, self.own_rows(self.back.shape[2:]), modes, modes]
            + [self.part(), self.parts(1), self.parts(2)],
            [self.part(), self.parts(1), self.parts(2)],
            self.quad_shapes(fields),
            [pltpu.VMEM((self.cycles, QUAD, self.block, self.cells), jnp.float32)],
            token,
        )

    def place_near(self, mine, core, chip, held, lo, hi, token):
        carried = [] if held is None else [held]

        def kernel(ints, reals, mine, core, chip, *refs):
            out, stage = refs[-2:]
            rank = self.scalars(ints, reals).rank
            for k, part in enumerate((mine[0], core[0, 0], chip[0, 0], core[1, 0])):
                stage[rank ^ k] = part
            for o in range(QUAD):
                for j in range(self.owned):
                    for a in range(2):
                        out[0, :, o * self.owned + j + a * self.pairs, :] = stage[o, 2 * j + a]

        return call(
            kernel,
            "place_near",
            token,
            (hi - lo,),
            [self.ints, self.reals, mine, core, chip] + carried,
            [SMEM, SMEM, self.part(), self.parts(2), self.parts(1)] + [ANY] * len(carried),
            self.side(lo, 0),
            shaped(*self.shape),
            [pltpu.VMEM((QUAD, self.cycles, self.block, self.cells), jnp.float32)],
            alias={5: 0} if carried else None,
        )

    def place_far(self, local, others, held, lo, hi, token):
        def kernel(ints, reals, local, *refs):
            others, out = refs[: len(refs) - 1 - len(carried)], refs[-1]
            out[0] = sums(self.scalars(ints, reals), local, others)

        carried = [] if held is None else [held]
        return call(
            kernel,
            "place_far",
            token,
            (hi - lo,),
            [self.ints, self.reals, local] + others + carried,
            [SMEM, SMEM, self.side(lo, 0)]
            + [self.side(0, 0)] * len(others)
            + [ANY] * len(carried),
            self.side(lo, 1),
            shaped(*self.shape),
            alias={3 + len(others): 0} if carried else None,
        )


def spans(sizes, total):
    ends = np.cumsum(sizes)
    return [(int(end - size), int(end)) for size, end in zip(sizes, ends)]


def body(adjoint, source, viscosity, kappa, coupling, bc_flags, inst_map):
    slots = lax.axis_size("inst")
    sectors = lax.axis_size("space")
    center = adjoint[0]
    fields, block, cycles, cells = center.shape
    near = cycles // 2
    points = block * sectors
    quads = sectors // QUAD

    def to_partner(x, pick):
        pairs = []
        for i in range(slots):
            for p in range(sectors):
                pairs.append((i * sectors + p, pick(i, p % 2) * sectors + p))
        return lax.ppermute(x, ("inst", "space"), pairs)

    def to_first(x):
        return to_partner(x, lambda i, core: first_partner(i, core, slots))

    def to_later(x, s):
        return to_partner(x, lambda i, core: later_partner(i, core, slots, s))

    def to_sector(x, k):
        return lax.ppermute(x, "space", [(i, i ^ k) for i in range(sectors)])

    def ring(x, step):
        return lax.ppermute(x, "space", [(i, (i + step) % sectors) for i in range(sectors)])

    table, split, base, scale = mode_layout(points, near)
    table = table.reshape(table.shape[0], table.shape[1], quads, QUAD * block).transpose(2, 0, 1, 3)
    here = jnp.stack([lax.axis_index("inst"), lax.axis_index("space")])
    ints = jnp.concatenate([here, inst_map, jnp.asarray(split)])
    reals = jnp.asarray(np.concatenate([spectral_values(slots), base, scale]).astype(np.float32))
    plan = Plan(
        ints,
        reals,
        slots,
        center.shape,
        near,
        jnp.asarray(np.ascontiguousarray(table)),
        jnp.asarray(np.ascontiguousarray(table.transpose(0, 1, 3, 2))),
    )

    groups = [(lo, hi, 0) for lo, hi in spans(NEAR_SIZES, fields)]
    groups += [(lo, hi, 1) for lo, hi in spans(FAR_SIZES, fields)]
    first, others, parts, own, done = {}, {}, {}, {}, {}
    made, local, held, halos = {}, {}, None, None
    for step, g in ORDER:
        lo, hi, index = groups[g]
        token = [made[before] for before, after in EDGES if after == (step, g)]
        if step == "pack":
            early = 0 not in local
            *packed, stamp = pack(center, viscosity, lo, hi, index, near, halos is None, token, early)
            first[g] = to_first(packed[0])
            if halos is None:
                halos = ring(packed[1], 1), ring(packed[2], -1)
        elif step == "local":
            local[g], stamp = local_part(
                g, center, source[0], viscosity, kappa, coupling, bc_flags, *halos, token
            )
        elif step == "mix":
            *mixed, stamp = plan.mix(center, first[g], lo, hi, index, token)
            others[g] = [first[g]] + [to_later(x, s + 1) for s, x in enumerate(mixed)]
        elif step == "spread":
            mine, core, chip, stamp = plan.spread(local[0], others[g], lo, hi, token)
            parts[g] = mine, to_sector(core, 1), chip
        elif step == "join":
            mine, core, chip = parts[g]
            chip, stamp = plan.join(chip, core, token)
            parts[g] = mine, core, to_sector(chip, 2)
        elif step == "coef":
            part, stamp = plan.coefficients(*parts[g], token)
            stride = QUAD
            while 2 * stride < sectors:
                part = part + to_sector(part, stride)
                stride = 2 * stride
            other = to_sector(part, stride) if stride < sectors else jnp.zeros_like(part)
            own[g] = part, other
        elif step == "filter":
            mine, core, chip, stamp = plan.filtered(*own[g], *parts[g], token)
            done[g] = mine, core, to_sector(chip, 2)
        elif step == "back":
            mine, core, chip = done[g]
            core, stamp = plan.join(core, chip, token)
            done[g] = mine, to_sector(core, 1), chip
        elif step == "near":
            held, stamp = plan.place_near(*done[g], held, lo, hi, token)
        else:
            held, stamp = plan.place_far(local[1], others[g], held, lo, hi, token)
        made[step, g] = stamp
    return held[None]


def solution(mesh):
    return jax.shard_map(
        body,
        mesh=mesh,
        in_specs=(
            P("inst", None, "space", None, None),
            P("inst", None, "space", None, None),
            P("space", None, None),
            P(),
            P(),
            P(),
            P(),
        ),
        out_specs=P("inst", None, "space", None, None),
        check_vma=False,
    )
```

```python
import functools

import jax
import jax.numpy as jnp
import numpy as np
from jax import lax
from jax.experimental import pallas as pl
from jax.experimental.pallas import tpu as pltpu
from jax.sharding import PartitionSpec as P

QUAD = 4
NEAR_SIZES = (2, 2, 1)
FAR_SIZES = (2, 2, 1)
ORDER = (
    ("pack", 0),
    ("pack", 1),
    ("pack", 4),
    ("local", 0),
    ("mix", 0),
    ("local", 1),
    ("mix", 1),
    ("pack", 2),
    ("pack", 3),
    ("spread", 0),
    ("join", 0),
    ("spread", 1),
    ("mix", 2),
    ("coef", 0),
    ("join", 1),
    ("spread", 2),
    ("join", 2),
    ("pack", 5),
    ("mix", 4),
    ("coef", 1),
    ("filter", 0),
    ("mix", 3),
    ("coef", 2),
    ("mix", 5),
    ("filter", 1),
    ("filter", 2),
    ("back", 0),
    ("far", 4),
    ("back", 1),
    ("near", 0),
    ("far", 3),
    ("back", 2),
    ("far", 5),
    ("near", 2),
    ("near", 1),
)
EDGES = tuple(zip(ORDER[:-1], ORDER[1:]))
PACK = 60
LOCAL = 52
SMEM = pl.BlockSpec(memory_space=pltpu.SMEM)
ANY = pl.BlockSpec(memory_space=pl.ANY)
COST = pl.CostEstimate(flops=0, bytes_accessed=0, transcendentals=0)
MIB = 1024 * 1024


def spectral_values(slots):
    offset = np.arange(1 - slots, slots)
    safe = np.where(offset == 0, 1.0, np.sin(np.pi * offset / slots))
    return np.where(offset == 0, 0.0, 0.5 * (1.0 - 2.0 * (np.abs(offset) % 2)) / safe)


def mode_layout(points, near):
    half = points // 2
    pairs = near // 2
    theta = np.arange(points)
    bases, base, scale = [], np.zeros(near), np.zeros(near)
    for r in range(near):
        cutoff = max(4, points * (r + 1) // (2 * near))
        weight = max(1.0 - r / near, 0.0)
        kept = [m for m in range(half + 1) if m < cutoff]
        out = [m for m in range(half + 1) if m >= cutoff]
        count = [sum(1 if m in (0, half) else 2 for m in modes) for modes in (kept, out)]
        low = count[0] <= count[1]
        rows = []
        for m in kept if low else out:
            angle = 2.0 * np.pi * (m * theta % points) / points
            if m in (0, half):
                rows.append(np.cos(angle) / np.sqrt(points))
            else:
                rows.append(np.cos(angle) * np.sqrt(2.0 / points))
                rows.append(np.sin(angle) * np.sqrt(2.0 / points))
        bases.append(rows)
        base[r] = 1.0 - weight if low else 1.0
        scale[r] = weight if low else -weight
    depth = max(len(bases[p]) + len(bases[p + pairs]) for p in range(pairs))
    depth = -(-depth // 8) * 8
    table = np.zeros((pairs, depth, points), np.float32)
    split = np.zeros(pairs, np.int32)
    for p in range(pairs):
        rows = bases[p] + bases[p + pairs]
        table[p, : len(rows)] = np.stack(rows)
        split[p] = len(bases[p])
    return table, split, base, scale


class Scalars:
    def __init__(self, ints, reals, slots, near):
        self.ints, self.reals, self.slots, self.near = ints, reals, slots, near
        self.slot, self.place = ints[0], ints[1]
        self.rank = self.place % QUAD

    def weight(self, i, j):
        return self.reals[self.ints[2 + i] - self.ints[2 + j] + self.slots - 1]

    def split(self, pair):
        return self.ints[2 + self.slots + pair]

    def base(self, r):
        return self.reals[2 * self.slots - 1 + r]

    def scale(self, r):
        return self.reals[2 * self.slots - 1 + self.near + r]

    def first(self):
        return first_partner(self.slot, self.place % 2, self.slots)

    def target(self, s):
        return later_partner(self.slot, self.place % 2, self.slots, s)


def first_partner(slot, core, slots):
    if slots == 4:
        return slot ^ (2 - core)
    return slot ^ 1


def later_partner(slot, core, slots, s):
    if slots == 4:
        return slot ^ (1 + core)
    return (slot // 2 + s) % (slots // 2) * 2 + slot % 2


def stamped(kernel, inputs, extra, out_specs, out_shape):
    out_specs = out_specs if isinstance(out_specs, list) else [out_specs]
    out_shape = out_shape if isinstance(out_shape, list) else [out_shape]
    skip, end = inputs + extra, inputs + extra + len(out_shape)

    def body(*refs):
        refs[end][...] = jnp.zeros_like(refs[end])
        kernel(*refs[:inputs], *refs[skip:end], *refs[end + 1 :])

    stamp = pl.BlockSpec((8, 128), lambda i, *_: (0, 0))
    return body, out_specs + [stamp], out_shape + [shaped(8, 128)]


def call(kernel, name, token, grid, inputs, in_specs, out_specs, out_shape, scratch=(), alias=None, grant=24):
    extra = list(token)
    kernel, out_specs, out_shape = stamped(kernel, len(inputs), len(extra), out_specs, out_shape)
    return pl.pallas_call(
        kernel,
        grid=grid,
        in_specs=list(in_specs) + [ANY] * len(extra),
        out_specs=out_specs,
        out_shape=out_shape,
        scratch_shapes=list(scratch),
        input_output_aliases=alias or {},
        compiler_params=pltpu.CompilerParams(vmem_limit_bytes=grant * MIB),
        cost_estimate=COST,
        name=name,
    )(*inputs, *extra)


def shaped(*shape):
    return jax.ShapeDtypeStruct(shape, jnp.float32)


def pack(center, viscosity, lo, hi, index, near, edges, token, early):
    fields, block, rows, cells = center.shape
    inputs, in_specs = [center], [pl.BlockSpec((1, block, near, cells), lambda i: (lo + i, 0, index, 0))]
    shapes = [shaped(hi - lo, block, near, cells)]
    out_specs = [pl.BlockSpec((1, block, near, cells), lambda i: (i, 0, 0, 0))]
    if edges:
        for start in (block - 1, 0):
            inputs += [center, viscosity]
            in_specs.append(pl.BlockSpec((fields, 1, rows, cells), lambda i, s=start: (0, s, 0, 0)))
            in_specs.append(pl.BlockSpec((1, rows, cells), lambda i, s=start: (s, 0, 0)))
            shapes.append(shaped(fields + 1, 1, rows, cells))
            out_specs.append(pl.BlockSpec((fields + 1, 1, rows, cells), lambda i: (0, 0, 0, 0)))

    def kernel(source, *refs):
        out, rest = refs[len(inputs) - 1], refs[len(inputs) :]
        out[...] = source[...]
        for e, edge in enumerate(rest):
            edge[:fields] = refs[2 * e][...]
            edge[fields] = refs[2 * e + 1][...]

    return call(kernel, "pack", token, (hi - lo,), inputs, in_specs, out_specs, shapes, grant=PACK if early else 24)


def local_kernel(
    far, coupling, kappa, flags, adj, before, after, next_to, src, mu, mu_before, mu_after, mu_next, out
):
    fields, planes, rows, cells = adj.shape
    step = pl.program_id(0)
    first = step == 0
    last = step == pl.num_programs(0) - 1
    row = lax.broadcasted_iota(jnp.int32, (rows, cells), 0)
    col = lax.broadcasted_iota(jnp.int32, (rows, cells), 1)
    ring = 0.5 / ((row + rows * far).astype(jnp.float32) + 1.0)

    def visc(k):
        return mu_before[0] if k < 0 else mu_after[0] if k >= planes else mu[k]

    def cell(f, k):
        return before[f, 0] if k < 0 else after[f, 0] if k >= planes else adj[f, k]

    def outward(x, edge):
        moved = pltpu.roll(x, rows - 1, 0)
        return moved if far else jnp.where(row == rows - 1, edge[:1], moved)

    def inward(x, edge):
        moved = pltpu.roll(x, 1, 0)
        return jnp.where(row == 0, edge[-1:], moved) if far else moved

    walls = []
    for f in range(fields):
        opens = [(1 - flags[f, i]).astype(jnp.float32) for i in range(3)]
        wall = jnp.where(col == 0, opens[0], 0.0)
        wall = wall + jnp.where(col == cells - 1, opens[1], 0.0)
        walls.append(wall + jnp.where(row == rows - 1, opens[2], 0.0) if far else wall)

    for k in range(planes):
        m = visc(k)
        up = ring * (m + visc(k + 1))
        down = ring * (m + visc(k - 1))
        if k == planes - 1:
            up = jnp.where(last, 0.0, up)
        if k == 0:
            down = jnp.where(first, 0.0, down)
        outer = 0.5 * (m + outward(m, mu_next[k]))
        inner = 0.5 * (m + inward(m, mu_next[k]))
        if far:
            outer = jnp.where(row < rows - 1, outer, 0.0)
        else:
            inner = jnp.where(row > 0, inner, 0.0)
        east = jnp.where(col < cells - 1, 0.5 * (m + pltpu.roll(m, cells - 1, 1)), 0.0)
        west = jnp.where(col > 0, 0.5 * (m + pltpu.roll(m, 1, 1)), 0.0)
        diag = up + down + outer + inner + east + west
        for f in range(fields):
            p = adj[f, k]
            flux = (diag + walls[f] * m) * p
            flux = flux - up * cell(f, k + 1) - down * cell(f, k - 1)
            flux = flux - outer * outward(p, next_to[f, k]) - inner * inward(p, next_to[f, k])
            flux = flux - east * pltpu.roll(p, cells - 1, 1) - west * pltpu.roll(p, 1, 1)
            total = src[f, k] + kappa[f] * flux
            for g in range(fields):
                total = total + coupling[g, f] * adj[g, k]
            out[f, k] = total


def local_part(far, center, source, viscosity, kappa, coupling, flags, token):
    fields, block, rows, cells = center.shape
    half = rows // 2
    planes = min(4, block)
    edge = half // 8 - 1 if far else half // 8

    def whole(width, index):
        return pl.BlockSpec((fields, width, half, cells), lambda i: (0, index(i), far, 0))

    def plane(width, index):
        return pl.BlockSpec((width, half, cells), lambda i: (index(i), far, 0))

    behind = lambda i: jnp.maximum(i * planes - 1, 0)
    ahead = lambda i: jnp.minimum(i * planes + planes, block - 1)
    here = lambda i: i
    return call(
        functools.partial(local_kernel, far),
        "local_part",
        token,
        (block // planes,),
        [coupling, kappa, flags, center, center, center, center, source]
        + [viscosity] * 4,
        [
            SMEM,
            SMEM,
            SMEM,
            whole(planes, here),
            whole(1, behind),
            whole(1, ahead),
            pl.BlockSpec((fields, planes, 8, cells), lambda i: (0, i, edge, 0)),
            whole(planes, here),
            plane(planes, here),
            plane(1, behind),
            plane(1, ahead),
            pl.BlockSpec((planes, 8, cells), lambda i: (i, edge, 0)),
        ],
        pl.BlockSpec((fields, planes, half, cells), lambda i: (0, i, 0, 0)),
        shaped(fields, block, half, cells),
        grant=24 if far else LOCAL,
    )


def sums(scalars, local, others):
    total = local[0] + scalars.weight(scalars.first(), scalars.slot) * others[0][0]
    for part in others[1:]:
        total = total + part[0]
    return total


class Plan:
    def __init__(self, ints, reals, slots, shape, near, table, back):
        self.ints, self.reals, self.slots, self.near = ints, reals, slots, near
        self.shape, self.table, self.back = shape, table, back
        self.fields, self.block, self.rows, self.cells = shape
        self.pairs = near // 2
        self.owned = self.pairs // QUAD
        self.cycles = near // QUAD
        self.depth = table.shape[2]

    def scalars(self, ints, reals):
        return Scalars(ints, reals, self.slots, self.near)

    def side(self, first, index):
        return pl.BlockSpec((1, self.block, self.near, self.cells), lambda i: (first + i, 0, index, 0))

    def faces(self, lo, side):
        shape = (1, 1, self.near, self.cells)
        at = lambda f, k: pl.BlockSpec(shape, lambda i: (f(i), k, side, 0))
        field = lambda i: lo + i
        inputs, specs = [self.kappa], [SMEM]
        for k, halo in zip((0, self.block - 1), self.halos):
            inputs += [self.center, halo, self.viscosity[None], halo]
            specs += [at(field, k), at(field, 0), at(lambda i: 0, k), at(lambda i: self.fields, 0)]
        return inputs, specs

    def face_terms(self, refs, lo, side):
        kappa, rest = refs[0], refs[1:9]
        row = lax.broadcasted_iota(jnp.int32, (self.near, self.cells), 0) + side * self.near
        ring = 0.5 * kappa[lo + pl.program_id(0)] / (row.astype(jnp.float32) + 1.0)
        here, there, mu, mu_there = rest[:4]
        low = ring * (mu[0, 0] + mu_there[0, 0]) * (here[0, 0] - there[0, 0])
        here, there, mu, mu_there = rest[4:]
        return low, ring * (mu[0, 0] + mu_there[0, 0]) * (here[0, 0] - there[0, 0])

    def part(self):
        return pl.BlockSpec((1, self.cycles, self.block, self.cells), lambda i, *_: (i, 0, 0, 0))

    def parts(self, count, first=0):
        shape = (count, 1, self.cycles, self.block, self.cells)
        return pl.BlockSpec(shape, lambda i, *_: (first, i, 0, 0, 0))

    def quad_shapes(self, fields):
        one = (fields, self.cycles, self.block, self.cells)
        return [shaped(*one), shaped(2, *one), shaped(2, *one)]

    def mix(self, center, first, lo, hi, index, token):
        count = max(1, self.slots // 2 - 1)

        def kernel(ints, reals, own, got, *outs):
            scalars = self.scalars(ints, reals)
            for s in range(count):
                target = scalars.target(s + 1)
                outs[s][0] = (
                    scalars.weight(scalars.slot, target) * own[0]
                    + scalars.weight(scalars.first(), target) * got[0]
                )

        return call(
            kernel,
            "mix",
            token,
            (hi - lo,),
            [self.ints, self.reals, center, first],
            [SMEM, SMEM, self.side(lo, index), self.side(0, 0)],
            [self.side(0, 0)] * count,
            [shaped(hi - lo, self.block, self.near, self.cells)] * count,
        )

    def spread(self, local, others, lo, hi, token):
        faces, face_specs = self.faces(lo, 0)

        def kernel(ints, reals, local, *refs):
            others, (mine, core, chip), (flat, stage) = refs[9:-5], refs[-5:-2], refs[-2:]
            scalars = self.scalars(ints, reals)
            flat[...] = sums(scalars, local, others).reshape(flat.shape)
            low, high = self.face_terms(refs, lo, 0)
            flat[: self.near] += low
            flat[-self.near :] += high
            for o in range(QUAD):
                for j in range(self.owned):
                    for a in range(2):
                        r = o * self.owned + j + a * self.pairs
                        stage[o, 2 * j + a] = flat[pl.ds(r, self.block, stride=self.near), :]
            mine[0] = stage[scalars.rank]
            core[0, 0] = stage[scalars.rank ^ 1]
            core[1, 0] = stage[scalars.rank ^ 3]
            chip[0, 0] = stage[scalars.rank ^ 2]

        return call(
            kernel,
            "spread",
            token,
            (hi - lo,),
            [self.ints, self.reals, local] + faces + others,
            [SMEM, SMEM, self.side(lo, 0)] + face_specs + [self.side(0, 0)] * len(others),
            [self.part(), self.parts(2), self.parts(1)],
            self.quad_shapes(hi - lo),
            [
                pltpu.VMEM((self.block * self.near, self.cells), jnp.float32),
                pltpu.VMEM((QUAD, self.cycles, self.block, self.cells), jnp.float32),
            ],
        )

    def join(self, held, new, token):
        def kernel(held, new, out):
            out[...] = new[...]

        return call(
            kernel,
            "join",
            token,
            (held.shape[1],),
            [held, new],
            [ANY, self.parts(1, 1)],
            self.parts(1, 1),
            shaped(*held.shape),
            alias={0: 0},
        )

    def own_rows(self, shape):
        return pl.BlockSpec(
            (1, self.owned) + shape, lambda i, ints: (ints[1] // QUAD, ints[1] % QUAD, 0, 0)
        )

    def table_call(self, kernel, name, fields, inputs, in_specs, out_specs, out_shape, scratch, token):
        extra = list(token)
        kernel, out_specs, out_shape = stamped(kernel, 1 + len(inputs), len(extra), out_specs, out_shape)
        return pl.pallas_call(
            kernel,
            grid_spec=pltpu.PrefetchScalarGridSpec(
                num_scalar_prefetch=1,
                grid=(fields,),
                in_specs=in_specs + [ANY] * len(extra),
                out_specs=out_specs,
                scratch_shapes=scratch,
            ),
            out_shape=out_shape,
            compiler_params=pltpu.CompilerParams(vmem_limit_bytes=24 * MIB),
            cost_estimate=COST,
            name=name,
        )(self.ints, *inputs, *extra)

    def block4(self, *shape):
        return pl.BlockSpec((1,) + shape, lambda i, ints: (i, 0, 0, 0))

    def coefficients(self, mine, core, chip, token):
        fields = mine.shape[0]

        def kernel(ints, reals, table, mine, core, chip, out, column):
            scalars = self.scalars(ints, reals)
            row = lax.broadcasted_iota(jnp.int32, (self.depth, self.cells), 0)
            for k, part in enumerate((mine[0], core[0, 0], chip[0, 0], chip[1, 0])):
                column[:, scalars.rank ^ k] = part
            for j in range(self.owned):
                modes = [
                    jnp.dot(
                        table[0, j],
                        column[2 * j + a].reshape(QUAD * self.block, self.cells),
                        precision=lax.Precision.HIGHEST,
                        preferred_element_type=jnp.float32,
                    )
                    for a in range(2)
                ]
                split = scalars.split(scalars.rank * self.owned + j)
                out[0, j] = jnp.where(row < split, modes[0], modes[1])

        return self.table_call(
            kernel,
            "coefficients",
            fields,
            [self.reals, self.table, mine, core, chip],
            [SMEM, self.own_rows(self.table.shape[2:]), self.part(), self.parts(1), self.parts(2)],
            self.block4(self.owned, self.depth, self.cells),
            shaped(fields, self.owned, self.depth, self.cells),
            [pltpu.VMEM((self.cycles, QUAD, self.block, self.cells), jnp.float32)],
            token,
        )

    def filtered(self, own, other, mine, core, chip, token):
        fields = mine.shape[0]

        def kernel(ints, reals, back, own, other, mine, core, chip, *refs):
            (mine_out, core_out, chip_out), waves = refs[:3], refs[3]
            scalars = self.scalars(ints, reals)
            row = lax.broadcasted_iota(jnp.int32, (self.depth, self.cells), 0)
            source = (mine.at[0], core.at[0, 0], chip.at[0, 0], chip.at[1, 0])
            result = (mine_out.at[0], core_out.at[0, 0], chip_out.at[0, 0], chip_out.at[1, 0])
            for j in range(self.owned):
                pair = scalars.rank * self.owned + j
                total = own[0, j] + other[0, j]
                keep = row < scalars.split(pair)
                for a in range(2):
                    waves[2 * j + a] = jnp.dot(
                        back[0, j],
                        jnp.where(keep if a == 0 else jnp.logical_not(keep), total, 0.0),
                        precision=lax.Precision.HIGHEST,
                        preferred_element_type=jnp.float32,
                    ).reshape(QUAD, self.block, self.cells)
                    r = pair + a * self.pairs
                    for k in range(QUAD):
                        result[k][2 * j + a] = (
                            scalars.base(r) * source[k][2 * j + a]
                            + scalars.scale(r) * waves[2 * j + a, scalars.rank ^ k]
                        )

        modes = self.block4(self.owned, self.depth, self.cells)
        return self.table_call(
            kernel,
            "filtered",
            fields,
            [self.reals, self.back, own, other, mine, core, chip],
            [SMEM, self.own_rows(self.back.shape[2:]), modes, modes]
            + [self.part(), self.parts(1), self.parts(2)],
            [self.part(), self.parts(1), self.parts(2)],
            self.quad_shapes(fields),
            [pltpu.VMEM((self.cycles, QUAD, self.block, self.cells), jnp.float32)],
            token,
        )

    def place_near(self, mine, core, chip, held, lo, hi, token):
        carried = [] if held is None else [held]

        def kernel(ints, reals, mine, core, chip, *refs):
            out, stage = refs[-2:]
            rank = self.scalars(ints, reals).rank
            for k, part in enumerate((mine[0], core[0, 0], chip[0, 0], core[1, 0])):
                stage[rank ^ k] = part
            for o in range(QUAD):
                for j in range(self.owned):
                    for a in range(2):
                        out[0, :, o * self.owned + j + a * self.pairs, :] = stage[o, 2 * j + a]

        return call(
            kernel,
            "place_near",
            token,
            (hi - lo,),
            [self.ints, self.reals, mine, core, chip] + carried,
            [SMEM, SMEM, self.part(), self.parts(2), self.parts(1)] + [ANY] * len(carried),
            self.side(lo, 0),
            shaped(*self.shape),
            [pltpu.VMEM((QUAD, self.cycles, self.block, self.cells), jnp.float32)],
            alias={5: 0} if carried else None,
        )

    def place_far(self, local, others, held, lo, hi, token):
        carried = [] if held is None else [held]
        faces, face_specs = self.faces(lo, 1)

        def kernel(ints, reals, local, *refs):
            others, out = refs[9 : len(refs) - 1 - len(carried)], refs[-1]
            out[0] = sums(self.scalars(ints, reals), local, others)
            low, high = self.face_terms(refs, lo, 1)
            out[0, 0] += low
            out[0, self.block - 1] += high

        return call(
            kernel,
            "place_far",
            token,
            (hi - lo,),
            [self.ints, self.reals, local] + faces + others + carried,
            [SMEM, SMEM, self.side(lo, 0)]
            + face_specs
            + [self.side(0, 0)] * len(others)
            + [ANY] * len(carried),
            self.side(lo, 1),
            shaped(*self.shape),
            alias={3 + len(faces) + len(others): 0} if carried else None,
        )


def spans(sizes, total):
    ends = np.cumsum(sizes)
    return [(int(end - size), int(end)) for size, end in zip(sizes, ends)]


def body(adjoint, source, viscosity, kappa, coupling, bc_flags, inst_map):
    slots = lax.axis_size("inst")
    sectors = lax.axis_size("space")
    center = adjoint[0]
    fields, block, cycles, cells = center.shape
    near = cycles // 2
    points = block * sectors
    quads = sectors // QUAD

    def to_partner(x, pick):
        pairs = []
        for i in range(slots):
            for p in range(sectors):
                pairs.append((i * sectors + p, pick(i, p % 2) * sectors + p))
        return lax.ppermute(x, ("inst", "space"), pairs)

    def to_first(x):
        return to_partner(x, lambda i, core: first_partner(i, core, slots))

    def to_later(x, s):
        return to_partner(x, lambda i, core: later_partner(i, core, slots, s))

    def to_sector(x, k):
        return lax.ppermute(x, "space", [(i, i ^ k) for i in range(sectors)])

    def ring(x, step):
        return lax.ppermute(x, "space", [(i, (i + step) % sectors) for i in range(sectors)])

    table, split, base, scale = mode_layout(points, near)
    table = table.reshape(table.shape[0], table.shape[1], quads, QUAD * block).transpose(2, 0, 1, 3)
    here = jnp.stack([lax.axis_index("inst"), lax.axis_index("space")])
    ints = jnp.concatenate([here, inst_map, jnp.asarray(split)])
    reals = jnp.asarray(np.concatenate([spectral_values(slots), base, scale]).astype(np.float32))
    plan = Plan(
        ints,
        reals,
        slots,
        center.shape,
        near,
        jnp.asarray(np.ascontiguousarray(table)),
        jnp.asarray(np.ascontiguousarray(table.transpose(0, 1, 3, 2))),
    )

    groups = [(lo, hi, 0) for lo, hi in spans(NEAR_SIZES, fields)]
    groups += [(lo, hi, 1) for lo, hi in spans(FAR_SIZES, fields)]
    first, others, parts, own, done = {}, {}, {}, {}, {}
    made, local, held, halos = {}, {}, None, None
    for step, g in ORDER:
        lo, hi, index = groups[g]
        token = [made[before] for before, after in EDGES if after == (step, g)]
        if step == "pack":
            early = 0 not in local
            *packed, stamp = pack(center, viscosity, lo, hi, index, near, halos is None, token, early)
            first[g] = to_first(packed[0])
            if halos is None:
                halos = ring(packed[1], 1), ring(packed[2], -1)
                plan.halos, plan.center, plan.viscosity, plan.kappa = halos, center, viscosity, kappa
        elif step == "local":
            local[g], stamp = local_part(
                g, center, source[0], viscosity, kappa, coupling, bc_flags, token
            )
        elif step == "mix":
            *mixed, stamp = plan.mix(center, first[g], lo, hi, index, token)
            others[g] = [first[g]] + [to_later(x, s + 1) for s, x in enumerate(mixed)]
        elif step == "spread":
            mine, core, chip, stamp = plan.spread(local[0], others[g], lo, hi, token)
            parts[g] = mine, to_sector(core, 1), chip
        elif step == "join":
            mine, core, chip = parts[g]
            chip, stamp = plan.join(chip, core, token)
            parts[g] = mine, core, to_sector(chip, 2)
        elif step == "coef":
            part, stamp = plan.coefficients(*parts[g], token)
            stride = QUAD
            while 2 * stride < sectors:
                part = part + to_sector(part, stride)
                stride = 2 * stride
            other = to_sector(part, stride) if stride < sectors else jnp.zeros_like(part)
            own[g] = part, other
        elif step == "filter":
            mine, core, chip, stamp = plan.filtered(*own[g], *parts[g], token)
            done[g] = mine, core, to_sector(chip, 2)
        elif step == "back":
            mine, core, chip = done[g]
            core, stamp = plan.join(core, chip, token)
            done[g] = mine, to_sector(core, 1), chip
        elif step == "near":
            held, stamp = plan.place_near(*done[g], held, lo, hi, token)
        else:
            held, stamp = plan.place_far(local[1], others[g], held, lo, hi, token)
        made[step, g] = stamp
    return held[None]


def solution(mesh):
    return jax.shard_map(
        body,
        mesh=mesh,
        in_specs=(
            P("inst", None, "space", None, None),
            P("inst", None, "space", None, None),
            P("space", None, None),
            P(),
            P(),
            P(),
            P(),
        ),
        out_specs=P("inst", None, "space", None, None),
        check_vma=False,
    )
```

```python
import functools

import jax
import jax.numpy as jnp
import numpy as np
from jax import lax
from jax.experimental import pallas as pl
from jax.experimental.pallas import tpu as pltpu
from jax.sharding import PartitionSpec as P

QUAD = 4
NEAR_SIZES = (2, 2, 1)
FAR_SIZES = (2, 2, 1)
ORDER = (
    ("pack", 0),
    ("pack", 3),
    ("pack", 2),
    ("pack", 1),
    ("local", 1),
    ("mix", 0),
    ("local", 0),
    ("mix", 1),
    ("pack", 4),
    ("spread", 0),
    ("join", 0),
    ("spread", 1),
    ("mix", 2),
    ("coef", 0),
    ("join", 1),
    ("spread", 2),
    ("pack", 5),
    ("join", 2),
    ("mix", 4),
    ("coef", 1),
    ("filter", 0),
    ("mix", 3),
    ("coef", 2),
    ("mix", 5),
    ("filter", 1),
    ("filter", 2),
    ("back", 0),
    ("far", 4),
    ("back", 1),
    ("near", 0),
    ("far", 3),
    ("back", 2),
    ("far", 5),
    ("near", 2),
    ("near", 1),
)
EDGES = tuple(zip(ORDER[:-1], ORDER[1:]))
PACK = 60
LOCAL = 52
SMEM = pl.BlockSpec(memory_space=pltpu.SMEM)
ANY = pl.BlockSpec(memory_space=pl.ANY)
COST = pl.CostEstimate(flops=0, bytes_accessed=0, transcendentals=0)
MIB = 1024 * 1024


def spectral_values(slots):
    offset = np.arange(1 - slots, slots)
    safe = np.where(offset == 0, 1.0, np.sin(np.pi * offset / slots))
    return np.where(offset == 0, 0.0, 0.5 * (1.0 - 2.0 * (np.abs(offset) % 2)) / safe)


def mode_layout(points, near):
    half = points // 2
    pairs = near // 2
    theta = np.arange(points)
    bases, base, scale = [], np.zeros(near), np.zeros(near)
    for r in range(near):
        cutoff = max(4, points * (r + 1) // (2 * near))
        weight = max(1.0 - r / near, 0.0)
        kept = [m for m in range(half + 1) if m < cutoff]
        out = [m for m in range(half + 1) if m >= cutoff]
        count = [sum(1 if m in (0, half) else 2 for m in modes) for modes in (kept, out)]
        low = count[0] <= count[1]
        rows = []
        for m in kept if low else out:
            angle = 2.0 * np.pi * (m * theta % points) / points
            if m in (0, half):
                rows.append(np.cos(angle) / np.sqrt(points))
            else:
                rows.append(np.cos(angle) * np.sqrt(2.0 / points))
                rows.append(np.sin(angle) * np.sqrt(2.0 / points))
        bases.append(rows)
        base[r] = 1.0 - weight if low else 1.0
        scale[r] = weight if low else -weight
    depth = max(len(bases[p]) + len(bases[p + pairs]) for p in range(pairs))
    depth = -(-depth // 8) * 8
    table = np.zeros((pairs, depth, points), np.float32)
    split = np.zeros(pairs, np.int32)
    for p in range(pairs):
        rows = bases[p] + bases[p + pairs]
        table[p, : len(rows)] = np.stack(rows)
        split[p] = len(bases[p])
    return table, split, base, scale


class Scalars:
    def __init__(self, ints, reals, slots, near):
        self.ints, self.reals, self.slots, self.near = ints, reals, slots, near
        self.slot, self.place = ints[0], ints[1]
        self.rank = self.place % QUAD

    def weight(self, i, j):
        return self.reals[self.ints[2 + i] - self.ints[2 + j] + self.slots - 1]

    def split(self, pair):
        return self.ints[2 + self.slots + pair]

    def base(self, r):
        return self.reals[2 * self.slots - 1 + r]

    def scale(self, r):
        return self.reals[2 * self.slots - 1 + self.near + r]

    def first(self):
        return first_partner(self.slot, self.place % 2, self.slots)

    def target(self, s):
        return later_partner(self.slot, self.place % 2, self.slots, s)


def first_partner(slot, core, slots):
    if slots == 4:
        return slot ^ (2 - core)
    return slot ^ 1


def later_partner(slot, core, slots, s):
    if slots == 4:
        return slot ^ (1 + core)
    return (slot // 2 + s) % (slots // 2) * 2 + slot % 2


def stamped(kernel, inputs, extra, out_specs, out_shape):
    out_specs = out_specs if isinstance(out_specs, list) else [out_specs]
    out_shape = out_shape if isinstance(out_shape, list) else [out_shape]
    skip, end = inputs + extra, inputs + extra + len(out_shape)

    def body(*refs):
        refs[end][...] = jnp.zeros_like(refs[end])
        kernel(*refs[:inputs], *refs[skip:end], *refs[end + 1 :])

    stamp = pl.BlockSpec((8, 128), lambda i, *_: (0, 0))
    return body, out_specs + [stamp], out_shape + [shaped(8, 128)]


def call(kernel, name, token, grid, inputs, in_specs, out_specs, out_shape, scratch=(), alias=None, grant=24):
    extra = list(token)
    kernel, out_specs, out_shape = stamped(kernel, len(inputs), len(extra), out_specs, out_shape)
    return pl.pallas_call(
        kernel,
        grid=grid,
        in_specs=list(in_specs) + [ANY] * len(extra),
        out_specs=out_specs,
        out_shape=out_shape,
        scratch_shapes=list(scratch),
        input_output_aliases=alias or {},
        compiler_params=pltpu.CompilerParams(vmem_limit_bytes=grant * MIB),
        cost_estimate=COST,
        name=name,
    )(*inputs, *extra)


def shaped(*shape):
    return jax.ShapeDtypeStruct(shape, jnp.float32)


def pack(center, viscosity, lo, hi, index, near, edges, token, early):
    fields, block, rows, cells = center.shape
    inputs, in_specs = [center], [pl.BlockSpec((1, block, near, cells), lambda i: (lo + i, 0, index, 0))]
    shapes = [shaped(hi - lo, block, near, cells)]
    out_specs = [pl.BlockSpec((1, block, near, cells), lambda i: (i, 0, 0, 0))]
    if edges:
        for start in (block - 1, 0):
            inputs += [center, viscosity]
            in_specs.append(pl.BlockSpec((fields, 1, rows, cells), lambda i, s=start: (0, s, 0, 0)))
            in_specs.append(pl.BlockSpec((1, rows, cells), lambda i, s=start: (s, 0, 0)))
            shapes.append(shaped(fields + 1, 1, rows, cells))
            out_specs.append(pl.BlockSpec((fields + 1, 1, rows, cells), lambda i: (0, 0, 0, 0)))

    def kernel(source, *refs):
        out, rest = refs[len(inputs) - 1], refs[len(inputs) :]
        out[...] = source[...]
        for e, edge in enumerate(rest):
            edge[:fields] = refs[2 * e][...]
            edge[fields] = refs[2 * e + 1][...]

    return call(kernel, "pack", token, (hi - lo,), inputs, in_specs, out_specs, shapes, grant=PACK if early else 24)


def local_kernel(
    far, coupling, kappa, flags, adj, before, after, next_to, src, mu, mu_before, mu_after, mu_next, out
):
    fields, planes, rows, cells = adj.shape
    step = pl.program_id(0)
    first = step == 0
    last = step == pl.num_programs(0) - 1
    row = lax.broadcasted_iota(jnp.int32, (rows, cells), 0)
    col = lax.broadcasted_iota(jnp.int32, (rows, cells), 1)
    ring = 0.5 / ((row + rows * far).astype(jnp.float32) + 1.0)

    def visc(k):
        return mu_before[0] if k < 0 else mu_after[0] if k >= planes else mu[k]

    def cell(f, k):
        return before[f, 0] if k < 0 else after[f, 0] if k >= planes else adj[f, k]

    def outward(x, edge):
        moved = pltpu.roll(x, rows - 1, 0)
        return moved if far else jnp.where(row == rows - 1, edge[:1], moved)

    def inward(x, edge):
        moved = pltpu.roll(x, 1, 0)
        return jnp.where(row == 0, edge[-1:], moved) if far else moved

    walls = []
    for f in range(fields):
        opens = [(1 - flags[f, i]).astype(jnp.float32) for i in range(3)]
        wall = jnp.where(col == 0, opens[0], 0.0)
        wall = wall + jnp.where(col == cells - 1, opens[1], 0.0)
        walls.append(wall + jnp.where(row == rows - 1, opens[2], 0.0) if far else wall)

    for k in range(planes):
        m = visc(k)
        up = ring * (m + visc(k + 1))
        down = ring * (m + visc(k - 1))
        if k == planes - 1:
            up = jnp.where(last, 0.0, up)
        if k == 0:
            down = jnp.where(first, 0.0, down)
        outer = 0.5 * (m + outward(m, mu_next[k]))
        inner = 0.5 * (m + inward(m, mu_next[k]))
        if far:
            outer = jnp.where(row < rows - 1, outer, 0.0)
        else:
            inner = jnp.where(row > 0, inner, 0.0)
        east = jnp.where(col < cells - 1, 0.5 * (m + pltpu.roll(m, cells - 1, 1)), 0.0)
        west = jnp.where(col > 0, 0.5 * (m + pltpu.roll(m, 1, 1)), 0.0)
        diag = up + down + outer + inner + east + west
        for f in range(fields):
            p = adj[f, k]
            flux = (diag + walls[f] * m) * p
            flux = flux - up * cell(f, k + 1) - down * cell(f, k - 1)
            flux = flux - outer * outward(p, next_to[f, k]) - inner * inward(p, next_to[f, k])
            flux = flux - east * pltpu.roll(p, cells - 1, 1) - west * pltpu.roll(p, 1, 1)
            total = src[f, k] + kappa[f] * flux
            for g in range(fields):
                total = total + coupling[g, f] * adj[g, k]
            out[f, k] = total


def local_part(far, center, source, viscosity, kappa, coupling, flags, token):
    fields, block, rows, cells = center.shape
    half = rows // 2
    planes = min(4, block)
    edge = half // 8 - 1 if far else half // 8

    def whole(width, index):
        return pl.BlockSpec((fields, width, half, cells), lambda i: (0, index(i), far, 0))

    def plane(width, index):
        return pl.BlockSpec((width, half, cells), lambda i: (index(i), far, 0))

    behind = lambda i: jnp.maximum(i * planes - 1, 0)
    ahead = lambda i: jnp.minimum(i * planes + planes, block - 1)
    here = lambda i: i
    return call(
        functools.partial(local_kernel, far),
        "local_part",
        token,
        (block // planes,),
        [coupling, kappa, flags, center, center, center, center, source]
        + [viscosity] * 4,
        [
            SMEM,
            SMEM,
            SMEM,
            whole(planes, here),
            whole(1, behind),
            whole(1, ahead),
            pl.BlockSpec((fields, planes, 8, cells), lambda i: (0, i, edge, 0)),
            whole(planes, here),
            plane(planes, here),
            plane(1, behind),
            plane(1, ahead),
            pl.BlockSpec((planes, 8, cells), lambda i: (i, edge, 0)),
        ],
        pl.BlockSpec((fields, planes, half, cells), lambda i: (0, i, 0, 0)),
        shaped(fields, block, half, cells),
        grant=24 if far else LOCAL,
    )


def sums(scalars, local, others):
    total = local[0] + scalars.weight(scalars.first(), scalars.slot) * others[0][0]
    for part in others[1:]:
        total = total + part[0]
    return total


class Plan:
    def __init__(self, ints, reals, slots, shape, near, table, back):
        self.ints, self.reals, self.slots, self.near = ints, reals, slots, near
        self.shape, self.table, self.back = shape, table, back
        self.fields, self.block, self.rows, self.cells = shape
        self.pairs = near // 2
        self.owned = self.pairs // QUAD
        self.cycles = near // QUAD
        self.depth = table.shape[2]

    def scalars(self, ints, reals):
        return Scalars(ints, reals, self.slots, self.near)

    def side(self, first, index):
        return pl.BlockSpec((1, self.block, self.near, self.cells), lambda i: (first + i, 0, index, 0))

    def faces(self, lo, side):
        shape = (1, 1, self.near, self.cells)
        at = lambda f, k: pl.BlockSpec(shape, lambda i: (f(i), k, side, 0))
        field = lambda i: lo + i
        inputs, specs = [self.kappa], [SMEM]
        for k, halo in zip((0, self.block - 1), self.halos):
            inputs += [self.center, halo, self.viscosity[None], halo]
            specs += [at(field, k), at(field, 0), at(lambda i: 0, k), at(lambda i: self.fields, 0)]
        return inputs, specs

    def face_terms(self, refs, lo, side):
        kappa, rest = refs[0], refs[1:9]
        row = lax.broadcasted_iota(jnp.int32, (self.near, self.cells), 0) + side * self.near
        ring = 0.5 * kappa[lo + pl.program_id(0)] / (row.astype(jnp.float32) + 1.0)
        here, there, mu, mu_there = rest[:4]
        low = ring * (mu[0, 0] + mu_there[0, 0]) * (here[0, 0] - there[0, 0])
        here, there, mu, mu_there = rest[4:]
        return low, ring * (mu[0, 0] + mu_there[0, 0]) * (here[0, 0] - there[0, 0])

    def part(self):
        return pl.BlockSpec((1, self.cycles, self.block, self.cells), lambda i, *_: (i, 0, 0, 0))

    def parts(self, count, first=0):
        shape = (count, 1, self.cycles, self.block, self.cells)
        return pl.BlockSpec(shape, lambda i, *_: (first, i, 0, 0, 0))

    def quad_shapes(self, fields):
        one = (fields, self.cycles, self.block, self.cells)
        return [shaped(*one), shaped(2, *one), shaped(2, *one)]

    def mix(self, center, first, lo, hi, index, token):
        count = max(1, self.slots // 2 - 1)

        def kernel(ints, reals, own, got, *outs):
            scalars = self.scalars(ints, reals)
            for s in range(count):
                target = scalars.target(s + 1)
                outs[s][0] = (
                    scalars.weight(scalars.slot, target) * own[0]
                    + scalars.weight(scalars.first(), target) * got[0]
                )

        return call(
            kernel,
            "mix",
            token,
            (hi - lo,),
            [self.ints, self.reals, center, first],
            [SMEM, SMEM, self.side(lo, index), self.side(0, 0)],
            [self.side(0, 0)] * count,
            [shaped(hi - lo, self.block, self.near, self.cells)] * count,
        )

    def spread(self, local, others, lo, hi, token):
        faces, face_specs = self.faces(lo, 0)

        def kernel(ints, reals, local, *refs):
            others, (mine, core, chip), (flat, stage) = refs[9:-5], refs[-5:-2], refs[-2:]
            scalars = self.scalars(ints, reals)
            flat[...] = sums(scalars, local, others).reshape(flat.shape)
            low, high = self.face_terms(refs, lo, 0)
            flat[: self.near] += low
            flat[-self.near :] += high
            for o in range(QUAD):
                for j in range(self.owned):
                    for a in range(2):
                        r = o * self.owned + j + a * self.pairs
                        stage[o, 2 * j + a] = flat[pl.ds(r, self.block, stride=self.near), :]
            mine[0] = stage[scalars.rank]
            core[0, 0] = stage[scalars.rank ^ 1]
            core[1, 0] = stage[scalars.rank ^ 3]
            chip[0, 0] = stage[scalars.rank ^ 2]

        return call(
            kernel,
            "spread",
            token,
            (hi - lo,),
            [self.ints, self.reals, local] + faces + others,
            [SMEM, SMEM, self.side(lo, 0)] + face_specs + [self.side(0, 0)] * len(others),
            [self.part(), self.parts(2), self.parts(1)],
            self.quad_shapes(hi - lo),
            [
                pltpu.VMEM((self.block * self.near, self.cells), jnp.float32),
                pltpu.VMEM((QUAD, self.cycles, self.block, self.cells), jnp.float32),
            ],
        )

    def join(self, held, new, token):
        def kernel(held, new, out):
            out[...] = new[...]

        return call(
            kernel,
            "join",
            token,
            (held.shape[1],),
            [held, new],
            [ANY, self.parts(1, 1)],
            self.parts(1, 1),
            shaped(*held.shape),
            alias={0: 0},
        )

    def own_rows(self, shape):
        return pl.BlockSpec(
            (1, self.owned) + shape, lambda i, ints: (ints[1] // QUAD, ints[1] % QUAD, 0, 0)
        )

    def table_call(self, kernel, name, fields, inputs, in_specs, out_specs, out_shape, scratch, token):
        extra = list(token)
        kernel, out_specs, out_shape = stamped(kernel, 1 + len(inputs), len(extra), out_specs, out_shape)
        return pl.pallas_call(
            kernel,
            grid_spec=pltpu.PrefetchScalarGridSpec(
                num_scalar_prefetch=1,
                grid=(fields,),
                in_specs=in_specs + [ANY] * len(extra),
                out_specs=out_specs,
                scratch_shapes=scratch,
            ),
            out_shape=out_shape,
            compiler_params=pltpu.CompilerParams(vmem_limit_bytes=24 * MIB),
            cost_estimate=COST,
            name=name,
        )(self.ints, *inputs, *extra)

    def block4(self, *shape):
        return pl.BlockSpec((1,) + shape, lambda i, ints: (i, 0, 0, 0))

    def coefficients(self, mine, core, chip, token):
        fields = mine.shape[0]

        def kernel(ints, reals, table, mine, core, chip, out, column):
            scalars = self.scalars(ints, reals)
            row = lax.broadcasted_iota(jnp.int32, (self.depth, self.cells), 0)
            for k, part in enumerate((mine[0], core[0, 0], chip[0, 0], chip[1, 0])):
                column[:, scalars.rank ^ k] = part
            for j in range(self.owned):
                modes = [
                    jnp.dot(
                        table[0, j],
                        column[2 * j + a].reshape(QUAD * self.block, self.cells),
                        precision=lax.Precision.HIGHEST,
                        preferred_element_type=jnp.float32,
                    )
                    for a in range(2)
                ]
                split = scalars.split(scalars.rank * self.owned + j)
                out[0, j] = jnp.where(row < split, modes[0], modes[1])

        return self.table_call(
            kernel,
            "coefficients",
            fields,
            [self.reals, self.table, mine, core, chip],
            [SMEM, self.own_rows(self.table.shape[2:]), self.part(), self.parts(1), self.parts(2)],
            self.block4(self.owned, self.depth, self.cells),
            shaped(fields, self.owned, self.depth, self.cells),
            [pltpu.VMEM((self.cycles, QUAD, self.block, self.cells), jnp.float32)],
            token,
        )

    def filtered(self, own, other, mine, core, chip, token):
        fields = mine.shape[0]

        def kernel(ints, reals, back, own, other, mine, core, chip, *refs):
            (mine_out, core_out, chip_out), waves = refs[:3], refs[3]
            scalars = self.scalars(ints, reals)
            row = lax.broadcasted_iota(jnp.int32, (self.depth, self.cells), 0)
            source = (mine.at[0], core.at[0, 0], chip.at[0, 0], chip.at[1, 0])
            result = (mine_out.at[0], core_out.at[0, 0], chip_out.at[0, 0], chip_out.at[1, 0])
            for j in range(self.owned):
                pair = scalars.rank * self.owned + j
                total = own[0, j] + other[0, j]
                keep = row < scalars.split(pair)
                for a in range(2):
                    waves[2 * j + a] = jnp.dot(
                        back[0, j],
                        jnp.where(keep if a == 0 else jnp.logical_not(keep), total, 0.0),
                        precision=lax.Precision.HIGHEST,
                        preferred_element_type=jnp.float32,
                    ).reshape(QUAD, self.block, self.cells)
                    r = pair + a * self.pairs
                    for k in range(QUAD):
                        result[k][2 * j + a] = (
                            scalars.base(r) * source[k][2 * j + a]
                            + scalars.scale(r) * waves[2 * j + a, scalars.rank ^ k]
                        )

        modes = self.block4(self.owned, self.depth, self.cells)
        return self.table_call(
            kernel,
            "filtered",
            fields,
            [self.reals, self.back, own, other, mine, core, chip],
            [SMEM, self.own_rows(self.back.shape[2:]), modes, modes]
            + [self.part(), self.parts(1), self.parts(2)],
            [self.part(), self.parts(1), self.parts(2)],
            self.quad_shapes(fields),
            [pltpu.VMEM((self.cycles, QUAD, self.block, self.cells), jnp.float32)],
            token,
        )

    def place_near(self, mine, core, chip, held, lo, hi, token):
        carried = [] if held is None else [held]

        def kernel(ints, reals, mine, core, chip, *refs):
            out, stage = refs[-2:]
            rank = self.scalars(ints, reals).rank
            for k, part in enumerate((mine[0], core[0, 0], chip[0, 0], core[1, 0])):
                stage[rank ^ k] = part
            for o in range(QUAD):
                for j in range(self.owned):
                    for a in range(2):
                        out[0, :, o * self.owned + j + a * self.pairs, :] = stage[o, 2 * j + a]

        return call(
            kernel,
            "place_near",
            token,
            (hi - lo,),
            [self.ints, self.reals, mine, core, chip] + carried,
            [SMEM, SMEM, self.part(), self.parts(2), self.parts(1)] + [ANY] * len(carried),
            self.side(lo, 0),
            shaped(*self.shape),
            [pltpu.VMEM((QUAD, self.cycles, self.block, self.cells), jnp.float32)],
            alias={5: 0} if carried else None,
        )

    def place_far(self, local, others, held, lo, hi, token):
        carried = [] if held is None else [held]
        faces, face_specs = self.faces(lo, 1)

        def kernel(ints, reals, local, *refs):
            others, out = refs[9 : len(refs) - 1 - len(carried)], refs[-1]
            out[0] = sums(self.scalars(ints, reals), local, others)
            low, high = self.face_terms(refs, lo, 1)
            out[0, 0] += low
            out[0, self.block - 1] += high

        return call(
            kernel,
            "place_far",
            token,
            (hi - lo,),
            [self.ints, self.reals, local] + faces + others + carried,
            [SMEM, SMEM, self.side(lo, 0)]
            + face_specs
            + [self.side(0, 0)] * len(others)
            + [ANY] * len(carried),
            self.side(lo, 1),
            shaped(*self.shape),
            alias={3 + len(faces) + len(others): 0} if carried else None,
        )


def spans(sizes, total):
    ends = np.cumsum(sizes)
    return [(int(end - size), int(end)) for size, end in zip(sizes, ends)]


def body(adjoint, source, viscosity, kappa, coupling, bc_flags, inst_map):
    slots = lax.axis_size("inst")
    sectors = lax.axis_size("space")
    center = adjoint[0]
    fields, block, cycles, cells = center.shape
    near = cycles // 2
    points = block * sectors
    quads = sectors // QUAD

    def to_partner(x, pick):
        pairs = []
        for i in range(slots):
            for p in range(sectors):
                pairs.append((i * sectors + p, pick(i, p % 2) * sectors + p))
        return lax.ppermute(x, ("inst", "space"), pairs)

    def to_first(x):
        return to_partner(x, lambda i, core: first_partner(i, core, slots))

    def to_later(x, s):
        return to_partner(x, lambda i, core: later_partner(i, core, slots, s))

    def to_sector(x, k):
        return lax.ppermute(x, "space", [(i, i ^ k) for i in range(sectors)])

    def ring(x, step):
        return lax.ppermute(x, "space", [(i, (i + step) % sectors) for i in range(sectors)])

    table, split, base, scale = mode_layout(points, near)
    table = table.reshape(table.shape[0], table.shape[1], quads, QUAD * block).transpose(2, 0, 1, 3)
    here = jnp.stack([lax.axis_index("inst"), lax.axis_index("space")])
    ints = jnp.concatenate([here, inst_map, jnp.asarray(split)])
    reals = jnp.asarray(np.concatenate([spectral_values(slots), base, scale]).astype(np.float32))
    plan = Plan(
        ints,
        reals,
        slots,
        center.shape,
        near,
        jnp.asarray(np.ascontiguousarray(table)),
        jnp.asarray(np.ascontiguousarray(table.transpose(0, 1, 3, 2))),
    )

    groups = [(lo, hi, 0) for lo, hi in spans(NEAR_SIZES, fields)]
    groups += [(lo, hi, 1) for lo, hi in spans(FAR_SIZES, fields)]
    first, others, parts, own, done = {}, {}, {}, {}, {}
    made, local, held, halos = {}, {}, None, None
    for step, g in ORDER:
        lo, hi, index = groups[g]
        token = [made[before] for before, after in EDGES if after == (step, g)]
        if step == "pack":
            early = 0 not in local
            *packed, stamp = pack(center, viscosity, lo, hi, index, near, halos is None, token, early)
            first[g] = to_first(packed[0])
            if halos is None:
                halos = ring(packed[1], 1), ring(packed[2], -1)
                plan.halos, plan.center, plan.viscosity, plan.kappa = halos, center, viscosity, kappa
        elif step == "local":
            local[g], stamp = local_part(
                g, center, source[0], viscosity, kappa, coupling, bc_flags, token
            )
        elif step == "mix":
            *mixed, stamp = plan.mix(center, first[g], lo, hi, index, token)
            others[g] = [first[g]] + [to_later(x, s + 1) for s, x in enumerate(mixed)]
        elif step == "spread":
            mine, core, chip, stamp = plan.spread(local[0], others[g], lo, hi, token)
            parts[g] = mine, to_sector(core, 1), chip
        elif step == "join":
            mine, core, chip = parts[g]
            chip, stamp = plan.join(chip, core, token)
            parts[g] = mine, core, to_sector(chip, 2)
        elif step == "coef":
            part, stamp = plan.coefficients(*parts[g], token)
            stride = QUAD
            while 2 * stride < sectors:
                part = part + to_sector(part, stride)
                stride = 2 * stride
            other = to_sector(part, stride) if stride < sectors else jnp.zeros_like(part)
            own[g] = part, other
        elif step == "filter":
            mine, core, chip, stamp = plan.filtered(*own[g], *parts[g], token)
            done[g] = mine, core, to_sector(chip, 2)
        elif step == "back":
            mine, core, chip = done[g]
            core, stamp = plan.join(core, chip, token)
            done[g] = mine, to_sector(core, 1), chip
        elif step == "near":
            held, stamp = plan.place_near(*done[g], held, lo, hi, token)
        else:
            held, stamp = plan.place_far(local[1], others[g], held, lo, hi, token)
        made[step, g] = stamp
    return held[None]


def solution(mesh):
    return jax.shard_map(
        body,
        mesh=mesh,
        in_specs=(
            P("inst", None, "space", None, None),
            P("inst", None, "space", None, None),
            P("space", None, None),
            P(),
            P(),
            P(),
            P(),
        ),
        out_specs=P("inst", None, "space", None, None),
        check_vma=False,
    )
```

```python
import functools

import jax
import jax.numpy as jnp
import numpy as np
from jax import lax
from jax.experimental import pallas as pl
from jax.experimental.pallas import tpu as pltpu
from jax.sharding import PartitionSpec as P

QUAD = 4
NEAR_SIZES = (2, 2, 1)
FAR_SIZES = (2, 2, 1)
ORDER = (
    ("pack", 0),
    ("pack", 3),
    ("pack", 2),
    ("pack", 1),
    ("local", 1),
    ("mix", 0),
    ("local", 0),
    ("mix", 1),
    ("pack", 4),
    ("spread", 0),
    ("join", 0),
    ("spread", 1),
    ("mix", 2),
    ("coef", 0),
    ("join", 1),
    ("spread", 2),
    ("pack", 5),
    ("join", 2),
    ("mix", 4),
    ("coef", 1),
    ("filter", 0),
    ("mix", 3),
    ("coef", 2),
    ("mix", 5),
    ("filter", 1),
    ("filter", 2),
    ("back", 0),
    ("far", 4),
    ("back", 1),
    ("near", 0),
    ("far", 3),
    ("back", 2),
    ("far", 5),
    ("near", 2),
    ("near", 1),
)
EDGES = tuple(zip(ORDER[:-1], ORDER[1:]))
PACK = 60
LOCAL = 24
SMEM = pl.BlockSpec(memory_space=pltpu.SMEM)
ANY = pl.BlockSpec(memory_space=pl.ANY)
COST = pl.CostEstimate(flops=0, bytes_accessed=0, transcendentals=0)
MIB = 1024 * 1024


def spectral_values(slots):
    offset = np.arange(1 - slots, slots)
    safe = np.where(offset == 0, 1.0, np.sin(np.pi * offset / slots))
    return np.where(offset == 0, 0.0, 0.5 * (1.0 - 2.0 * (np.abs(offset) % 2)) / safe)


def mode_layout(points, near):
    half = points // 2
    pairs = near // 2
    theta = np.arange(points)
    bases, base, scale = [], np.zeros(near), np.zeros(near)
    for r in range(near):
        cutoff = max(4, points * (r + 1) // (2 * near))
        weight = max(1.0 - r / near, 0.0)
        kept = [m for m in range(half + 1) if m < cutoff]
        out = [m for m in range(half + 1) if m >= cutoff]
        count = [sum(1 if m in (0, half) else 2 for m in modes) for modes in (kept, out)]
        low = count[0] <= count[1]
        rows = []
        for m in kept if low else out:
            angle = 2.0 * np.pi * (m * theta % points) / points
            if m in (0, half):
                rows.append(np.cos(angle) / np.sqrt(points))
            else:
                rows.append(np.cos(angle) * np.sqrt(2.0 / points))
                rows.append(np.sin(angle) * np.sqrt(2.0 / points))
        bases.append(rows)
        base[r] = 1.0 - weight if low else 1.0
        scale[r] = weight if low else -weight
    depth = max(len(bases[p]) + len(bases[p + pairs]) for p in range(pairs))
    depth = -(-depth // 8) * 8
    table = np.zeros((pairs, depth, points), np.float32)
    split = np.zeros(pairs, np.int32)
    for p in range(pairs):
        rows = bases[p] + bases[p + pairs]
        table[p, : len(rows)] = np.stack(rows)
        split[p] = len(bases[p])
    return table, split, base, scale


class Scalars:
    def __init__(self, ints, reals, slots, near):
        self.ints, self.reals, self.slots, self.near = ints, reals, slots, near
        self.slot, self.place = ints[0], ints[1]
        self.rank = self.place % QUAD

    def weight(self, i, j):
        return self.reals[self.ints[2 + i] - self.ints[2 + j] + self.slots - 1]

    def split(self, pair):
        return self.ints[2 + self.slots + pair]

    def base(self, r):
        return self.reals[2 * self.slots - 1 + r]

    def scale(self, r):
        return self.reals[2 * self.slots - 1 + self.near + r]

    def first(self):
        return first_partner(self.slot, self.place % 2, self.slots)

    def target(self, s):
        return later_partner(self.slot, self.place % 2, self.slots, s)


def first_partner(slot, core, slots):
    if slots == 4:
        return slot ^ (2 - core)
    return slot ^ 1


def later_partner(slot, core, slots, s):
    if slots == 4:
        return slot ^ (1 + core)
    return (slot // 2 + s) % (slots // 2) * 2 + slot % 2


def stamped(kernel, inputs, extra, out_specs, out_shape):
    out_specs = out_specs if isinstance(out_specs, list) else [out_specs]
    out_shape = out_shape if isinstance(out_shape, list) else [out_shape]
    skip, end = inputs + extra, inputs + extra + len(out_shape)

    def body(*refs):
        refs[end][...] = jnp.zeros_like(refs[end])
        kernel(*refs[:inputs], *refs[skip:end], *refs[end + 1 :])

    stamp = pl.BlockSpec((8, 128), lambda i, *_: (0, 0))
    return body, out_specs + [stamp], out_shape + [shaped(8, 128)]


def call(kernel, name, token, grid, inputs, in_specs, out_specs, out_shape, scratch=(), alias=None, grant=24):
    extra = list(token)
    kernel, out_specs, out_shape = stamped(kernel, len(inputs), len(extra), out_specs, out_shape)
    return pl.pallas_call(
        kernel,
        grid=grid,
        in_specs=list(in_specs) + [ANY] * len(extra),
        out_specs=out_specs,
        out_shape=out_shape,
        scratch_shapes=list(scratch),
        input_output_aliases=alias or {},
        compiler_params=pltpu.CompilerParams(vmem_limit_bytes=grant * MIB),
        cost_estimate=COST,
        name=name,
    )(*inputs, *extra)


def shaped(*shape):
    return jax.ShapeDtypeStruct(shape, jnp.float32)


def pack(center, viscosity, lo, hi, index, near, edges, token, early):
    fields, block, rows, cells = center.shape
    inputs, in_specs = [center], [pl.BlockSpec((1, block, near, cells), lambda i: (lo + i, 0, index, 0))]
    shapes = [shaped(hi - lo, block, near, cells)]
    out_specs = [pl.BlockSpec((1, block, near, cells), lambda i: (i, 0, 0, 0))]
    if edges:
        for start in (block - 1, 0):
            inputs += [center, viscosity]
            in_specs.append(pl.BlockSpec((fields, 1, rows, cells), lambda i, s=start: (0, s, 0, 0)))
            in_specs.append(pl.BlockSpec((1, rows, cells), lambda i, s=start: (s, 0, 0)))
            shapes.append(shaped(fields + 1, 1, rows, cells))
            out_specs.append(pl.BlockSpec((fields + 1, 1, rows, cells), lambda i: (0, 0, 0, 0)))

    def kernel(source, *refs):
        out, rest = refs[len(inputs) - 1], refs[len(inputs) :]
        out[...] = source[...]
        for e, edge in enumerate(rest):
            edge[:fields] = refs[2 * e][...]
            edge[fields] = refs[2 * e + 1][...]

    return call(kernel, "pack", token, (hi - lo,), inputs, in_specs, out_specs, shapes, grant=PACK if early else 24)


def local_kernel(
    far, coupling, kappa, flags, adj, before, after, next_to, src, mu, mu_before, mu_after, mu_next, out
):
    fields, planes, rows, cells = adj.shape
    step = pl.program_id(0)
    first = step == 0
    last = step == pl.num_programs(0) - 1
    row = lax.broadcasted_iota(jnp.int32, (rows, cells), 0)
    col = lax.broadcasted_iota(jnp.int32, (rows, cells), 1)
    ring = 0.5 / ((row + rows * far).astype(jnp.float32) + 1.0)

    def visc(k):
        return mu_before[0] if k < 0 else mu_after[0] if k >= planes else mu[k]

    def cell(f, k):
        return before[f, 0] if k < 0 else after[f, 0] if k >= planes else adj[f, k]

    def outward(x, edge):
        moved = pltpu.roll(x, rows - 1, 0)
        return moved if far else jnp.where(row == rows - 1, edge[:1], moved)

    def inward(x, edge):
        moved = pltpu.roll(x, 1, 0)
        return jnp.where(row == 0, edge[-1:], moved) if far else moved

    walls = []
    for f in range(fields):
        opens = [(1 - flags[f, i]).astype(jnp.float32) for i in range(3)]
        wall = jnp.where(col == 0, opens[0], 0.0)
        wall = wall + jnp.where(col == cells - 1, opens[1], 0.0)
        walls.append(wall + jnp.where(row == rows - 1, opens[2], 0.0) if far else wall)

    for k in range(planes):
        m = visc(k)
        up = ring * (m + visc(k + 1))
        down = ring * (m + visc(k - 1))
        if k == planes - 1:
            up = jnp.where(last, 0.0, up)
        if k == 0:
            down = jnp.where(first, 0.0, down)
        outer = 0.5 * (m + outward(m, mu_next[k]))
        inner = 0.5 * (m + inward(m, mu_next[k]))
        if far:
            outer = jnp.where(row < rows - 1, outer, 0.0)
        else:
            inner = jnp.where(row > 0, inner, 0.0)
        east = jnp.where(col < cells - 1, 0.5 * (m + pltpu.roll(m, cells - 1, 1)), 0.0)
        west = jnp.where(col > 0, 0.5 * (m + pltpu.roll(m, 1, 1)), 0.0)
        diag = up + down + outer + inner + east + west
        for f in range(fields):
            p = adj[f, k]
            flux = (diag + walls[f] * m) * p
            flux = flux - up * cell(f, k + 1) - down * cell(f, k - 1)
            flux = flux - outer * outward(p, next_to[f, k]) - inner * inward(p, next_to[f, k])
            flux = flux - east * pltpu.roll(p, cells - 1, 1) - west * pltpu.roll(p, 1, 1)
            total = src[f, k] + kappa[f] * flux
            for g in range(fields):
                total = total + coupling[g, f] * adj[g, k]
            out[f, k] = total


def local_part(far, center, source, viscosity, kappa, coupling, flags, token):
    fields, block, rows, cells = center.shape
    half = rows // 2
    planes = min(4, block)
    edge = half // 8 - 1 if far else half // 8

    def whole(width, index):
        return pl.BlockSpec((fields, width, half, cells), lambda i: (0, index(i), far, 0))

    def plane(width, index):
        return pl.BlockSpec((width, half, cells), lambda i: (index(i), far, 0))

    behind = lambda i: jnp.maximum(i * planes - 1, 0)
    ahead = lambda i: jnp.minimum(i * planes + planes, block - 1)
    here = lambda i: i
    return call(
        functools.partial(local_kernel, far),
        "local_part",
        token,
        (block // planes,),
        [coupling, kappa, flags, center, center, center, center, source]
        + [viscosity] * 4,
        [
            SMEM,
            SMEM,
            SMEM,
            whole(planes, here),
            whole(1, behind),
            whole(1, ahead),
            pl.BlockSpec((fields, planes, 8, cells), lambda i: (0, i, edge, 0)),
            whole(planes, here),
            plane(planes, here),
            plane(1, behind),
            plane(1, ahead),
            pl.BlockSpec((planes, 8, cells), lambda i: (i, edge, 0)),
        ],
        pl.BlockSpec((fields, planes, half, cells), lambda i: (0, i, 0, 0)),
        shaped(fields, block, half, cells),
        grant=24 if far else LOCAL,
    )


def sums(scalars, local, others):
    total = local[0] + scalars.weight(scalars.first(), scalars.slot) * others[0][0]
    for part in others[1:]:
        total = total + part[0]
    return total


class Plan:
    def __init__(self, ints, reals, slots, shape, near, table, back):
        self.ints, self.reals, self.slots, self.near = ints, reals, slots, near
        self.shape, self.table, self.back = shape, table, back
        self.fields, self.block, self.rows, self.cells = shape
        self.pairs = near // 2
        self.owned = self.pairs // QUAD
        self.cycles = near // QUAD
        self.depth = table.shape[2]

    def scalars(self, ints, reals):
        return Scalars(ints, reals, self.slots, self.near)

    def side(self, first, index):
        return pl.BlockSpec((1, self.block, self.near, self.cells), lambda i: (first + i, 0, index, 0))

    def faces(self, lo, side):
        shape = (1, 1, self.near, self.cells)
        at = lambda f, k: pl.BlockSpec(shape, lambda i: (f(i), k, side, 0))
        field = lambda i: lo + i
        inputs, specs = [self.kappa], [SMEM]
        for k, halo in zip((0, self.block - 1), self.halos):
            inputs += [self.center, halo, self.viscosity[None], halo]
            specs += [at(field, k), at(field, 0), at(lambda i: 0, k), at(lambda i: self.fields, 0)]
        return inputs, specs

    def face_terms(self, refs, lo, side):
        kappa, rest = refs[0], refs[1:9]
        row = lax.broadcasted_iota(jnp.int32, (self.near, self.cells), 0) + side * self.near
        ring = 0.5 * kappa[lo + pl.program_id(0)] / (row.astype(jnp.float32) + 1.0)
        here, there, mu, mu_there = rest[:4]
        low = ring * (mu[0, 0] + mu_there[0, 0]) * (here[0, 0] - there[0, 0])
        here, there, mu, mu_there = rest[4:]
        return low, ring * (mu[0, 0] + mu_there[0, 0]) * (here[0, 0] - there[0, 0])

    def part(self):
        return pl.BlockSpec((1, self.cycles, self.block, self.cells), lambda i, *_: (i, 0, 0, 0))

    def parts(self, count, first=0):
        shape = (count, 1, self.cycles, self.block, self.cells)
        return pl.BlockSpec(shape, lambda i, *_: (first, i, 0, 0, 0))

    def quad_shapes(self, fields):
        one = (fields, self.cycles, self.block, self.cells)
        return [shaped(*one), shaped(2, *one), shaped(2, *one)]

    def mix(self, center, first, lo, hi, index, token):
        count = max(1, self.slots // 2 - 1)

        def kernel(ints, reals, own, got, *outs):
            scalars = self.scalars(ints, reals)
            for s in range(count):
                target = scalars.target(s + 1)
                outs[s][0] = (
                    scalars.weight(scalars.slot, target) * own[0]
                    + scalars.weight(scalars.first(), target) * got[0]
                )

        return call(
            kernel,
            "mix",
            token,
            (hi - lo,),
            [self.ints, self.reals, center, first],
            [SMEM, SMEM, self.side(lo, index), self.side(0, 0)],
            [self.side(0, 0)] * count,
            [shaped(hi - lo, self.block, self.near, self.cells)] * count,
        )

    def spread(self, local, others, lo, hi, token):
        faces, face_specs = self.faces(lo, 0)

        def kernel(ints, reals, local, *refs):
            others, (mine, core, chip), (flat, stage) = refs[9:-5], refs[-5:-2], refs[-2:]
            scalars = self.scalars(ints, reals)
            flat[...] = sums(scalars, local, others).reshape(flat.shape)
            low, high = self.face_terms(refs, lo, 0)
            flat[: self.near] += low
            flat[-self.near :] += high
            for o in range(QUAD):
                for j in range(self.owned):
                    for a in range(2):
                        r = o * self.owned + j + a * self.pairs
                        stage[o, 2 * j + a] = flat[pl.ds(r, self.block, stride=self.near), :]
            mine[0] = stage[scalars.rank]
            core[0, 0] = stage[scalars.rank ^ 1]
            core[1, 0] = stage[scalars.rank ^ 3]
            chip[0, 0] = stage[scalars.rank ^ 2]

        return call(
            kernel,
            "spread",
            token,
            (hi - lo,),
            [self.ints, self.reals, local] + faces + others,
            [SMEM, SMEM, self.side(lo, 0)] + face_specs + [self.side(0, 0)] * len(others),
            [self.part(), self.parts(2), self.parts(1)],
            self.quad_shapes(hi - lo),
            [
                pltpu.VMEM((self.block * self.near, self.cells), jnp.float32),
                pltpu.VMEM((QUAD, self.cycles, self.block, self.cells), jnp.float32),
            ],
        )

    def join(self, held, new, token):
        def kernel(held, new, out):
            out[...] = new[...]

        return call(
            kernel,
            "join",
            token,
            (held.shape[1],),
            [held, new],
            [ANY, self.parts(1, 1)],
            self.parts(1, 1),
            shaped(*held.shape),
            alias={0: 0},
        )

    def own_rows(self, shape):
        return pl.BlockSpec(
            (1, self.owned) + shape, lambda i, ints: (ints[1] // QUAD, ints[1] % QUAD, 0, 0)
        )

    def table_call(self, kernel, name, fields, inputs, in_specs, out_specs, out_shape, scratch, token):
        extra = list(token)
        kernel, out_specs, out_shape = stamped(kernel, 1 + len(inputs), len(extra), out_specs, out_shape)
        return pl.pallas_call(
            kernel,
            grid_spec=pltpu.PrefetchScalarGridSpec(
                num_scalar_prefetch=1,
                grid=(fields,),
                in_specs=in_specs + [ANY] * len(extra),
                out_specs=out_specs,
                scratch_shapes=scratch,
            ),
            out_shape=out_shape,
            compiler_params=pltpu.CompilerParams(vmem_limit_bytes=24 * MIB),
            cost_estimate=COST,
            name=name,
        )(self.ints, *inputs, *extra)

    def block4(self, *shape):
        return pl.BlockSpec((1,) + shape, lambda i, ints: (i, 0, 0, 0))

    def coefficients(self, mine, core, chip, token):
        fields = mine.shape[0]

        def kernel(ints, reals, table, mine, core, chip, out, column):
            scalars = self.scalars(ints, reals)
            row = lax.broadcasted_iota(jnp.int32, (self.depth, self.cells), 0)
            for k, part in enumerate((mine[0], core[0, 0], chip[0, 0], chip[1, 0])):
                column[:, scalars.rank ^ k] = part
            for j in range(self.owned):
                modes = [
                    jnp.dot(
                        table[0, j],
                        column[2 * j + a].reshape(QUAD * self.block, self.cells),
                        precision=lax.Precision.HIGHEST,
                        preferred_element_type=jnp.float32,
                    )
                    for a in range(2)
                ]
                split = scalars.split(scalars.rank * self.owned + j)
                out[0, j] = jnp.where(row < split, modes[0], modes[1])

        return self.table_call(
            kernel,
            "coefficients",
            fields,
            [self.reals, self.table, mine, core, chip],
            [SMEM, self.own_rows(self.table.shape[2:]), self.part(), self.parts(1), self.parts(2)],
            self.block4(self.owned, self.depth, self.cells),
            shaped(fields, self.owned, self.depth, self.cells),
            [pltpu.VMEM((self.cycles, QUAD, self.block, self.cells), jnp.float32)],
            token,
        )

    def filtered(self, own, other, mine, core, chip, token):
        fields = mine.shape[0]

        def kernel(ints, reals, back, own, other, mine, core, chip, *refs):
            (mine_out, core_out, chip_out), waves = refs[:3], refs[3]
            scalars = self.scalars(ints, reals)
            row = lax.broadcasted_iota(jnp.int32, (self.depth, self.cells), 0)
            source = (mine.at[0], core.at[0, 0], chip.at[0, 0], chip.at[1, 0])
            result = (mine_out.at[0], core_out.at[0, 0], chip_out.at[0, 0], chip_out.at[1, 0])
            for j in range(self.owned):
                pair = scalars.rank * self.owned + j
                total = own[0, j] + other[0, j]
                keep = row < scalars.split(pair)
                for a in range(2):
                    waves[2 * j + a] = jnp.dot(
                        back[0, j],
                        jnp.where(keep if a == 0 else jnp.logical_not(keep), total, 0.0),
                        precision=lax.Precision.HIGHEST,
                        preferred_element_type=jnp.float32,
                    ).reshape(QUAD, self.block, self.cells)
                    r = pair + a * self.pairs
                    for k in range(QUAD):
                        result[k][2 * j + a] = (
                            scalars.base(r) * source[k][2 * j + a]
                            + scalars.scale(r) * waves[2 * j + a, scalars.rank ^ k]
                        )

        modes = self.block4(self.owned, self.depth, self.cells)
        return self.table_call(
            kernel,
            "filtered",
            fields,
            [self.reals, self.back, own, other, mine, core, chip],
            [SMEM, self.own_rows(self.back.shape[2:]), modes, modes]
            + [self.part(), self.parts(1), self.parts(2)],
            [self.part(), self.parts(1), self.parts(2)],
            self.quad_shapes(fields),
            [pltpu.VMEM((self.cycles, QUAD, self.block, self.cells), jnp.float32)],
            token,
        )

    def place_near(self, mine, core, chip, held, lo, hi, token):
        carried = [] if held is None else [held]

        def kernel(ints, reals, mine, core, chip, *refs):
            out, stage = refs[-2:]
            rank = self.scalars(ints, reals).rank
            for k, part in enumerate((mine[0], core[0, 0], chip[0, 0], core[1, 0])):
                stage[rank ^ k] = part
            for o in range(QUAD):
                for j in range(self.owned):
                    for a in range(2):
                        out[0, :, o * self.owned + j + a * self.pairs, :] = stage[o, 2 * j + a]

        return call(
            kernel,
            "place_near",
            token,
            (hi - lo,),
            [self.ints, self.reals, mine, core, chip] + carried,
            [SMEM, SMEM, self.part(), self.parts(2), self.parts(1)] + [ANY] * len(carried),
            self.side(lo, 0),
            shaped(*self.shape),
            [pltpu.VMEM((QUAD, self.cycles, self.block, self.cells), jnp.float32)],
            alias={5: 0} if carried else None,
        )

    def place_far(self, local, others, held, lo, hi, token):
        carried = [] if held is None else [held]
        faces, face_specs = self.faces(lo, 1)

        def kernel(ints, reals, local, *refs):
            others, out = refs[9 : len(refs) - 1 - len(carried)], refs[-1]
            out[0] = sums(self.scalars(ints, reals), local, others)
            low, high = self.face_terms(refs, lo, 1)
            out[0, 0] += low
            out[0, self.block - 1] += high

        return call(
            kernel,
            "place_far",
            token,
            (hi - lo,),
            [self.ints, self.reals, local] + faces + others + carried,
            [SMEM, SMEM, self.side(lo, 0)]
            + face_specs
            + [self.side(0, 0)] * len(others)
            + [ANY] * len(carried),
            self.side(lo, 1),
            shaped(*self.shape),
            alias={3 + len(faces) + len(others): 0} if carried else None,
        )


def spans(sizes, total):
    ends = np.cumsum(sizes)
    return [(int(end - size), int(end)) for size, end in zip(sizes, ends)]


def body(adjoint, source, viscosity, kappa, coupling, bc_flags, inst_map):
    slots = lax.axis_size("inst")
    sectors = lax.axis_size("space")
    center = adjoint[0]
    fields, block, cycles, cells = center.shape
    near = cycles // 2
    points = block * sectors
    quads = sectors // QUAD

    def to_partner(x, pick):
        pairs = []
        for i in range(slots):
            for p in range(sectors):
                pairs.append((i * sectors + p, pick(i, p % 2) * sectors + p))
        return lax.ppermute(x, ("inst", "space"), pairs)

    def to_first(x):
        return to_partner(x, lambda i, core: first_partner(i, core, slots))

    def to_later(x, s):
        return to_partner(x, lambda i, core: later_partner(i, core, slots, s))

    def to_sector(x, k):
        return lax.ppermute(x, "space", [(i, i ^ k) for i in range(sectors)])

    def ring(x, step):
        return lax.ppermute(x, "space", [(i, (i + step) % sectors) for i in range(sectors)])

    table, split, base, scale = mode_layout(points, near)
    table = table.reshape(table.shape[0], table.shape[1], quads, QUAD * block).transpose(2, 0, 1, 3)
    here = jnp.stack([lax.axis_index("inst"), lax.axis_index("space")])
    ints = jnp.concatenate([here, inst_map, jnp.asarray(split)])
    reals = jnp.asarray(np.concatenate([spectral_values(slots), base, scale]).astype(np.float32))
    plan = Plan(
        ints,
        reals,
        slots,
        center.shape,
        near,
        jnp.asarray(np.ascontiguousarray(table)),
        jnp.asarray(np.ascontiguousarray(table.transpose(0, 1, 3, 2))),
    )

    groups = [(lo, hi, 0) for lo, hi in spans(NEAR_SIZES, fields)]
    groups += [(lo, hi, 1) for lo, hi in spans(FAR_SIZES, fields)]
    first, others, parts, own, done = {}, {}, {}, {}, {}
    made, local, held, halos = {}, {}, None, None
    for step, g in ORDER:
        lo, hi, index = groups[g]
        token = [made[before] for before, after in EDGES if after == (step, g)]
        if step == "pack":
            *packed, stamp = pack(center, viscosity, lo, hi, index, near, halos is None, token, halos is None)
            first[g] = to_first(packed[0])
            if halos is None:
                halos = ring(packed[1], 1), ring(packed[2], -1)
                plan.halos, plan.center, plan.viscosity, plan.kappa = halos, center, viscosity, kappa
        elif step == "local":
            local[g], stamp = local_part(
                g, center, source[0], viscosity, kappa, coupling, bc_flags, token
            )
        elif step == "mix":
            *mixed, stamp = plan.mix(center, first[g], lo, hi, index, token)
            others[g] = [first[g]] + [to_later(x, s + 1) for s, x in enumerate(mixed)]
        elif step == "spread":
            mine, core, chip, stamp = plan.spread(local[0], others[g], lo, hi, token)
            parts[g] = mine, to_sector(core, 1), chip
        elif step == "join":
            mine, core, chip = parts[g]
            chip, stamp = plan.join(chip, core, token)
            parts[g] = mine, core, to_sector(chip, 2)
        elif step == "coef":
            part, stamp = plan.coefficients(*parts[g], token)
            stride = QUAD
            while 2 * stride < sectors:
                part = part + to_sector(part, stride)
                stride = 2 * stride
            other = to_sector(part, stride) if stride < sectors else jnp.zeros_like(part)
            own[g] = part, other
        elif step == "filter":
            mine, core, chip, stamp = plan.filtered(*own[g], *parts[g], token)
            done[g] = mine, core, to_sector(chip, 2)
        elif step == "back":
            mine, core, chip = done[g]
            core, stamp = plan.join(core, chip, token)
            done[g] = mine, to_sector(core, 1), chip
        elif step == "near":
            held, stamp = plan.place_near(*done[g], held, lo, hi, token)
        else:
            held, stamp = plan.place_far(local[1], others[g], held, lo, hi, token)
        made[step, g] = stamp
    return held[None]


def solution(mesh):
    return jax.shard_map(
        body,
        mesh=mesh,
        in_specs=(
            P("inst", None, "space", None, None),
            P("inst", None, "space", None, None),
            P("space", None, None),
            P(),
            P(),
            P(),
            P(),
        ),
        out_specs=P("inst", None, "space", None, None),
        check_vma=False,
    )
```

```python
import functools

import jax
import jax.numpy as jnp
import numpy as np
from jax import lax
from jax.experimental import pallas as pl
from jax.experimental.pallas import tpu as pltpu
from jax.sharding import PartitionSpec as P

QUAD = 4
NEAR_SIZES = (2, 2, 1)
FAR_SIZES = (2, 2, 1)
ORDER = (
    ("pack", 0),
    ("pack", 3),
    ("pack", 2),
    ("pack", 1),
    ("local", 1),
    ("mix", 0),
    ("local", 0),
    ("mix", 1),
    ("pack", 4),
    ("spread", 0),
    ("join", 0),
    ("spread", 1),
    ("mix", 2),
    ("coef", 0),
    ("join", 1),
    ("spread", 2),
    ("pack", 5),
    ("join", 2),
    ("mix", 4),
    ("coef", 1),
    ("filter", 0),
    ("mix", 3),
    ("coef", 2),
    ("mix", 5),
    ("filter", 1),
    ("filter", 2),
    ("back", 0),
    ("far", 4),
    ("back", 1),
    ("near", 0),
    ("far", 3),
    ("back", 2),
    ("far", 5),
    ("near", 2),
    ("near", 1),
)
EDGES = tuple(zip(ORDER[:-1], ORDER[1:]))
PACK = 60
LOCAL = 52
SMEM = pl.BlockSpec(memory_space=pltpu.SMEM)
ANY = pl.BlockSpec(memory_space=pl.ANY)
COST = pl.CostEstimate(flops=0, bytes_accessed=0, transcendentals=0)
MIB = 1024 * 1024


def spectral_values(slots):
    offset = np.arange(1 - slots, slots)
    safe = np.where(offset == 0, 1.0, np.sin(np.pi * offset / slots))
    return np.where(offset == 0, 0.0, 0.5 * (1.0 - 2.0 * (np.abs(offset) % 2)) / safe)


def mode_layout(points, near):
    half = points // 2
    pairs = near // 2
    theta = np.arange(points)
    bases, base, scale = [], np.zeros(near), np.zeros(near)
    for r in range(near):
        cutoff = max(4, points * (r + 1) // (2 * near))
        weight = max(1.0 - r / near, 0.0)
        kept = [m for m in range(half + 1) if m < cutoff]
        out = [m for m in range(half + 1) if m >= cutoff]
        count = [sum(1 if m in (0, half) else 2 for m in modes) for modes in (kept, out)]
        low = count[0] <= count[1]
        rows = []
        for m in kept if low else out:
            angle = 2.0 * np.pi * (m * theta % points) / points
            if m in (0, half):
                rows.append(np.cos(angle) / np.sqrt(points))
            else:
                rows.append(np.cos(angle) * np.sqrt(2.0 / points))
                rows.append(np.sin(angle) * np.sqrt(2.0 / points))
        bases.append(rows)
        base[r] = 1.0 - weight if low else 1.0
        scale[r] = weight if low else -weight
    depth = max(len(bases[p]) + len(bases[p + pairs]) for p in range(pairs))
    depth = -(-depth // 8) * 8
    table = np.zeros((pairs, depth, points), np.float32)
    split = np.zeros(pairs, np.int32)
    for p in range(pairs):
        rows = bases[p] + bases[p + pairs]
        table[p, : len(rows)] = np.stack(rows)
        split[p] = len(bases[p])
    return table, split, base, scale


class Scalars:
    def __init__(self, ints, reals, slots, near):
        self.ints, self.reals, self.slots, self.near = ints, reals, slots, near
        self.slot, self.place = ints[0], ints[1]
        self.rank = self.place % QUAD

    def weight(self, i, j):
        return self.reals[self.ints[2 + i] - self.ints[2 + j] + self.slots - 1]

    def split(self, pair):
        return self.ints[2 + self.slots + pair]

    def base(self, r):
        return self.reals[2 * self.slots - 1 + r]

    def scale(self, r):
        return self.reals[2 * self.slots - 1 + self.near + r]

    def first(self):
        return first_partner(self.slot, self.place % 2, self.slots)

    def target(self, s):
        return later_partner(self.slot, self.place % 2, self.slots, s)


def first_partner(slot, core, slots):
    if slots == 4:
        return slot ^ (2 - core)
    return slot ^ 1


def later_partner(slot, core, slots, s):
    if slots == 4:
        return slot ^ (1 + core)
    return (slot // 2 + s) % (slots // 2) * 2 + slot % 2


def stamped(kernel, inputs, extra, out_specs, out_shape):
    out_specs = out_specs if isinstance(out_specs, list) else [out_specs]
    out_shape = out_shape if isinstance(out_shape, list) else [out_shape]
    skip, end = inputs + extra, inputs + extra + len(out_shape)

    def body(*refs):
        refs[end][...] = jnp.zeros_like(refs[end])
        kernel(*refs[:inputs], *refs[skip:end], *refs[end + 1 :])

    stamp = pl.BlockSpec((8, 128), lambda i, *_: (0, 0))
    return body, out_specs + [stamp], out_shape + [shaped(8, 128)]


def call(kernel, name, token, grid, inputs, in_specs, out_specs, out_shape, scratch=(), alias=None, grant=24):
    extra = list(token)
    kernel, out_specs, out_shape = stamped(kernel, len(inputs), len(extra), out_specs, out_shape)
    return pl.pallas_call(
        kernel,
        grid=grid,
        in_specs=list(in_specs) + [ANY] * len(extra),
        out_specs=out_specs,
        out_shape=out_shape,
        scratch_shapes=list(scratch),
        input_output_aliases=alias or {},
        compiler_params=pltpu.CompilerParams(vmem_limit_bytes=grant * MIB),
        cost_estimate=COST,
        name=name,
    )(*inputs, *extra)


def shaped(*shape):
    return jax.ShapeDtypeStruct(shape, jnp.float32)


def pack(center, viscosity, lo, hi, index, near, edges, token, early):
    fields, block, rows, cells = center.shape
    inputs, in_specs = [center], [pl.BlockSpec((1, block, near, cells), lambda i: (lo + i, 0, index, 0))]
    shapes = [shaped(hi - lo, block, near, cells)]
    out_specs = [pl.BlockSpec((1, block, near, cells), lambda i: (i, 0, 0, 0))]
    if edges:
        for start in (block - 1, 0):
            inputs += [center, viscosity]
            in_specs.append(pl.BlockSpec((fields, 1, rows, cells), lambda i, s=start: (0, s, 0, 0)))
            in_specs.append(pl.BlockSpec((1, rows, cells), lambda i, s=start: (s, 0, 0)))
            shapes.append(shaped(fields + 1, 1, rows, cells))
            out_specs.append(pl.BlockSpec((fields + 1, 1, rows, cells), lambda i: (0, 0, 0, 0)))

    def kernel(source, *refs):
        out, rest = refs[len(inputs) - 1], refs[len(inputs) :]
        out[...] = source[...]
        for e, edge in enumerate(rest):
            edge[:fields] = refs[2 * e][...]
            edge[fields] = refs[2 * e + 1][...]

    return call(kernel, "pack", token, (hi - lo,), inputs, in_specs, out_specs, shapes, grant=PACK if early else 24)


def local_kernel(
    far, coupling, kappa, flags, adj, before, after, next_to, src, mu, mu_before, mu_after, mu_next, out
):
    fields, planes, rows, cells = adj.shape
    step = pl.program_id(0)
    first = step == 0
    last = step == pl.num_programs(0) - 1
    row = lax.broadcasted_iota(jnp.int32, (rows, cells), 0)
    col = lax.broadcasted_iota(jnp.int32, (rows, cells), 1)
    ring = 0.5 / ((row + rows * far).astype(jnp.float32) + 1.0)

    def visc(k):
        return mu_before[0] if k < 0 else mu_after[0] if k >= planes else mu[k]

    def cell(f, k):
        return before[f, 0] if k < 0 else after[f, 0] if k >= planes else adj[f, k]

    def outward(x, edge):
        moved = pltpu.roll(x, rows - 1, 0)
        return moved if far else jnp.where(row == rows - 1, edge[:1], moved)

    def inward(x, edge):
        moved = pltpu.roll(x, 1, 0)
        return jnp.where(row == 0, edge[-1:], moved) if far else moved

    walls = []
    for f in range(fields):
        opens = [(1 - flags[f, i]).astype(jnp.float32) for i in range(3)]
        wall = jnp.where(col == 0, opens[0], 0.0)
        wall = wall + jnp.where(col == cells - 1, opens[1], 0.0)
        walls.append(wall + jnp.where(row == rows - 1, opens[2], 0.0) if far else wall)

    for k in range(planes):
        m = visc(k)
        up = ring * (m + visc(k + 1))
        down = ring * (m + visc(k - 1))
        if k == planes - 1:
            up = jnp.where(last, 0.0, up)
        if k == 0:
            down = jnp.where(first, 0.0, down)
        outer = 0.5 * (m + outward(m, mu_next[k]))
        inner = 0.5 * (m + inward(m, mu_next[k]))
        if far:
            outer = jnp.where(row < rows - 1, outer, 0.0)
        else:
            inner = jnp.where(row > 0, inner, 0.0)
        east = jnp.where(col < cells - 1, 0.5 * (m + pltpu.roll(m, cells - 1, 1)), 0.0)
        west = jnp.where(col > 0, 0.5 * (m + pltpu.roll(m, 1, 1)), 0.0)
        diag = up + down + outer + inner + east + west
        for f in range(fields):
            p = adj[f, k]
            flux = (diag + walls[f] * m) * p
            flux = flux - up * cell(f, k + 1) - down * cell(f, k - 1)
            flux = flux - outer * outward(p, next_to[f, k]) - inner * inward(p, next_to[f, k])
            flux = flux - east * pltpu.roll(p, cells - 1, 1) - west * pltpu.roll(p, 1, 1)
            total = src[f, k] + kappa[f] * flux
            for g in range(fields):
                total = total + coupling[g, f] * adj[g, k]
            out[f, k] = total


def local_part(far, center, source, viscosity, kappa, coupling, flags, token):
    fields, block, rows, cells = center.shape
    half = rows // 2
    planes = min(8, block)
    edge = half // 8 - 1 if far else half // 8

    def whole(width, index):
        return pl.BlockSpec((fields, width, half, cells), lambda i: (0, index(i), far, 0))

    def plane(width, index):
        return pl.BlockSpec((width, half, cells), lambda i: (index(i), far, 0))

    behind = lambda i: jnp.maximum(i * planes - 1, 0)
    ahead = lambda i: jnp.minimum(i * planes + planes, block - 1)
    here = lambda i: i
    return call(
        functools.partial(local_kernel, far),
        "local_part",
        token,
        (block // planes,),
        [coupling, kappa, flags, center, center, center, center, source]
        + [viscosity] * 4,
        [
            SMEM,
            SMEM,
            SMEM,
            whole(planes, here),
            whole(1, behind),
            whole(1, ahead),
            pl.BlockSpec((fields, planes, 8, cells), lambda i: (0, i, edge, 0)),
            whole(planes, here),
            plane(planes, here),
            plane(1, behind),
            plane(1, ahead),
            pl.BlockSpec((planes, 8, cells), lambda i: (i, edge, 0)),
        ],
        pl.BlockSpec((fields, planes, half, cells), lambda i: (0, i, 0, 0)),
        shaped(fields, block, half, cells),
        grant=LOCAL,
    )


def sums(scalars, local, others):
    total = local[0] + scalars.weight(scalars.first(), scalars.slot) * others[0][0]
    for part in others[1:]:
        total = total + part[0]
    return total


class Plan:
    def __init__(self, ints, reals, slots, shape, near, table, back):
        self.ints, self.reals, self.slots, self.near = ints, reals, slots, near
        self.shape, self.table, self.back = shape, table, back
        self.fields, self.block, self.rows, self.cells = shape
        self.pairs = near // 2
        self.owned = self.pairs // QUAD
        self.cycles = near // QUAD
        self.depth = table.shape[2]

    def scalars(self, ints, reals):
        return Scalars(ints, reals, self.slots, self.near)

    def side(self, first, index):
        return pl.BlockSpec((1, self.block, self.near, self.cells), lambda i: (first + i, 0, index, 0))

    def faces(self, lo, side):
        shape = (1, 1, self.near, self.cells)
        at = lambda f, k: pl.BlockSpec(shape, lambda i: (f(i), k, side, 0))
        field = lambda i: lo + i
        inputs, specs = [self.kappa], [SMEM]
        for k, halo in zip((0, self.block - 1), self.halos):
            inputs += [self.center, halo, self.viscosity[None], halo]
            specs += [at(field, k), at(field, 0), at(lambda i: 0, k), at(lambda i: self.fields, 0)]
        return inputs, specs

    def face_terms(self, refs, lo, side):
        kappa, rest = refs[0], refs[1:9]
        row = lax.broadcasted_iota(jnp.int32, (self.near, self.cells), 0) + side * self.near
        ring = 0.5 * kappa[lo + pl.program_id(0)] / (row.astype(jnp.float32) + 1.0)
        here, there, mu, mu_there = rest[:4]
        low = ring * (mu[0, 0] + mu_there[0, 0]) * (here[0, 0] - there[0, 0])
        here, there, mu, mu_there = rest[4:]
        return low, ring * (mu[0, 0] + mu_there[0, 0]) * (here[0, 0] - there[0, 0])

    def part(self):
        return pl.BlockSpec((1, self.cycles, self.block, self.cells), lambda i, *_: (i, 0, 0, 0))

    def parts(self, count, first=0):
        shape = (count, 1, self.cycles, self.block, self.cells)
        return pl.BlockSpec(shape, lambda i, *_: (first, i, 0, 0, 0))

    def quad_shapes(self, fields):
        one = (fields, self.cycles, self.block, self.cells)
        return [shaped(*one), shaped(2, *one), shaped(2, *one)]

    def mix(self, center, first, lo, hi, index, token):
        count = max(1, self.slots // 2 - 1)

        def kernel(ints, reals, own, got, *outs):
            scalars = self.scalars(ints, reals)
            for s in range(count):
                target = scalars.target(s + 1)
                outs[s][0] = (
                    scalars.weight(scalars.slot, target) * own[0]
                    + scalars.weight(scalars.first(), target) * got[0]
                )

        return call(
            kernel,
            "mix",
            token,
            (hi - lo,),
            [self.ints, self.reals, center, first],
            [SMEM, SMEM, self.side(lo, index), self.side(0, 0)],
            [self.side(0, 0)] * count,
            [shaped(hi - lo, self.block, self.near, self.cells)] * count,
        )

    def spread(self, local, others, lo, hi, token):
        faces, face_specs = self.faces(lo, 0)

        def kernel(ints, reals, local, *refs):
            others, (mine, core, chip), (flat, stage) = refs[9:-5], refs[-5:-2], refs[-2:]
            scalars = self.scalars(ints, reals)
            flat[...] = sums(scalars, local, others).reshape(flat.shape)
            low, high = self.face_terms(refs, lo, 0)
            flat[: self.near] += low
            flat[-self.near :] += high
            for o in range(QUAD):
                for j in range(self.owned):
                    for a in range(2):
                        r = o * self.owned + j + a * self.pairs
                        stage[o, 2 * j + a] = flat[pl.ds(r, self.block, stride=self.near), :]
            mine[0] = stage[scalars.rank]
            core[0, 0] = stage[scalars.rank ^ 1]
            core[1, 0] = stage[scalars.rank ^ 3]
            chip[0, 0] = stage[scalars.rank ^ 2]

        return call(
            kernel,
            "spread",
            token,
            (hi - lo,),
            [self.ints, self.reals, local] + faces + others,
            [SMEM, SMEM, self.side(lo, 0)] + face_specs + [self.side(0, 0)] * len(others),
            [self.part(), self.parts(2), self.parts(1)],
            self.quad_shapes(hi - lo),
            [
                pltpu.VMEM((self.block * self.near, self.cells), jnp.float32),
                pltpu.VMEM((QUAD, self.cycles, self.block, self.cells), jnp.float32),
            ],
        )

    def join(self, held, new, token):
        def kernel(held, new, out):
            out[...] = new[...]

        return call(
            kernel,
            "join",
            token,
            (held.shape[1],),
            [held, new],
            [ANY, self.parts(1, 1)],
            self.parts(1, 1),
            shaped(*held.shape),
            alias={0: 0},
        )

    def own_rows(self, shape):
        return pl.BlockSpec(
            (1, self.owned) + shape, lambda i, ints: (ints[1] // QUAD, ints[1] % QUAD, 0, 0)
        )

    def table_call(self, kernel, name, fields, inputs, in_specs, out_specs, out_shape, scratch, token):
        extra = list(token)
        kernel, out_specs, out_shape = stamped(kernel, 1 + len(inputs), len(extra), out_specs, out_shape)
        return pl.pallas_call(
            kernel,
            grid_spec=pltpu.PrefetchScalarGridSpec(
                num_scalar_prefetch=1,
                grid=(fields,),
                in_specs=in_specs + [ANY] * len(extra),
                out_specs=out_specs,
                scratch_shapes=scratch,
            ),
            out_shape=out_shape,
            compiler_params=pltpu.CompilerParams(vmem_limit_bytes=24 * MIB),
            cost_estimate=COST,
            name=name,
        )(self.ints, *inputs, *extra)

    def block4(self, *shape):
        return pl.BlockSpec((1,) + shape, lambda i, ints: (i, 0, 0, 0))

    def coefficients(self, mine, core, chip, token):
        fields = mine.shape[0]

        def kernel(ints, reals, table, mine, core, chip, out, column):
            scalars = self.scalars(ints, reals)
            row = lax.broadcasted_iota(jnp.int32, (self.depth, self.cells), 0)
            for k, part in enumerate((mine[0], core[0, 0], chip[0, 0], chip[1, 0])):
                column[:, scalars.rank ^ k] = part
            for j in range(self.owned):
                modes = [
                    jnp.dot(
                        table[0, j],
                        column[2 * j + a].reshape(QUAD * self.block, self.cells),
                        precision=lax.Precision.HIGHEST,
                        preferred_element_type=jnp.float32,
                    )
                    for a in range(2)
                ]
                split = scalars.split(scalars.rank * self.owned + j)
                out[0, j] = jnp.where(row < split, modes[0], modes[1])

        return self.table_call(
            kernel,
            "coefficients",
            fields,
            [self.reals, self.table, mine, core, chip],
            [SMEM, self.own_rows(self.table.shape[2:]), self.part(), self.parts(1), self.parts(2)],
            self.block4(self.owned, self.depth, self.cells),
            shaped(fields, self.owned, self.depth, self.cells),
            [pltpu.VMEM((self.cycles, QUAD, self.block, self.cells), jnp.float32)],
            token,
        )

    def filtered(self, own, other, mine, core, chip, token):
        fields = mine.shape[0]

        def kernel(ints, reals, back, own, other, mine, core, chip, *refs):
            (mine_out, core_out, chip_out), waves = refs[:3], refs[3]
            scalars = self.scalars(ints, reals)
            row = lax.broadcasted_iota(jnp.int32, (self.depth, self.cells), 0)
            source = (mine.at[0], core.at[0, 0], chip.at[0, 0], chip.at[1, 0])
            result = (mine_out.at[0], core_out.at[0, 0], chip_out.at[0, 0], chip_out.at[1, 0])
            for j in range(self.owned):
                pair = scalars.rank * self.owned + j
                total = own[0, j] + other[0, j]
                keep = row < scalars.split(pair)
                for a in range(2):
                    waves[2 * j + a] = jnp.dot(
                        back[0, j],
                        jnp.where(keep if a == 0 else jnp.logical_not(keep), total, 0.0),
                        precision=lax.Precision.HIGHEST,
                        preferred_element_type=jnp.float32,
                    ).reshape(QUAD, self.block, self.cells)
                    r = pair + a * self.pairs
                    for k in range(QUAD):
                        result[k][2 * j + a] = (
                            scalars.base(r) * source[k][2 * j + a]
                            + scalars.scale(r) * waves[2 * j + a, scalars.rank ^ k]
                        )

        modes = self.block4(self.owned, self.depth, self.cells)
        return self.table_call(
            kernel,
            "filtered",
            fields,
            [self.reals, self.back, own, other, mine, core, chip],
            [SMEM, self.own_rows(self.back.shape[2:]), modes, modes]
            + [self.part(), self.parts(1), self.parts(2)],
            [self.part(), self.parts(1), self.parts(2)],
            self.quad_shapes(fields),
            [pltpu.VMEM((self.cycles, QUAD, self.block, self.cells), jnp.float32)],
            token,
        )

    def place_near(self, mine, core, chip, held, lo, hi, token):
        carried = [] if held is None else [held]

        def kernel(ints, reals, mine, core, chip, *refs):
            out, stage = refs[-2:]
            rank = self.scalars(ints, reals).rank
            for k, part in enumerate((mine[0], core[0, 0], chip[0, 0], core[1, 0])):
                stage[rank ^ k] = part
            for o in range(QUAD):
                for j in range(self.owned):
                    for a in range(2):
                        out[0, :, o * self.owned + j + a * self.pairs, :] = stage[o, 2 * j + a]

        return call(
            kernel,
            "place_near",
            token,
            (hi - lo,),
            [self.ints, self.reals, mine, core, chip] + carried,
            [SMEM, SMEM, self.part(), self.parts(2), self.parts(1)] + [ANY] * len(carried),
            self.side(lo, 0),
            shaped(*self.shape),
            [pltpu.VMEM((QUAD, self.cycles, self.block, self.cells), jnp.float32)],
            alias={5: 0} if carried else None,
        )

    def place_far(self, local, others, held, lo, hi, token):
        carried = [] if held is None else [held]
        faces, face_specs = self.faces(lo, 1)

        def kernel(ints, reals, local, *refs):
            others, out = refs[9 : len(refs) - 1 - len(carried)], refs[-1]
            out[0] = sums(self.scalars(ints, reals), local, others)
            low, high = self.face_terms(refs, lo, 1)
            out[0, 0] += low
            out[0, self.block - 1] += high

        return call(
            kernel,
            "place_far",
            token,
            (hi - lo,),
            [self.ints, self.reals, local] + faces + others + carried,
            [SMEM, SMEM, self.side(lo, 0)]
            + face_specs
            + [self.side(0, 0)] * len(others)
            + [ANY] * len(carried),
            self.side(lo, 1),
            shaped(*self.shape),
            alias={3 + len(faces) + len(others): 0} if carried else None,
        )


def spans(sizes, total):
    ends = np.cumsum(sizes)
    return [(int(end - size), int(end)) for size, end in zip(sizes, ends)]


def body(adjoint, source, viscosity, kappa, coupling, bc_flags, inst_map):
    slots = lax.axis_size("inst")
    sectors = lax.axis_size("space")
    center = adjoint[0]
    fields, block, cycles, cells = center.shape
    near = cycles // 2
    points = block * sectors
    quads = sectors // QUAD

    def to_partner(x, pick):
        pairs = []
        for i in range(slots):
            for p in range(sectors):
                pairs.append((i * sectors + p, pick(i, p % 2) * sectors + p))
        return lax.ppermute(x, ("inst", "space"), pairs)

    def to_first(x):
        return to_partner(x, lambda i, core: first_partner(i, core, slots))

    def to_later(x, s):
        return to_partner(x, lambda i, core: later_partner(i, core, slots, s))

    def to_sector(x, k):
        return lax.ppermute(x, "space", [(i, i ^ k) for i in range(sectors)])

    def ring(x, step):
        return lax.ppermute(x, "space", [(i, (i + step) % sectors) for i in range(sectors)])

    table, split, base, scale = mode_layout(points, near)
    table = table.reshape(table.shape[0], table.shape[1], quads, QUAD * block).transpose(2, 0, 1, 3)
    here = jnp.stack([lax.axis_index("inst"), lax.axis_index("space")])
    ints = jnp.concatenate([here, inst_map, jnp.asarray(split)])
    reals = jnp.asarray(np.concatenate([spectral_values(slots), base, scale]).astype(np.float32))
    plan = Plan(
        ints,
        reals,
        slots,
        center.shape,
        near,
        jnp.asarray(np.ascontiguousarray(table)),
        jnp.asarray(np.ascontiguousarray(table.transpose(0, 1, 3, 2))),
    )

    groups = [(lo, hi, 0) for lo, hi in spans(NEAR_SIZES, fields)]
    groups += [(lo, hi, 1) for lo, hi in spans(FAR_SIZES, fields)]
    first, others, parts, own, done = {}, {}, {}, {}, {}
    made, local, held, halos = {}, {}, None, None
    for step, g in ORDER:
        lo, hi, index = groups[g]
        token = [made[before] for before, after in EDGES if after == (step, g)]
        if step == "pack":
            early = 0 not in local
            *packed, stamp = pack(center, viscosity, lo, hi, index, near, halos is None, token, early)
            first[g] = to_first(packed[0])
            if halos is None:
                halos = ring(packed[1], 1), ring(packed[2], -1)
                plan.halos, plan.center, plan.viscosity, plan.kappa = halos, center, viscosity, kappa
        elif step == "local":
            local[g], stamp = local_part(
                g, center, source[0], viscosity, kappa, coupling, bc_flags, token
            )
        elif step == "mix":
            *mixed, stamp = plan.mix(center, first[g], lo, hi, index, token)
            others[g] = [first[g]] + [to_later(x, s + 1) for s, x in enumerate(mixed)]
        elif step == "spread":
            mine, core, chip, stamp = plan.spread(local[0], others[g], lo, hi, token)
            parts[g] = mine, to_sector(core, 1), chip
        elif step == "join":
            mine, core, chip = parts[g]
            chip, stamp = plan.join(chip, core, token)
            parts[g] = mine, core, to_sector(chip, 2)
        elif step == "coef":
            part, stamp = plan.coefficients(*parts[g], token)
            stride = QUAD
            while 2 * stride < sectors:
                part = part + to_sector(part, stride)
                stride = 2 * stride
            other = to_sector(part, stride) if stride < sectors else jnp.zeros_like(part)
            own[g] = part, other
        elif step == "filter":
            mine, core, chip, stamp = plan.filtered(*own[g], *parts[g], token)
            done[g] = mine, core, to_sector(chip, 2)
        elif step == "back":
            mine, core, chip = done[g]
            core, stamp = plan.join(core, chip, token)
            done[g] = mine, to_sector(core, 1), chip
        elif step == "near":
            held, stamp = plan.place_near(*done[g], held, lo, hi, token)
        else:
            held, stamp = plan.place_far(local[1], others[g], held, lo, hi, token)
        made[step, g] = stamp
    return held[None]


def solution(mesh):
    return jax.shard_map(
        body,
        mesh=mesh,
        in_specs=(
            P("inst", None, "space", None, None),
            P("inst", None, "space", None, None),
            P("space", None, None),
            P(),
            P(),
            P(),
            P(),
        ),
        out_specs=P("inst", None, "space", None, None),
        check_vma=False,
    )
```

```python
import functools

import jax
import jax.numpy as jnp
import numpy as np
from jax import lax
from jax.experimental import pallas as pl
from jax.experimental.pallas import tpu as pltpu
from jax.sharding import PartitionSpec as P

QUAD = 4
NEAR_SIZES = (2, 1, 2)
FAR_SIZES = (2, 2, 1)
ORDER = (
    ("pack", 0),
    ("pack", 2),
    ("local", 0),
    ("pack", 1),
    ("pack", 4),
    ("pack", 3),
    ("mix", 0),
    ("pack", 5),
    ("mix", 2),
    ("spread", 0),
    ("join", 0),
    ("spread", 2),
    ("mix", 1),
    ("coef", 0),
    ("join", 2),
    ("spread", 1),
    ("join", 1),
    ("local", 1),
    ("mix", 4),
    ("coef", 2),
    ("filter", 0),
    ("mix", 3),
    ("coef", 1),
    ("mix", 5),
    ("filter", 2),
    ("filter", 1),
    ("back", 0),
    ("far", 4),
    ("back", 2),
    ("near", 0),
    ("far", 3),
    ("back", 1),
    ("far", 5),
    ("near", 1),
    ("near", 2),
)
EDGES = tuple(zip(ORDER[:-1], ORDER[1:]))
PACK = 60
LOCAL = 52
SMEM = pl.BlockSpec(memory_space=pltpu.SMEM)
ANY = pl.BlockSpec(memory_space=pl.ANY)
COST = pl.CostEstimate(flops=0, bytes_accessed=0, transcendentals=0)
MIB = 1024 * 1024


def spectral_values(slots):
    offset = np.arange(1 - slots, slots)
    safe = np.where(offset == 0, 1.0, np.sin(np.pi * offset / slots))
    return np.where(offset == 0, 0.0, 0.5 * (1.0 - 2.0 * (np.abs(offset) % 2)) / safe)


def mode_layout(points, near):
    half = points // 2
    pairs = near // 2
    theta = np.arange(points)
    bases, base, scale = [], np.zeros(near), np.zeros(near)
    for r in range(near):
        cutoff = max(4, points * (r + 1) // (2 * near))
        weight = max(1.0 - r / near, 0.0)
        kept = [m for m in range(half + 1) if m < cutoff]
        out = [m for m in range(half + 1) if m >= cutoff]
        count = [sum(1 if m in (0, half) else 2 for m in modes) for modes in (kept, out)]
        low = count[0] <= count[1]
        rows = []
        for m in kept if low else out:
            angle = 2.0 * np.pi * (m * theta % points) / points
            if m in (0, half):
                rows.append(np.cos(angle) / np.sqrt(points))
            else:
                rows.append(np.cos(angle) * np.sqrt(2.0 / points))
                rows.append(np.sin(angle) * np.sqrt(2.0 / points))
        bases.append(rows)
        base[r] = 1.0 - weight if low else 1.0
        scale[r] = weight if low else -weight
    depth = max(len(bases[p]) + len(bases[p + pairs]) for p in range(pairs))
    depth = -(-depth // 8) * 8
    table = np.zeros((pairs, depth, points), np.float32)
    split = np.zeros(pairs, np.int32)
    for p in range(pairs):
        rows = bases[p] + bases[p + pairs]
        table[p, : len(rows)] = np.stack(rows)
        split[p] = len(bases[p])
    return table, split, base, scale


class Scalars:
    def __init__(self, ints, reals, slots, near):
        self.ints, self.reals, self.slots, self.near = ints, reals, slots, near
        self.slot, self.place = ints[0], ints[1]
        self.rank = self.place % QUAD

    def weight(self, i, j):
        return self.reals[self.ints[2 + i] - self.ints[2 + j] + self.slots - 1]

    def split(self, pair):
        return self.ints[2 + self.slots + pair]

    def base(self, r):
        return self.reals[2 * self.slots - 1 + r]

    def scale(self, r):
        return self.reals[2 * self.slots - 1 + self.near + r]

    def first(self):
        return first_partner(self.slot, self.place % 2, self.slots)

    def target(self, s):
        return later_partner(self.slot, self.place % 2, self.slots, s)


def first_partner(slot, core, slots):
    if slots == 4:
        return slot ^ (2 - core)
    return slot ^ 1


def later_partner(slot, core, slots, s):
    if slots == 4:
        return slot ^ (1 + core)
    return (slot // 2 + s) % (slots // 2) * 2 + slot % 2


def stamped(kernel, inputs, extra, out_specs, out_shape):
    out_specs = out_specs if isinstance(out_specs, list) else [out_specs]
    out_shape = out_shape if isinstance(out_shape, list) else [out_shape]
    skip, end = inputs + extra, inputs + extra + len(out_shape)

    def body(*refs):
        refs[end][...] = jnp.zeros_like(refs[end])
        kernel(*refs[:inputs], *refs[skip:end], *refs[end + 1 :])

    stamp = pl.BlockSpec((8, 128), lambda i, *_: (0, 0))
    return body, out_specs + [stamp], out_shape + [shaped(8, 128)]


def call(kernel, name, token, grid, inputs, in_specs, out_specs, out_shape, scratch=(), alias=None, grant=24):
    extra = list(token)
    kernel, out_specs, out_shape = stamped(kernel, len(inputs), len(extra), out_specs, out_shape)
    return pl.pallas_call(
        kernel,
        grid=grid,
        in_specs=list(in_specs) + [ANY] * len(extra),
        out_specs=out_specs,
        out_shape=out_shape,
        scratch_shapes=list(scratch),
        input_output_aliases=alias or {},
        compiler_params=pltpu.CompilerParams(vmem_limit_bytes=grant * MIB),
        cost_estimate=COST,
        name=name,
    )(*inputs, *extra)


def shaped(*shape):
    return jax.ShapeDtypeStruct(shape, jnp.float32)


def pack(center, viscosity, lo, hi, index, near, edges, token, early):
    fields, block, rows, cells = center.shape
    inputs, in_specs = [center], [pl.BlockSpec((1, block, near, cells), lambda i: (lo + i, 0, index, 0))]
    shapes = [shaped(hi - lo, block, near, cells)]
    out_specs = [pl.BlockSpec((1, block, near, cells), lambda i: (i, 0, 0, 0))]
    if edges:
        for start in (block - 1, 0):
            inputs += [center, viscosity]
            in_specs.append(pl.BlockSpec((fields, 1, rows, cells), lambda i, s=start: (0, s, 0, 0)))
            in_specs.append(pl.BlockSpec((1, rows, cells), lambda i, s=start: (s, 0, 0)))
            shapes.append(shaped(fields + 1, 1, rows, cells))
            out_specs.append(pl.BlockSpec((fields + 1, 1, rows, cells), lambda i: (0, 0, 0, 0)))

    def kernel(source, *refs):
        out, rest = refs[len(inputs) - 1], refs[len(inputs) :]
        out[...] = source[...]
        for e, edge in enumerate(rest):
            edge[:fields] = refs[2 * e][...]
            edge[fields] = refs[2 * e + 1][...]

    return call(kernel, "pack", token, (hi - lo,), inputs, in_specs, out_specs, shapes, grant=PACK if early else 24)


def local_kernel(
    far, coupling, kappa, flags, adj, before, after, next_to, src, mu, mu_before, mu_after, mu_next, out
):
    fields, planes, rows, cells = adj.shape
    step = pl.program_id(0)
    first = step == 0
    last = step == pl.num_programs(0) - 1
    row = lax.broadcasted_iota(jnp.int32, (rows, cells), 0)
    col = lax.broadcasted_iota(jnp.int32, (rows, cells), 1)
    ring = 0.5 / ((row + rows * far).astype(jnp.float32) + 1.0)

    def visc(k):
        return mu_before[0] if k < 0 else mu_after[0] if k >= planes else mu[k]

    def cell(f, k):
        return before[f, 0] if k < 0 else after[f, 0] if k >= planes else adj[f, k]

    def outward(x, edge):
        moved = pltpu.roll(x, rows - 1, 0)
        return moved if far else jnp.where(row == rows - 1, edge[:1], moved)

    def inward(x, edge):
        moved = pltpu.roll(x, 1, 0)
        return jnp.where(row == 0, edge[-1:], moved) if far else moved

    walls = []
    for f in range(fields):
        opens = [(1 - flags[f, i]).astype(jnp.float32) for i in range(3)]
        wall = jnp.where(col == 0, opens[0], 0.0)
        wall = wall + jnp.where(col == cells - 1, opens[1], 0.0)
        walls.append(wall + jnp.where(row == rows - 1, opens[2], 0.0) if far else wall)

    for k in range(planes):
        m = visc(k)
        up = ring * (m + visc(k + 1))
        down = ring * (m + visc(k - 1))
        if k == planes - 1:
            up = jnp.where(last, 0.0, up)
        if k == 0:
            down = jnp.where(first, 0.0, down)
        outer = 0.5 * (m + outward(m, mu_next[k]))
        inner = 0.5 * (m + inward(m, mu_next[k]))
        if far:
            outer = jnp.where(row < rows - 1, outer, 0.0)
        else:
            inner = jnp.where(row > 0, inner, 0.0)
        east = jnp.where(col < cells - 1, 0.5 * (m + pltpu.roll(m, cells - 1, 1)), 0.0)
        west = jnp.where(col > 0, 0.5 * (m + pltpu.roll(m, 1, 1)), 0.0)
        diag = up + down + outer + inner + east + west
        for f in range(fields):
            p = adj[f, k]
            flux = (diag + walls[f] * m) * p
            flux = flux - up * cell(f, k + 1) - down * cell(f, k - 1)
            flux = flux - outer * outward(p, next_to[f, k]) - inner * inward(p, next_to[f, k])
            flux = flux - east * pltpu.roll(p, cells - 1, 1) - west * pltpu.roll(p, 1, 1)
            total = src[f, k] + kappa[f] * flux
            for g in range(fields):
                total = total + coupling[g, f] * adj[g, k]
            out[f, k] = total


def local_part(far, center, source, viscosity, kappa, coupling, flags, token):
    fields, block, rows, cells = center.shape
    half = rows // 2
    planes = min(4, block)
    edge = half // 8 - 1 if far else half // 8

    def whole(width, index):
        return pl.BlockSpec((fields, width, half, cells), lambda i: (0, index(i), far, 0))

    def plane(width, index):
        return pl.BlockSpec((width, half, cells), lambda i: (index(i), far, 0))

    behind = lambda i: jnp.maximum(i * planes - 1, 0)
    ahead = lambda i: jnp.minimum(i * planes + planes, block - 1)
    here = lambda i: i
    return call(
        functools.partial(local_kernel, far),
        "local_part",
        token,
        (block // planes,),
        [coupling, kappa, flags, center, center, center, center, source]
        + [viscosity] * 4,
        [
            SMEM,
            SMEM,
            SMEM,
            whole(planes, here),
            whole(1, behind),
            whole(1, ahead),
            pl.BlockSpec((fields, planes, 8, cells), lambda i: (0, i, edge, 0)),
            whole(planes, here),
            plane(planes, here),
            plane(1, behind),
            plane(1, ahead),
            pl.BlockSpec((planes, 8, cells), lambda i: (i, edge, 0)),
        ],
        pl.BlockSpec((fields, planes, half, cells), lambda i: (0, i, 0, 0)),
        shaped(fields, block, half, cells),
        grant=24 if far else LOCAL,
    )


def sums(scalars, local, others):
    total = local[0] + scalars.weight(scalars.first(), scalars.slot) * others[0][0]
    for part in others[1:]:
        total = total + part[0]
    return total


class Plan:
    def __init__(self, ints, reals, slots, shape, near, table, back):
        self.ints, self.reals, self.slots, self.near = ints, reals, slots, near
        self.shape, self.table, self.back = shape, table, back
        self.fields, self.block, self.rows, self.cells = shape
        self.pairs = near // 2
        self.owned = self.pairs // QUAD
        self.cycles = near // QUAD
        self.depth = table.shape[2]

    def scalars(self, ints, reals):
        return Scalars(ints, reals, self.slots, self.near)

    def side(self, first, index):
        return pl.BlockSpec((1, self.block, self.near, self.cells), lambda i: (first + i, 0, index, 0))

    def faces(self, lo, side):
        shape = (1, 1, self.near, self.cells)
        at = lambda f, k: pl.BlockSpec(shape, lambda i: (f(i), k, side, 0))
        field = lambda i: lo + i
        inputs, specs = [self.kappa], [SMEM]
        for k, halo in zip((0, self.block - 1), self.halos):
            inputs += [self.center, halo, self.viscosity[None], halo]
            specs += [at(field, k), at(field, 0), at(lambda i: 0, k), at(lambda i: self.fields, 0)]
        return inputs, specs

    def face_terms(self, refs, lo, side):
        kappa, rest = refs[0], refs[1:9]
        row = lax.broadcasted_iota(jnp.int32, (self.near, self.cells), 0) + side * self.near
        ring = 0.5 * kappa[lo + pl.program_id(0)] / (row.astype(jnp.float32) + 1.0)
        here, there, mu, mu_there = rest[:4]
        low = ring * (mu[0, 0] + mu_there[0, 0]) * (here[0, 0] - there[0, 0])
        here, there, mu, mu_there = rest[4:]
        return low, ring * (mu[0, 0] + mu_there[0, 0]) * (here[0, 0] - there[0, 0])

    def part(self):
        return pl.BlockSpec((1, self.cycles, self.block, self.cells), lambda i, *_: (i, 0, 0, 0))

    def parts(self, count, first=0):
        shape = (count, 1, self.cycles, self.block, self.cells)
        return pl.BlockSpec(shape, lambda i, *_: (first, i, 0, 0, 0))

    def quad_shapes(self, fields):
        one = (fields, self.cycles, self.block, self.cells)
        return [shaped(*one), shaped(2, *one), shaped(2, *one)]

    def mix(self, center, first, lo, hi, index, token):
        count = max(1, self.slots // 2 - 1)

        def kernel(ints, reals, own, got, *outs):
            scalars = self.scalars(ints, reals)
            for s in range(count):
                target = scalars.target(s + 1)
                outs[s][0] = (
                    scalars.weight(scalars.slot, target) * own[0]
                    + scalars.weight(scalars.first(), target) * got[0]
                )

        return call(
            kernel,
            "mix",
            token,
            (hi - lo,),
            [self.ints, self.reals, center, first],
            [SMEM, SMEM, self.side(lo, index), self.side(0, 0)],
            [self.side(0, 0)] * count,
            [shaped(hi - lo, self.block, self.near, self.cells)] * count,
        )

    def spread(self, local, others, lo, hi, token):
        faces, face_specs = self.faces(lo, 0)

        def kernel(ints, reals, local, *refs):
            others, (mine, core, chip), (flat, stage) = refs[9:-5], refs[-5:-2], refs[-2:]
            scalars = self.scalars(ints, reals)
            flat[...] = sums(scalars, local, others).reshape(flat.shape)
            low, high = self.face_terms(refs, lo, 0)
            flat[: self.near] += low
            flat[-self.near :] += high
            for o in range(QUAD):
                for j in range(self.owned):
                    for a in range(2):
                        r = o * self.owned + j + a * self.pairs
                        stage[o, 2 * j + a] = flat[pl.ds(r, self.block, stride=self.near), :]
            mine[0] = stage[scalars.rank]
            core[0, 0] = stage[scalars.rank ^ 1]
            core[1, 0] = stage[scalars.rank ^ 3]
            chip[0, 0] = stage[scalars.rank ^ 2]

        return call(
            kernel,
            "spread",
            token,
            (hi - lo,),
            [self.ints, self.reals, local] + faces + others,
            [SMEM, SMEM, self.side(lo, 0)] + face_specs + [self.side(0, 0)] * len(others),
            [self.part(), self.parts(2), self.parts(1)],
            self.quad_shapes(hi - lo),
            [
                pltpu.VMEM((self.block * self.near, self.cells), jnp.float32),
                pltpu.VMEM((QUAD, self.cycles, self.block, self.cells), jnp.float32),
            ],
        )

    def join(self, held, new, token):
        def kernel(held, new, out):
            out[...] = new[...]

        return call(
            kernel,
            "join",
            token,
            (held.shape[1],),
            [held, new],
            [ANY, self.parts(1, 1)],
            self.parts(1, 1),
            shaped(*held.shape),
            alias={0: 0},
        )

    def own_rows(self, shape):
        return pl.BlockSpec(
            (1, self.owned) + shape, lambda i, ints: (ints[1] // QUAD, ints[1] % QUAD, 0, 0)
        )

    def table_call(self, kernel, name, fields, inputs, in_specs, out_specs, out_shape, scratch, token):
        extra = list(token)
        kernel, out_specs, out_shape = stamped(kernel, 1 + len(inputs), len(extra), out_specs, out_shape)
        return pl.pallas_call(
            kernel,
            grid_spec=pltpu.PrefetchScalarGridSpec(
                num_scalar_prefetch=1,
                grid=(fields,),
                in_specs=in_specs + [ANY] * len(extra),
                out_specs=out_specs,
                scratch_shapes=scratch,
            ),
            out_shape=out_shape,
            compiler_params=pltpu.CompilerParams(vmem_limit_bytes=24 * MIB),
            cost_estimate=COST,
            name=name,
        )(self.ints, *inputs, *extra)

    def block4(self, *shape):
        return pl.BlockSpec((1,) + shape, lambda i, ints: (i, 0, 0, 0))

    def coefficients(self, mine, core, chip, token):
        fields = mine.shape[0]

        def kernel(ints, reals, table, mine, core, chip, out, column):
            scalars = self.scalars(ints, reals)
            row = lax.broadcasted_iota(jnp.int32, (self.depth, self.cells), 0)
            for k, part in enumerate((mine[0], core[0, 0], chip[0, 0], chip[1, 0])):
                column[:, scalars.rank ^ k] = part
            for j in range(self.owned):
                modes = [
                    jnp.dot(
                        table[0, j],
                        column[2 * j + a].reshape(QUAD * self.block, self.cells),
                        precision=lax.Precision.HIGHEST,
                        preferred_element_type=jnp.float32,
                    )
                    for a in range(2)
                ]
                split = scalars.split(scalars.rank * self.owned + j)
                out[0, j] = jnp.where(row < split, modes[0], modes[1])

        return self.table_call(
            kernel,
            "coefficients",
            fields,
            [self.reals, self.table, mine, core, chip],
            [SMEM, self.own_rows(self.table.shape[2:]), self.part(), self.parts(1), self.parts(2)],
            self.block4(self.owned, self.depth, self.cells),
            shaped(fields, self.owned, self.depth, self.cells),
            [pltpu.VMEM((self.cycles, QUAD, self.block, self.cells), jnp.float32)],
            token,
        )

    def filtered(self, own, other, mine, core, chip, token):
        fields = mine.shape[0]

        def kernel(ints, reals, back, own, other, mine, core, chip, *refs):
            (mine_out, core_out, chip_out), waves = refs[:3], refs[3]
            scalars = self.scalars(ints, reals)
            row = lax.broadcasted_iota(jnp.int32, (self.depth, self.cells), 0)
            source = (mine.at[0], core.at[0, 0], chip.at[0, 0], chip.at[1, 0])
            result = (mine_out.at[0], core_out.at[0, 0], chip_out.at[0, 0], chip_out.at[1, 0])
            for j in range(self.owned):
                pair = scalars.rank * self.owned + j
                total = own[0, j] + other[0, j]
                keep = row < scalars.split(pair)
                for a in range(2):
                    waves[2 * j + a] = jnp.dot(
                        back[0, j],
                        jnp.where(keep if a == 0 else jnp.logical_not(keep), total, 0.0),
                        precision=lax.Precision.HIGHEST,
                        preferred_element_type=jnp.float32,
                    ).reshape(QUAD, self.block, self.cells)
                    r = pair + a * self.pairs
                    for k in range(QUAD):
                        result[k][2 * j + a] = (
                            scalars.base(r) * source[k][2 * j + a]
                            + scalars.scale(r) * waves[2 * j + a, scalars.rank ^ k]
                        )

        modes = self.block4(self.owned, self.depth, self.cells)
        return self.table_call(
            kernel,
            "filtered",
            fields,
            [self.reals, self.back, own, other, mine, core, chip],
            [SMEM, self.own_rows(self.back.shape[2:]), modes, modes]
            + [self.part(), self.parts(1), self.parts(2)],
            [self.part(), self.parts(1), self.parts(2)],
            self.quad_shapes(fields),
            [pltpu.VMEM((self.cycles, QUAD, self.block, self.cells), jnp.float32)],
            token,
        )

    def place_near(self, mine, core, chip, held, lo, hi, token):
        carried = [] if held is None else [held]

        def kernel(ints, reals, mine, core, chip, *refs):
            out, stage = refs[-2:]
            rank = self.scalars(ints, reals).rank
            for k, part in enumerate((mine[0], core[0, 0], chip[0, 0], core[1, 0])):
                stage[rank ^ k] = part
            for o in range(QUAD):
                for j in range(self.owned):
                    for a in range(2):
                        out[0, :, o * self.owned + j + a * self.pairs, :] = stage[o, 2 * j + a]

        return call(
            kernel,
            "place_near",
            token,
            (hi - lo,),
            [self.ints, self.reals, mine, core, chip] + carried,
            [SMEM, SMEM, self.part(), self.parts(2), self.parts(1)] + [ANY] * len(carried),
            self.side(lo, 0),
            shaped(*self.shape),
            [pltpu.VMEM((QUAD, self.cycles, self.block, self.cells), jnp.float32)],
            alias={5: 0} if carried else None,
        )

    def place_far(self, local, others, held, lo, hi, token):
        carried = [] if held is None else [held]
        faces, face_specs = self.faces(lo, 1)

        def kernel(ints, reals, local, *refs):
            others, out = refs[9 : len(refs) - 1 - len(carried)], refs[-1]
            out[0] = sums(self.scalars(ints, reals), local, others)
            low, high = self.face_terms(refs, lo, 1)
            out[0, 0] += low
            out[0, self.block - 1] += high

        return call(
            kernel,
            "place_far",
            token,
            (hi - lo,),
            [self.ints, self.reals, local] + faces + others + carried,
            [SMEM, SMEM, self.side(lo, 0)]
            + face_specs
            + [self.side(0, 0)] * len(others)
            + [ANY] * len(carried),
            self.side(lo, 1),
            shaped(*self.shape),
            alias={3 + len(faces) + len(others): 0} if carried else None,
        )


def spans(sizes, total):
    ends = np.cumsum(sizes)
    return [(int(end - size), int(end)) for size, end in zip(sizes, ends)]


def body(adjoint, source, viscosity, kappa, coupling, bc_flags, inst_map):
    slots = lax.axis_size("inst")
    sectors = lax.axis_size("space")
    center = adjoint[0]
    fields, block, cycles, cells = center.shape
    near = cycles // 2
    points = block * sectors
    quads = sectors // QUAD

    def to_partner(x, pick):
        pairs = []
        for i in range(slots):
            for p in range(sectors):
                pairs.append((i * sectors + p, pick(i, p % 2) * sectors + p))
        return lax.ppermute(x, ("inst", "space"), pairs)

    def to_first(x):
        return to_partner(x, lambda i, core: first_partner(i, core, slots))

    def to_later(x, s):
        return to_partner(x, lambda i, core: later_partner(i, core, slots, s))

    def to_sector(x, k):
        return lax.ppermute(x, "space", [(i, i ^ k) for i in range(sectors)])

    def ring(x, step):
        return lax.ppermute(x, "space", [(i, (i + step) % sectors) for i in range(sectors)])

    table, split, base, scale = mode_layout(points, near)
    table = table.reshape(table.shape[0], table.shape[1], quads, QUAD * block).transpose(2, 0, 1, 3)
    here = jnp.stack([lax.axis_index("inst"), lax.axis_index("space")])
    ints = jnp.concatenate([here, inst_map, jnp.asarray(split)])
    reals = jnp.asarray(np.concatenate([spectral_values(slots), base, scale]).astype(np.float32))
    plan = Plan(
        ints,
        reals,
        slots,
        center.shape,
        near,
        jnp.asarray(np.ascontiguousarray(table)),
        jnp.asarray(np.ascontiguousarray(table.transpose(0, 1, 3, 2))),
    )

    groups = [(lo, hi, 0) for lo, hi in spans(NEAR_SIZES, fields)]
    groups += [(lo, hi, 1) for lo, hi in spans(FAR_SIZES, fields)]
    first, others, parts, own, done = {}, {}, {}, {}, {}
    made, local, held, halos = {}, {}, None, None
    for step, g in ORDER:
        lo, hi, index = groups[g]
        token = [made[before] for before, after in EDGES if after == (step, g)]
        if step == "pack":
            early = 0 not in local
            *packed, stamp = pack(center, viscosity, lo, hi, index, near, halos is None, token, early)
            first[g] = to_first(packed[0])
            if halos is None:
                halos = ring(packed[1], 1), ring(packed[2], -1)
                plan.halos, plan.center, plan.viscosity, plan.kappa = halos, center, viscosity, kappa
        elif step == "local":
            local[g], stamp = local_part(
                g, center, source[0], viscosity, kappa, coupling, bc_flags, token
            )
        elif step == "mix":
            *mixed, stamp = plan.mix(center, first[g], lo, hi, index, token)
            others[g] = [first[g]] + [to_later(x, s + 1) for s, x in enumerate(mixed)]
        elif step == "spread":
            mine, core, chip, stamp = plan.spread(local[0], others[g], lo, hi, token)
            parts[g] = mine, to_sector(core, 1), chip
        elif step == "join":
            mine, core, chip = parts[g]
            chip, stamp = plan.join(chip, core, token)
            parts[g] = mine, core, to_sector(chip, 2)
        elif step == "coef":
            part, stamp = plan.coefficients(*parts[g], token)
            stride = QUAD
            while 2 * stride < sectors:
                part = part + to_sector(part, stride)
                stride = 2 * stride
            other = to_sector(part, stride) if stride < sectors else jnp.zeros_like(part)
            own[g] = part, other
        elif step == "filter":
            mine, core, chip, stamp = plan.filtered(*own[g], *parts[g], token)
            done[g] = mine, core, to_sector(chip, 2)
        elif step == "back":
            mine, core, chip = done[g]
            core, stamp = plan.join(core, chip, token)
            done[g] = mine, to_sector(core, 1), chip
        elif step == "near":
            held, stamp = plan.place_near(*done[g], held, lo, hi, token)
        else:
            held, stamp = plan.place_far(local[1], others[g], held, lo, hi, token)
        made[step, g] = stamp
    return held[None]


def solution(mesh):
    return jax.shard_map(
        body,
        mesh=mesh,
        in_specs=(
            P("inst", None, "space", None, None),
            P("inst", None, "space", None, None),
            P("space", None, None),
            P(),
            P(),
            P(),
            P(),
        ),
        out_specs=P("inst", None, "space", None, None),
        check_vma=False,
    )
```

```python
import functools

import jax
import jax.numpy as jnp
import numpy as np
from jax import lax
from jax.experimental import pallas as pl
from jax.experimental.pallas import tpu as pltpu
from jax.sharding import PartitionSpec as P

QUAD = 4
NEAR_SIZES = (2, 2, 1)
FAR_SIZES = (1, 2, 2)
ORDER = (
    ("pack", 0),
    ("pack", 5),
    ("pack", 3),
    ("pack", 1),
    ("local", 0),
    ("pack", 4),
    ("pack", 2),
    ("mix", 0),
    ("mix", 1),
    ("spread", 0),
    ("join", 0),
    ("spread", 1),
    ("mix", 2),
    ("coef", 0),
    ("join", 1),
    ("spread", 2),
    ("join", 2),
    ("mix", 5),
    ("coef", 1),
    ("filter", 0),
    ("mix", 4),
    ("coef", 2),
    ("mix", 3),
    ("local", 1),
    ("filter", 1),
    ("filter", 2),
    ("back", 0),
    ("far", 5),
    ("back", 1),
    ("near", 0),
    ("far", 4),
    ("back", 2),
    ("far", 3),
    ("near", 2),
    ("near", 1),
)
EDGES = tuple(zip(ORDER[:-1], ORDER[1:]))
PACK = 60
LOCAL = 52
SMEM = pl.BlockSpec(memory_space=pltpu.SMEM)
ANY = pl.BlockSpec(memory_space=pl.ANY)
COST = pl.CostEstimate(flops=0, bytes_accessed=0, transcendentals=0)
MIB = 1024 * 1024


def spectral_values(slots):
    offset = np.arange(1 - slots, slots)
    safe = np.where(offset == 0, 1.0, np.sin(np.pi * offset / slots))
    return np.where(offset == 0, 0.0, 0.5 * (1.0 - 2.0 * (np.abs(offset) % 2)) / safe)


def mode_layout(points, near):
    half = points // 2
    pairs = near // 2
    theta = np.arange(points)
    bases, base, scale = [], np.zeros(near), np.zeros(near)
    for r in range(near):
        cutoff = max(4, points * (r + 1) // (2 * near))
        weight = max(1.0 - r / near, 0.0)
        kept = [m for m in range(half + 1) if m < cutoff]
        out = [m for m in range(half + 1) if m >= cutoff]
        count = [sum(1 if m in (0, half) else 2 for m in modes) for modes in (kept, out)]
        low = count[0] <= count[1]
        rows = []
        for m in kept if low else out:
            angle = 2.0 * np.pi * (m * theta % points) / points
            if m in (0, half):
                rows.append(np.cos(angle) / np.sqrt(points))
            else:
                rows.append(np.cos(angle) * np.sqrt(2.0 / points))
                rows.append(np.sin(angle) * np.sqrt(2.0 / points))
        bases.append(rows)
        base[r] = 1.0 - weight if low else 1.0
        scale[r] = weight if low else -weight
    depth = max(len(bases[p]) + len(bases[p + pairs]) for p in range(pairs))
    depth = -(-depth // 8) * 8
    table = np.zeros((pairs, depth, points), np.float32)
    split = np.zeros(pairs, np.int32)
    for p in range(pairs):
        rows = bases[p] + bases[p + pairs]
        table[p, : len(rows)] = np.stack(rows)
        split[p] = len(bases[p])
    return table, split, base, scale


class Scalars:
    def __init__(self, ints, reals, slots, near):
        self.ints, self.reals, self.slots, self.near = ints, reals, slots, near
        self.slot, self.place = ints[0], ints[1]
        self.rank = self.place % QUAD

    def weight(self, i, j):
        return self.reals[self.ints[2 + i] - self.ints[2 + j] + self.slots - 1]

    def split(self, pair):
        return self.ints[2 + self.slots + pair]

    def base(self, r):
        return self.reals[2 * self.slots - 1 + r]

    def scale(self, r):
        return self.reals[2 * self.slots - 1 + self.near + r]

    def first(self):
        return first_partner(self.slot, self.place % 2, self.slots)

    def target(self, s):
        return later_partner(self.slot, self.place % 2, self.slots, s)


def first_partner(slot, core, slots):
    if slots == 4:
        return slot ^ (2 - core)
    return slot ^ 1


def later_partner(slot, core, slots, s):
    if slots == 4:
        return slot ^ (1 + core)
    return (slot // 2 + s) % (slots // 2) * 2 + slot % 2


def stamped(kernel, inputs, extra, out_specs, out_shape):
    out_specs = out_specs if isinstance(out_specs, list) else [out_specs]
    out_shape = out_shape if isinstance(out_shape, list) else [out_shape]
    skip, end = inputs + extra, inputs + extra + len(out_shape)

    def body(*refs):
        refs[end][...] = jnp.zeros_like(refs[end])
        kernel(*refs[:inputs], *refs[skip:end], *refs[end + 1 :])

    stamp = pl.BlockSpec((8, 128), lambda i, *_: (0, 0))
    return body, out_specs + [stamp], out_shape + [shaped(8, 128)]


def call(kernel, name, token, grid, inputs, in_specs, out_specs, out_shape, scratch=(), alias=None, grant=24):
    extra = list(token)
    kernel, out_specs, out_shape = stamped(kernel, len(inputs), len(extra), out_specs, out_shape)
    return pl.pallas_call(
        kernel,
        grid=grid,
        in_specs=list(in_specs) + [ANY] * len(extra),
        out_specs=out_specs,
        out_shape=out_shape,
        scratch_shapes=list(scratch),
        input_output_aliases=alias or {},
        compiler_params=pltpu.CompilerParams(vmem_limit_bytes=grant * MIB),
        cost_estimate=COST,
        name=name,
    )(*inputs, *extra)


def shaped(*shape):
    return jax.ShapeDtypeStruct(shape, jnp.float32)


def pack(center, viscosity, lo, hi, index, near, edges, token, early):
    fields, block, rows, cells = center.shape
    inputs, in_specs = [center], [pl.BlockSpec((1, block, near, cells), lambda i: (lo + i, 0, index, 0))]
    shapes = [shaped(hi - lo, block, near, cells)]
    out_specs = [pl.BlockSpec((1, block, near, cells), lambda i: (i, 0, 0, 0))]
    if edges:
        for start in (block - 1, 0):
            inputs += [center, viscosity]
            in_specs.append(pl.BlockSpec((fields, 1, rows, cells), lambda i, s=start: (0, s, 0, 0)))
            in_specs.append(pl.BlockSpec((1, rows, cells), lambda i, s=start: (s, 0, 0)))
            shapes.append(shaped(fields + 1, 1, rows, cells))
            out_specs.append(pl.BlockSpec((fields + 1, 1, rows, cells), lambda i: (0, 0, 0, 0)))

    def kernel(source, *refs):
        out, rest = refs[len(inputs) - 1], refs[len(inputs) :]
        out[...] = source[...]
        for e, edge in enumerate(rest):
            edge[:fields] = refs[2 * e][...]
            edge[fields] = refs[2 * e + 1][...]

    return call(kernel, "pack", token, (hi - lo,), inputs, in_specs, out_specs, shapes, grant=PACK if early else 24)


def local_kernel(
    far, coupling, kappa, flags, adj, before, after, next_to, src, mu, mu_before, mu_after, mu_next, out
):
    fields, planes, rows, cells = adj.shape
    step = pl.program_id(0)
    first = step == 0
    last = step == pl.num_programs(0) - 1
    row = lax.broadcasted_iota(jnp.int32, (rows, cells), 0)
    col = lax.broadcasted_iota(jnp.int32, (rows, cells), 1)
    ring = 0.5 / ((row + rows * far).astype(jnp.float32) + 1.0)

    def visc(k):
        return mu_before[0] if k < 0 else mu_after[0] if k >= planes else mu[k]

    def cell(f, k):
        return before[f, 0] if k < 0 else after[f, 0] if k >= planes else adj[f, k]

    def outward(x, edge):
        moved = pltpu.roll(x, rows - 1, 0)
        return moved if far else jnp.where(row == rows - 1, edge[:1], moved)

    def inward(x, edge):
        moved = pltpu.roll(x, 1, 0)
        return jnp.where(row == 0, edge[-1:], moved) if far else moved

    walls = []
    for f in range(fields):
        opens = [(1 - flags[f, i]).astype(jnp.float32) for i in range(3)]
        wall = jnp.where(col == 0, opens[0], 0.0)
        wall = wall + jnp.where(col == cells - 1, opens[1], 0.0)
        walls.append(wall + jnp.where(row == rows - 1, opens[2], 0.0) if far else wall)

    for k in range(planes):
        m = visc(k)
        up = ring * (m + visc(k + 1))
        down = ring * (m + visc(k - 1))
        if k == planes - 1:
            up = jnp.where(last, 0.0, up)
        if k == 0:
            down = jnp.where(first, 0.0, down)
        outer = 0.5 * (m + outward(m, mu_next[k]))
        inner = 0.5 * (m + inward(m, mu_next[k]))
        if far:
            outer = jnp.where(row < rows - 1, outer, 0.0)
        else:
            inner = jnp.where(row > 0, inner, 0.0)
        east = jnp.where(col < cells - 1, 0.5 * (m + pltpu.roll(m, cells - 1, 1)), 0.0)
        west = jnp.where(col > 0, 0.5 * (m + pltpu.roll(m, 1, 1)), 0.0)
        diag = up + down + outer + inner + east + west
        for f in range(fields):
            p = adj[f, k]
            flux = (diag + walls[f] * m) * p
            flux = flux - up * cell(f, k + 1) - down * cell(f, k - 1)
            flux = flux - outer * outward(p, next_to[f, k]) - inner * inward(p, next_to[f, k])
            flux = flux - east * pltpu.roll(p, cells - 1, 1) - west * pltpu.roll(p, 1, 1)
            total = src[f, k] + kappa[f] * flux
            for g in range(fields):
                total = total + coupling[g, f] * adj[g, k]
            out[f, k] = total


def local_part(far, center, source, viscosity, kappa, coupling, flags, token):
    fields, block, rows, cells = center.shape
    half = rows // 2
    planes = min(4, block)
    edge = half // 8 - 1 if far else half // 8

    def whole(width, index):
        return pl.BlockSpec((fields, width, half, cells), lambda i: (0, index(i), far, 0))

    def plane(width, index):
        return pl.BlockSpec((width, half, cells), lambda i: (index(i), far, 0))

    behind = lambda i: jnp.maximum(i * planes - 1, 0)
    ahead = lambda i: jnp.minimum(i * planes + planes, block - 1)
    here = lambda i: i
    return call(
        functools.partial(local_kernel, far),
        "local_part",
        token,
        (block // planes,),
        [coupling, kappa, flags, center, center, center, center, source]
        + [viscosity] * 4,
        [
            SMEM,
            SMEM,
            SMEM,
            whole(planes, here),
            whole(1, behind),
            whole(1, ahead),
            pl.BlockSpec((fields, planes, 8, cells), lambda i: (0, i, edge, 0)),
            whole(planes, here),
            plane(planes, here),
            plane(1, behind),
            plane(1, ahead),
            pl.BlockSpec((planes, 8, cells), lambda i: (i, edge, 0)),
        ],
        pl.BlockSpec((fields, planes, half, cells), lambda i: (0, i, 0, 0)),
        shaped(fields, block, half, cells),
        grant=24 if far else LOCAL,
    )


def sums(scalars, local, others):
    total = local[0] + scalars.weight(scalars.first(), scalars.slot) * others[0][0]
    for part in others[1:]:
        total = total + part[0]
    return total


class Plan:
    def __init__(self, ints, reals, slots, shape, near, table, back):
        self.ints, self.reals, self.slots, self.near = ints, reals, slots, near
        self.shape, self.table, self.back = shape, table, back
        self.fields, self.block, self.rows, self.cells = shape
        self.pairs = near // 2
        self.owned = self.pairs // QUAD
        self.cycles = near // QUAD
        self.depth = table.shape[2]

    def scalars(self, ints, reals):
        return Scalars(ints, reals, self.slots, self.near)

    def side(self, first, index):
        return pl.BlockSpec((1, self.block, self.near, self.cells), lambda i: (first + i, 0, index, 0))

    def faces(self, lo, side):
        shape = (1, 1, self.near, self.cells)
        at = lambda f, k: pl.BlockSpec(shape, lambda i: (f(i), k, side, 0))
        field = lambda i: lo + i
        inputs, specs = [self.kappa], [SMEM]
        for k, halo in zip((0, self.block - 1), self.halos):
            inputs += [self.center, halo, self.viscosity[None], halo]
            specs += [at(field, k), at(field, 0), at(lambda i: 0, k), at(lambda i: self.fields, 0)]
        return inputs, specs

    def face_terms(self, refs, lo, side):
        kappa, rest = refs[0], refs[1:9]
        row = lax.broadcasted_iota(jnp.int32, (self.near, self.cells), 0) + side * self.near
        ring = 0.5 * kappa[lo + pl.program_id(0)] / (row.astype(jnp.float32) + 1.0)
        here, there, mu, mu_there = rest[:4]
        low = ring * (mu[0, 0] + mu_there[0, 0]) * (here[0, 0] - there[0, 0])
        here, there, mu, mu_there = rest[4:]
        return low, ring * (mu[0, 0] + mu_there[0, 0]) * (here[0, 0] - there[0, 0])

    def part(self):
        return pl.BlockSpec((1, self.cycles, self.block, self.cells), lambda i, *_: (i, 0, 0, 0))

    def parts(self, count, first=0):
        shape = (count, 1, self.cycles, self.block, self.cells)
        return pl.BlockSpec(shape, lambda i, *_: (first, i, 0, 0, 0))

    def quad_shapes(self, fields):
        one = (fields, self.cycles, self.block, self.cells)
        return [shaped(*one), shaped(2, *one), shaped(2, *one)]

    def mix(self, center, first, lo, hi, index, token):
        count = max(1, self.slots // 2 - 1)

        def kernel(ints, reals, own, got, *outs):
            scalars = self.scalars(ints, reals)
            for s in range(count):
                target = scalars.target(s + 1)
                outs[s][0] = (
                    scalars.weight(scalars.slot, target) * own[0]
                    + scalars.weight(scalars.first(), target) * got[0]
                )

        return call(
            kernel,
            "mix",
            token,
            (hi - lo,),
            [self.ints, self.reals, center, first],
            [SMEM, SMEM, self.side(lo, index), self.side(0, 0)],
            [self.side(0, 0)] * count,
            [shaped(hi - lo, self.block, self.near, self.cells)] * count,
        )

    def spread(self, local, others, lo, hi, token):
        faces, face_specs = self.faces(lo, 0)

        def kernel(ints, reals, local, *refs):
            others, (mine, core, chip), (flat, stage) = refs[9:-5], refs[-5:-2], refs[-2:]
            scalars = self.scalars(ints, reals)
            flat[...] = sums(scalars, local, others).reshape(flat.shape)
            low, high = self.face_terms(refs, lo, 0)
            flat[: self.near] += low
            flat[-self.near :] += high
            for o in range(QUAD):
                for j in range(self.owned):
                    for a in range(2):
                        r = o * self.owned + j + a * self.pairs
                        stage[o, 2 * j + a] = flat[pl.ds(r, self.block, stride=self.near), :]
            mine[0] = stage[scalars.rank]
            core[0, 0] = stage[scalars.rank ^ 1]
            core[1, 0] = stage[scalars.rank ^ 3]
            chip[0, 0] = stage[scalars.rank ^ 2]

        return call(
            kernel,
            "spread",
            token,
            (hi - lo,),
            [self.ints, self.reals, local] + faces + others,
            [SMEM, SMEM, self.side(lo, 0)] + face_specs + [self.side(0, 0)] * len(others),
            [self.part(), self.parts(2), self.parts(1)],
            self.quad_shapes(hi - lo),
            [
                pltpu.VMEM((self.block * self.near, self.cells), jnp.float32),
                pltpu.VMEM((QUAD, self.cycles, self.block, self.cells), jnp.float32),
            ],
        )

    def join(self, held, new, token):
        def kernel(held, new, out):
            out[...] = new[...]

        return call(
            kernel,
            "join",
            token,
            (held.shape[1],),
            [held, new],
            [ANY, self.parts(1, 1)],
            self.parts(1, 1),
            shaped(*held.shape),
            alias={0: 0},
        )

    def own_rows(self, shape):
        return pl.BlockSpec(
            (1, self.owned) + shape, lambda i, ints: (ints[1] // QUAD, ints[1] % QUAD, 0, 0)
        )

    def table_call(self, kernel, name, fields, inputs, in_specs, out_specs, out_shape, scratch, token):
        extra = list(token)
        kernel, out_specs, out_shape = stamped(kernel, 1 + len(inputs), len(extra), out_specs, out_shape)
        return pl.pallas_call(
            kernel,
            grid_spec=pltpu.PrefetchScalarGridSpec(
                num_scalar_prefetch=1,
                grid=(fields,),
                in_specs=in_specs + [ANY] * len(extra),
                out_specs=out_specs,
                scratch_shapes=scratch,
            ),
            out_shape=out_shape,
            compiler_params=pltpu.CompilerParams(vmem_limit_bytes=24 * MIB),
            cost_estimate=COST,
            name=name,
        )(self.ints, *inputs, *extra)

    def block4(self, *shape):
        return pl.BlockSpec((1,) + shape, lambda i, ints: (i, 0, 0, 0))

    def coefficients(self, mine, core, chip, token):
        fields = mine.shape[0]

        def kernel(ints, reals, table, mine, core, chip, out, column):
            scalars = self.scalars(ints, reals)
            row = lax.broadcasted_iota(jnp.int32, (self.depth, self.cells), 0)
            for k, part in enumerate((mine[0], core[0, 0], chip[0, 0], chip[1, 0])):
                column[:, scalars.rank ^ k] = part
            for j in range(self.owned):
                modes = [
                    jnp.dot(
                        table[0, j],
                        column[2 * j + a].reshape(QUAD * self.block, self.cells),
                        precision=lax.Precision.HIGHEST,
                        preferred_element_type=jnp.float32,
                    )
                    for a in range(2)
                ]
                split = scalars.split(scalars.rank * self.owned + j)
                out[0, j] = jnp.where(row < split, modes[0], modes[1])

        return self.table_call(
            kernel,
            "coefficients",
            fields,
            [self.reals, self.table, mine, core, chip],
            [SMEM, self.own_rows(self.table.shape[2:]), self.part(), self.parts(1), self.parts(2)],
            self.block4(self.owned, self.depth, self.cells),
            shaped(fields, self.owned, self.depth, self.cells),
            [pltpu.VMEM((self.cycles, QUAD, self.block, self.cells), jnp.float32)],
            token,
        )

    def filtered(self, own, other, mine, core, chip, token):
        fields = mine.shape[0]

        def kernel(ints, reals, back, own, other, mine, core, chip, *refs):
            (mine_out, core_out, chip_out), waves = refs[:3], refs[3]
            scalars = self.scalars(ints, reals)
            row = lax.broadcasted_iota(jnp.int32, (self.depth, self.cells), 0)
            source = (mine.at[0], core.at[0, 0], chip.at[0, 0], chip.at[1, 0])
            result = (mine_out.at[0], core_out.at[0, 0], chip_out.at[0, 0], chip_out.at[1, 0])
            for j in range(self.owned):
                pair = scalars.rank * self.owned + j
                total = own[0, j] + other[0, j]
                keep = row < scalars.split(pair)
                for a in range(2):
                    waves[2 * j + a] = jnp.dot(
                        back[0, j],
                        jnp.where(keep if a == 0 else jnp.logical_not(keep), total, 0.0),
                        precision=lax.Precision.HIGHEST,
                        preferred_element_type=jnp.float32,
                    ).reshape(QUAD, self.block, self.cells)
                    r = pair + a * self.pairs
                    for k in range(QUAD):
                        result[k][2 * j + a] = (
                            scalars.base(r) * source[k][2 * j + a]
                            + scalars.scale(r) * waves[2 * j + a, scalars.rank ^ k]
                        )

        modes = self.block4(self.owned, self.depth, self.cells)
        return self.table_call(
            kernel,
            "filtered",
            fields,
            [self.reals, self.back, own, other, mine, core, chip],
            [SMEM, self.own_rows(self.back.shape[2:]), modes, modes]
            + [self.part(), self.parts(1), self.parts(2)],
            [self.part(), self.parts(1), self.parts(2)],
            self.quad_shapes(fields),
            [pltpu.VMEM((self.cycles, QUAD, self.block, self.cells), jnp.float32)],
            token,
        )

    def place_near(self, mine, core, chip, held, lo, hi, token):
        carried = [] if held is None else [held]

        def kernel(ints, reals, mine, core, chip, *refs):
            out, stage = refs[-2:]
            rank = self.scalars(ints, reals).rank
            for k, part in enumerate((mine[0], core[0, 0], chip[0, 0], core[1, 0])):
                stage[rank ^ k] = part
            for o in range(QUAD):
                for j in range(self.owned):
                    for a in range(2):
                        out[0, :, o * self.owned + j + a * self.pairs, :] = stage[o, 2 * j + a]

        return call(
            kernel,
            "place_near",
            token,
            (hi - lo,),
            [self.ints, self.reals, mine, core, chip] + carried,
            [SMEM, SMEM, self.part(), self.parts(2), self.parts(1)] + [ANY] * len(carried),
            self.side(lo, 0),
            shaped(*self.shape),
            [pltpu.VMEM((QUAD, self.cycles, self.block, self.cells), jnp.float32)],
            alias={5: 0} if carried else None,
        )

    def place_far(self, local, others, held, lo, hi, token):
        carried = [] if held is None else [held]
        faces, face_specs = self.faces(lo, 1)

        def kernel(ints, reals, local, *refs):
            others, out = refs[9 : len(refs) - 1 - len(carried)], refs[-1]
            out[0] = sums(self.scalars(ints, reals), local, others)
            low, high = self.face_terms(refs, lo, 1)
            out[0, 0] += low
            out[0, self.block - 1] += high

        return call(
            kernel,
            "place_far",
            token,
            (hi - lo,),
            [self.ints, self.reals, local] + faces + others + carried,
            [SMEM, SMEM, self.side(lo, 0)]
            + face_specs
            + [self.side(0, 0)] * len(others)
            + [ANY] * len(carried),
            self.side(lo, 1),
            shaped(*self.shape),
            alias={3 + len(faces) + len(others): 0} if carried else None,
        )


def spans(sizes, total):
    ends = np.cumsum(sizes)
    return [(int(end - size), int(end)) for size, end in zip(sizes, ends)]


def body(adjoint, source, viscosity, kappa, coupling, bc_flags, inst_map):
    slots = lax.axis_size("inst")
    sectors = lax.axis_size("space")
    center = adjoint[0]
    fields, block, cycles, cells = center.shape
    near = cycles // 2
    points = block * sectors
    quads = sectors // QUAD

    def to_partner(x, pick):
        pairs = []
        for i in range(slots):
            for p in range(sectors):
                pairs.append((i * sectors + p, pick(i, p % 2) * sectors + p))
        return lax.ppermute(x, ("inst", "space"), pairs)

    def to_first(x):
        return to_partner(x, lambda i, core: first_partner(i, core, slots))

    def to_later(x, s):
        return to_partner(x, lambda i, core: later_partner(i, core, slots, s))

    def to_sector(x, k):
        return lax.ppermute(x, "space", [(i, i ^ k) for i in range(sectors)])

    def ring(x, step):
        return lax.ppermute(x, "space", [(i, (i + step) % sectors) for i in range(sectors)])

    table, split, base, scale = mode_layout(points, near)
    table = table.reshape(table.shape[0], table.shape[1], quads, QUAD * block).transpose(2, 0, 1, 3)
    here = jnp.stack([lax.axis_index("inst"), lax.axis_index("space")])
    ints = jnp.concatenate([here, inst_map, jnp.asarray(split)])
    reals = jnp.asarray(np.concatenate([spectral_values(slots), base, scale]).astype(np.float32))
    plan = Plan(
        ints,
        reals,
        slots,
        center.shape,
        near,
        jnp.asarray(np.ascontiguousarray(table)),
        jnp.asarray(np.ascontiguousarray(table.transpose(0, 1, 3, 2))),
    )

    groups = [(lo, hi, 0) for lo, hi in spans(NEAR_SIZES, fields)]
    groups += [(lo, hi, 1) for lo, hi in spans(FAR_SIZES, fields)]
    first, others, parts, own, done = {}, {}, {}, {}, {}
    made, local, held, halos = {}, {}, None, None
    for step, g in ORDER:
        lo, hi, index = groups[g]
        token = [made[before] for before, after in EDGES if after == (step, g)]
        if step == "pack":
            early = 0 not in local
            *packed, stamp = pack(center, viscosity, lo, hi, index, near, halos is None, token, early)
            first[g] = to_first(packed[0])
            if halos is None:
                halos = ring(packed[1], 1), ring(packed[2], -1)
                plan.halos, plan.center, plan.viscosity, plan.kappa = halos, center, viscosity, kappa
        elif step == "local":
            local[g], stamp = local_part(
                g, center, source[0], viscosity, kappa, coupling, bc_flags, token
            )
        elif step == "mix":
            *mixed, stamp = plan.mix(center, first[g], lo, hi, index, token)
            others[g] = [first[g]] + [to_later(x, s + 1) for s, x in enumerate(mixed)]
        elif step == "spread":
            mine, core, chip, stamp = plan.spread(local[0], others[g], lo, hi, token)
            parts[g] = mine, to_sector(core, 1), chip
        elif step == "join":
            mine, core, chip = parts[g]
            chip, stamp = plan.join(chip, core, token)
            parts[g] = mine, core, to_sector(chip, 2)
        elif step == "coef":
            part, stamp = plan.coefficients(*parts[g], token)
            stride = QUAD
            while 2 * stride < sectors:
                part = part + to_sector(part, stride)
                stride = 2 * stride
            other = to_sector(part, stride) if stride < sectors else jnp.zeros_like(part)
            own[g] = part, other
        elif step == "filter":
            mine, core, chip, stamp = plan.filtered(*own[g], *parts[g], token)
            done[g] = mine, core, to_sector(chip, 2)
        elif step == "back":
            mine, core, chip = done[g]
            core, stamp = plan.join(core, chip, token)
            done[g] = mine, to_sector(core, 1), chip
        elif step == "near":
            held, stamp = plan.place_near(*done[g], held, lo, hi, token)
        else:
            held, stamp = plan.place_far(local[1], others[g], held, lo, hi, token)
        made[step, g] = stamp
    return held[None]


def solution(mesh):
    return jax.shard_map(
        body,
        mesh=mesh,
        in_specs=(
            P("inst", None, "space", None, None),
            P("inst", None, "space", None, None),
            P("space", None, None),
            P(),
            P(),
            P(),
            P(),
        ),
        out_specs=P("inst", None, "space", None, None),
        check_vma=False,
    )
```
